256 devices in a mesh: grp: 2 (over core), dev: 128 (over z, y, x).
Axes of the slice: x: 4, y: 4, z: 8, core: 2. Of those that a mesh axis runs over, the one named last changes fastest.
Arguments:
- spectra: float32 [1296, 32768], P(None, ('grp', 'dev')), may hold values from 0.05 to 1
- sea_mask: int32 [32768], P(('grp', 'dev')), may hold values 0 or 1
- card_map: int32 [32768], replicated, may hold values from 0 to 16383, as said below
- dia_table: int32 [4, 1296], replicated, may hold values from 0 to 1295
- dia_coef: float32 [1296], replicated, may hold values from 0.5 to 3
- speed: float32 [1296], replicated, may hold values from 0.1 to 0.6
- stokes_weight: float32 [1296], replicated, may hold values from 0.02 to 0.2
- couple_point: int32 [2048, 256], P(('grp', 'dev')), may hold values from -1 to 16383, as said below
- ocean_u: float32 [40, 2048, 256], P(None, ('grp', 'dev')), may hold values from -6 to 6
- ocean_v: float32 [40, 2048, 256], P(None, ('grp', 'dev')), may hold values from -6 to 6
- mixing: float32 [40], replicated, may hold values from 0.2 to 2
Outputs:
- new_spectra: float32 [1296, 32768], P(None, ('grp', 'dev'))
- new_u: float32 [40, 2048, 256], P(None, ('grp', 'dev'))
- new_v: float32 [40, 2048, 256], P(None, ('grp', 'dev'))
The draws below stay inside these ranges and needn't reach their ends.
Inputs may be any that keep to these rules, and one draw needn't show every extreme that they name: `card_map`: within each group's 128 * 128 entries every value appears exactly once. `couple_point`: the cell in column c of ocean row x couples to a point of its own group whose row lies within one of (x mod (1024)) // 8 and whose column lies within one of c // 2; -1 marks land.
All inputs are finite; a program needn't handle non-finite values. No bound on the sum of `sea_mask` on one device may be relied on, other than what follows from the above.
Results may differ from the reference program's by a relative error of at most 0.00007.
Values sent between devices are 32-bit elements; how exact they have to be, the bound alone decides.
A program may use at most 128 MiB of HBM per device.

```python
import math
import jax
import jax.numpy as jnp
from jax import lax

ND = 36
NF = 36
GX = 128
OCR = 8
OCC = 2
NZ = 40
PSTEPS = 2
OSTEPS = 2
K = 1296
PTS_DEV = 128
GROWS = 128
POINTS = 32768
OX = 2048
OY = 256
N_GRP = 2


def draw_card_map(key, part):
    key = jax.random.fold_in(key, 11)
    group_points = GROWS * GX
    pieces = [jax.random.permutation(jax.random.fold_in(key, index), group_points).astype(jnp.int32) for index in range(N_GRP)]
    return jnp.concatenate(pieces)


def draw_couple_point(key, part):
    key = jax.random.fold_in(key, 23)
    first, second, third = jax.random.split(key, 3)
    rows = jnp.arange(OX, dtype=jnp.int32)[:, None]
    columns = jnp.arange(OY, dtype=jnp.int32)[None, :]
    local_row = rows % (OX // N_GRP)
    base_row = local_row // OCR
    base_column = columns // OCC
    row_jitter = jax.random.randint(first, (OX, OY), -1, 2)
    column_jitter = jax.random.randint(second, (OX, OY), -1, 2)
    point_row = jnp.clip(base_row + row_jitter, 0, GROWS - 1)
    point_column = jnp.clip(base_column + column_jitter, 0, GX - 1)
    land = jax.random.randint(third, (OX, OY), 0, 4) == 0
    point = jnp.where(land, -1, point_row * GX + point_column)
    point = point.at[OX - 1, OY - 1].set(GROWS * GX - 1)
    point = point.at[0, 0].set(-1)
    return point.astype(jnp.int32)


def place_ends(drawn, key, low, high):
    longest = drawn.shape.index(max(drawn.shape))
    spots = []
    for shift in (0, 1):
        where = [jax.random.randint(jax.random.fold_in(key, axis), (), 0, length) for axis, length in enumerate(drawn.shape)]
        where[longest] = (where[longest] + shift) % drawn.shape[longest]
        spots.append(tuple(where))
    return drawn.at[spots[0]].set(low).at[spots[1]].set(high)


def block_scale(rng, shape, cuts, least, largest):
    loudness = 1.0
    for dim, shards_of in cuts:
        steps = jax.random.uniform(jax.random.fold_in(jax.random.fold_in(rng, 6), dim), (shards_of,), jnp.float32, least / len(cuts), largest / len(cuts))
        loudness = loudness * jnp.repeat(jnp.exp(steps), shape[dim] // shards_of).reshape((-1,) + (1,) * (len(shape) - 1 - dim))
    return loudness


def centred(own_key, shape, width, reach, cuts=(), held_as=jnp.bfloat16):
    factor_of = block_scale(own_key, shape, cuts, -0.22, 0.18) if cuts else 1.0
    entries = jax.random.normal(own_key, shape, jnp.float32) * width * factor_of
    return jnp.minimum(jnp.maximum(entries, -reach), reach).astype(held_as)


def setup_inputs(seed: int = 0) -> dict:
    key_list = jax.random.split(jax.random.key(seed), 12)
    return {
        "spectra": jnp.clip(jnp.exp(math.log(1.0) - 2.9957323 * jax.random.uniform(key_list[0], (K, POINTS), jnp.float32) ** block_scale(key_list[0], (K, POINTS), ((1, 256),), -0.2, 0.2)), 0.05, 1.0),
        "sea_mask": place_ends((jax.random.randint(key_list[1], (POINTS,), 0, 8) < 7).astype(jnp.int32), jax.random.fold_in(key_list[1], 1), 0, 1),
        "card_map": draw_card_map(jax.random.fold_in(key_list[11], 71), 0),
        "dia_table": place_ends(jax.random.randint(key_list[3], (4, K), 0, K), jax.random.fold_in(key_list[3], 1), 0, K - 1).astype(jnp.int32),
        "dia_coef": jnp.clip(jnp.exp(jax.random.uniform(key_list[4], (K,), jnp.float32, math.log(0.5), math.log(3.0))), 0.5, 3.0),
        "speed": jnp.clip(jnp.exp(jax.random.uniform(key_list[5], (K,), jnp.float32, math.log(0.1), math.log(0.6))), 0.1, 0.6),
        "stokes_weight": jnp.clip(jnp.exp(jax.random.uniform(key_list[6], (K,), jnp.float32, math.log(0.02), math.log(0.2))), 0.02, 0.2),
        "couple_point": draw_couple_point(jax.random.fold_in(key_list[11], 71), 0),
        "ocean_u": centred(key_list[8], (NZ, OX, OY), 1.0, 6.0, ((1, 256),), jnp.float32),
        "ocean_v": centred(key_list[9], (NZ, OX, OY), 1.0, 6.0, ((1, 256),), jnp.float32),
        "mixing": jnp.clip(jnp.exp(jax.random.uniform(key_list[10], (NZ,), jnp.float32, math.log(0.2), math.log(2.0))), 0.2, 2.0),
    }


DT_SRC = 0.5
CURRENT_GAIN = 0.3
DT_OCEAN = 0.2
VISCOSITY = 0.2
CORIOLIS = 1.0


def direction_cosines(index):
    theta = ((index % ND).astype(jnp.float32) + 0.5) * (2.0 * jnp.pi / ND)
    return jnp.cos(theta), jnp.sin(theta)


def source_terms(energy, table, coef):
    plus_one = energy[table[0]]
    minus_one = energy[table[1]]
    plus_two = energy[table[2]]
    minus_two = energy[table[3]]
    scale = coef[:, None]
    first = scale * (energy * energy * (plus_one + minus_one) - 2.0 * energy * plus_one * minus_one)
    second = scale * (energy * energy * (plus_two + minus_two) - 2.0 * energy * plus_two * minus_two)
    total = -2.0 * (first + second)
    total = total.at[table[0]].add(first).at[table[1]].add(first)
    total = total.at[table[2]].add(second).at[table[3]].add(second)
    return total


def along_columns(outgoing, incoming):
    dims = outgoing.ndim
    following = jnp.pad(incoming[..., 1:], [(0, 0)] * (dims - 1) + [(0, 1)])
    preceding = jnp.pad(outgoing[..., :-1], [(0, 0)] * (dims - 1) + [(1, 0)])
    return outgoing - incoming + following - preceding


def horizontal(values, prev_rows, next_rows):
    padded = jnp.pad(values, ((0, 0), (0, 0), (1, 1)))
    return next_rows + prev_rows + padded[:, :, 2:] + padded[:, :, :-2] - 4.0 * values


def vertical(values, mixing):
    above = jnp.concatenate([jnp.zeros_like(values[:1]), values[:-1]], 0)
    flux = mixing[:, None, None] * (values - above)
    below = jnp.concatenate([flux[1:], jnp.zeros_like(flux[:1])], 0)
    return below - flux


def reference(spectra, sea_mask, card_map, dia_table, dia_coef, speed, stokes_weight, couple_point, ocean_u, ocean_v, mixing):
    comp_count = ND * NF
    group_points = GROWS * GX
    slab_rows = POINTS // GX
    block_total = POINTS // PTS_DEV
    mask_float = sea_mask.astype(jnp.float32)

    def forcing(block):
        start = block * PTS_DEV
        energy = lax.dynamic_slice_in_dim(spectra, start, PTS_DEV, 1)
        weight = lax.dynamic_slice_in_dim(mask_float, start, PTS_DEV, 0)
        return weight * (energy + DT_SRC * source_terms(energy, dia_table, dia_coef))

    forced = lax.map(forcing, jnp.arange(block_total, dtype=jnp.int32))
    forced = jnp.transpose(forced, (1, 0, 2)).reshape(comp_count, POINTS)
    cosine, sine = direction_cosines(jnp.arange(comp_count, dtype=jnp.int32))
    weights = jnp.stack([stokes_weight * cosine, stokes_weight * sine])
    drift = jnp.dot(weights, forced, precision=lax.Precision.HIGHEST)
    position = card_map + (jnp.arange(POINTS, dtype=jnp.int32) // group_points) * group_points
    drift_grid = jnp.zeros((2, POINTS), jnp.float32).at[:, position].set(drift)

    ocean_rows = ocean_u.shape[1]
    cell_group = jnp.arange(ocean_rows, dtype=jnp.int32)[:, None] // (ocean_rows // N_GRP)
    valid = couple_point >= 0
    target = jnp.where(valid, couple_point + cell_group * group_points, POINTS)
    surface = jnp.stack([ocean_u[0], ocean_v[0], jnp.ones_like(ocean_u[0])]).reshape(3, -1)
    totals = jnp.zeros((3, POINTS + 1), jnp.float32).at[:, target.reshape(-1)].add(surface)[:, :POINTS]
    currents = (totals[:2] / (totals[2] + 1.0)).reshape(2, slab_rows, GX)

    grid = jnp.zeros((comp_count, POINTS), jnp.float32).at[:, position].set(forced)
    grid = grid.reshape(NF, ND, slab_rows, GX)
    cos_dir, sin_dir = direction_cosines(jnp.arange(ND, dtype=jnp.int32))

    def propagate(items):
        field, group_speed = items
        speed_x = group_speed[:, None, None] * cos_dir[:, None, None] + CURRENT_GAIN * currents[0]
        speed_y = group_speed[:, None, None] * sin_dir[:, None, None] + CURRENT_GAIN * currents[1]
        for substep in range(PSTEPS):
            out_x = jnp.maximum(speed_x, 0.0) * field
            in_x = jnp.minimum(speed_x, 0.0) * field
            out_y = jnp.maximum(speed_y, 0.0) * field
            in_y = jnp.minimum(speed_y, 0.0) * field
            prev_y = jnp.pad(out_y[:, :-1], ((0, 0), (1, 0), (0, 0)))
            next_y = jnp.pad(in_y[:, 1:], ((0, 0), (0, 1), (0, 0)))
            field = field - along_columns(out_x, in_x) - (out_y - in_y + next_y - prev_y)
        return field

    moved = lax.map(propagate, (grid, speed.reshape(NF, ND))).reshape(comp_count, POINTS)
    new_spectra = moved[:, position] * mask_float

    valid_float = valid.astype(jnp.float32)
    cell_point = jnp.where(valid, couple_point + cell_group * group_points, 0)
    drift_u = drift_grid[0][cell_point] * valid_float
    drift_v = drift_grid[1][cell_point] * valid_float
    coriolis = CORIOLIS * (0.5 + jnp.arange(ocean_rows, dtype=jnp.int32).astype(jnp.float32) / ocean_rows)[:, None]
    profile = jnp.exp(-3.0 * (jnp.arange(NZ, dtype=jnp.int32).astype(jnp.float32) + 0.5) / NZ)[:, None, None]
    current_u, current_v = ocean_u, ocean_v
    for substep in range(OSTEPS):
        padded_u = jnp.pad(current_u, ((0, 0), (1, 1), (0, 0)))
        padded_v = jnp.pad(current_v, ((0, 0), (1, 1), (0, 0)))
        lap_u = horizontal(current_u, padded_u[:, :-2], padded_u[:, 2:])
        lap_v = horizontal(current_v, padded_v[:, :-2], padded_v[:, 2:])
        next_u = current_u + DT_OCEAN * (VISCOSITY * lap_u + vertical(current_u, mixing) + coriolis * (current_v + profile * drift_v))
        next_v = current_v + DT_OCEAN * (VISCOSITY * lap_v + vertical(current_v, mixing) - coriolis * (current_u + profile * drift_u))
        current_u, current_v = next_u, next_v
    return (new_spectra, current_u, current_v)
```

```python
import jax
import jax.numpy as jnp
from jax import lax
from jax.experimental import pallas as pl
from jax.experimental.pallas import tpu as pltpu
from jax.sharding import PartitionSpec as P

ND = 36
NZ = 40
KC = 1296
KP = 1408
SHARE = 11
F32, BF16 = jnp.float32, jnp.bfloat16
NT = (((1,), (1,)), ((), ()))
HIGH = lax.Precision.HIGHEST
MESH = pl.DeviceIdType.MESH
VMEM_LIMIT = 56 << 20


def direction_cosines(index):
    theta = ((index % ND).astype(jnp.float32) + 0.5) * (2.0 * jnp.pi / ND)
    return (jnp.cos(theta), jnp.sin(theta))


def split(x):
    hi = x.astype(BF16)
    return hi, (x - hi.astype(F32)).astype(BF16)


def spread_matrix():
    wide = lax.broadcasted_iota(jnp.int32, (128, 768), 1)
    target = ((wide & 255) >> 1) + (wide >> 8) - 1
    return jnp.where(lax.broadcasted_iota(jnp.int32, (128, 768), 0) == target, 1.0, 0.0)


def couple_masks(cp, dev):
    row = (cp >> 7) - dev
    col = (cp & 127) - (lax.broadcasted_iota(jnp.int32, (8, 256), 1) >> 1)
    valid = cp >= 0
    return [
        [jnp.where(valid & (row == dr - 1) & (col == delta - 1), 1.0, 0.0) for delta in range(3)]
        for dr in range(3)
    ]


def partial_kernel(cp_ref, u_ref, v_ref, out_ref):
    masks = couple_masks(cp_ref[...], lax.axis_index("dev"))
    surface = [u_ref[...], v_ref[...], None]
    rows = []
    for dr in range(3):
        for q in range(3):
            parts = []
            for delta in range(3):
                m = masks[dr][delta]
                parts.append(jnp.sum(m if q == 2 else m * surface[q], axis=0, keepdims=True))
            rows.append(jnp.concatenate(parts, axis=1))
    rows.append(jnp.zeros((7, 768), F32))
    wide = jnp.concatenate(rows, axis=0)
    out_ref[...] = lax.dot_general(wide, spread_matrix(), NT, precision=HIGH, preferred_element_type=F32)


def dia_kernel(e_ref, mask_ref, trow_ref, col_ref, w_ref, cur_ref, out_ref, E, F1, F2, OH, forced_ref):
    CH = 432
    tail = jnp.zeros((KP - KC, 256), BF16)
    E[KC:, :] = tail
    F1[KC:, :] = tail
    F2[KC:, :] = tail
    hi, lo = split(e_ref[...])
    E[:KC, :128] = hi
    E[:KC, 128:] = lo

    def gather(i, _):
        rows = pl.ds(pl.multiple_of(i * CH, 16), CH)
        lanes = lax.broadcasted_iota(jnp.int32, (CH, KP), 1).astype(F32)
        e = e_ref[rows, :]
        cols = col_ref[rows, :]
        for m in range(4):
            OH[m * CH : (m + 1) * CH, :] = jnp.where(lanes == cols[:, m : m + 1], 1.0, 0.0).astype(BF16)
        p = jnp.dot(OH[...], E[...], preferred_element_type=F32)
        p = p[:, :128] + p[:, 128:]
        g = [p[m * CH : (m + 1) * CH] for m in range(4)]
        s = cols[:, 4:5]
        ee = e * e
        e2 = 2.0 * e
        a = s * (ee * (g[0] + g[1]) - e2 * g[0] * g[1])
        b = s * (ee * (g[2] + g[3]) - e2 * g[2] * g[3])
        forced_ref[rows, :] = e - (a + b)
        ah, al = split(a)
        bh, bl = split(b)
        F1[rows, :128] = ah
        F1[rows, 128:] = al
        F2[rows, :128] = bh
        F2[rows, 128:] = bl
        return 0

    lax.fori_loop(0, KC // CH, gather, 0)

    def scatter(i, _):
        rows = pl.ds(pl.multiple_of(i * CH, 16), CH)
        b = lax.broadcasted_iota(jnp.int32, (CH, KP), 0) + i * CH

        def onehot(m):
            return jnp.where(b == trow_ref[m : m + 1, :], 1.0, 0.0)

        p = jnp.dot((onehot(0) + onehot(1)).astype(BF16), F1[...], preferred_element_type=F32)
        p = p + jnp.dot((onehot(2) + onehot(3)).astype(BF16), F2[...], preferred_element_type=F32)
        forced_ref[rows, :] = mask_ref[...] * (forced_ref[rows, :] + 0.5 * (p[:, :128] + p[:, 128:]))
        return 0

    lax.fori_loop(0, KC // CH, scatter, 0)
    forced_ref[KC:, :] = jnp.zeros((KP - KC, 128), F32)
    drift = jnp.dot(w_ref[...], forced_ref[...], precision=HIGH, preferred_element_type=F32)
    extra = jnp.concatenate([drift[0:2], cur_ref[0:2, :], jnp.zeros((1, 128), F32)], axis=0)
    for d in range(128):
        out_ref[d, 0:SHARE, :] = forced_ref[d * SHARE : (d + 1) * SHARE, :]
        out_ref[d, SHARE:16, :] = extra


def build_maps(map_ref, CT, M, MF):
    def step(s, _):
        row = map_ref[pl.ds(s, 1), :]
        n = ((row >> 13) << 7) | (row & 127)
        rl = (row >> 7) & 63
        col = pl.ds(pl.multiple_of(s * 128, 128), 128)
        CT[:, col] = jnp.where(lax.broadcasted_iota(jnp.int32, (256, 128), 0) == n, 1.0, 0.0).astype(BF16)
        mf = jnp.where(lax.broadcasted_iota(jnp.int32, (64, 128), 0) == rl, 1.0, 0.0)
        MF[:, col] = mf
        M[:, col] = mf.astype(BF16)
        return 0

    lax.fori_loop(0, 128, step, 0)


def substep(f, cx, cy, first_lane, last_lane):
    ox = jnp.maximum(cx, 0.0) * f
    ix = jnp.minimum(cx, 0.0) * f
    oy = jnp.maximum(cy, 0.0) * f
    iy = jnp.minimum(cy, 0.0) * f
    rows = f.shape[0]
    nx = jnp.where(last_lane, 0.0, pltpu.roll(ix, 127, 1))
    px = jnp.where(first_lane, 0.0, pltpu.roll(ox, 1, 1))
    ny = pltpu.roll(iy, rows - 1, 0)
    py = pltpu.roll(oy, 1, 0)
    return f - (ox - ix + nx - px) - (oy - iy + ny - py)


S = 8
R = SHARE * 64


def grid_kernel(arr_ref, map_ref, speed_ref, out_ref, drift_ref, CT, M, MF, LH, acc, dacc, T, G, cur, edge, halo, send_sem, recv_sem):
    grp = lax.axis_index("grp")
    dev = lax.axis_index("dev")
    barrier = pltpu.get_barrier_semaphore()
    pl.semaphore_signal(barrier, inc=1, device_id=(1 - grp, dev), device_id_type=MESH)
    build_maps(map_ref, CT, M, MF)
    acc[...] = jnp.zeros_like(acc)
    dacc[...] = jnp.zeros_like(dacc)
    zero_row = jnp.zeros((1, 128), F32)

    def forward(i, _):
        drift_rows = []
        for j in range(S):
            cols = pl.ds(pl.multiple_of(i * (S * 128) + j * 128, 128), 128)
            c = slice(j * 128, (j + 1) * 128)
            for k in range(SHARE):
                x = jnp.broadcast_to(arr_ref[pl.ds(i * S + j, 1), k : k + 1, :].reshape(1, 128), (16, 128))
                hi, lo = split(x)
                for q in range(4):
                    m = M[q * 16 : (q + 1) * 16, cols]
                    r = k * 64 + q * 16
                    LH[r : r + 16, c] = m * hi
                    LH[R + r : R + r + 16, c] = m * lo
            row = map_ref[pl.ds(i * S + j, 1), :] >> 7
            pieces = []
            for q in range(2):
                x = arr_ref[pl.ds(i * S + j, 1), SHARE + q : SHARE + q + 1, :].reshape(1, 128)
                for dr in range(3):
                    pieces.append(jnp.where(row == dev + (dr - 1), x, zero_row))
            pieces += [zero_row, zero_row]
            piece = jnp.concatenate(pieces, axis=0)
            hi = piece.astype(BF16).astype(F32)
            drift_rows.append(jnp.concatenate([hi, piece - hi], axis=0).astype(BF16))
        c = CT[:, pl.ds(pl.multiple_of(i * (S * 128), 128), S * 128)]
        acc[...] += lax.dot_general(LH[:R], c, NT, preferred_element_type=F32) + lax.dot_general(
            LH[R:], c, NT, preferred_element_type=F32
        )
        dacc[...] += lax.dot_general(jnp.concatenate(drift_rows, axis=1), c, NT, preferred_element_type=F32)
        return 0

    lax.fori_loop(0, 128 // S, forward, 0)
    drift = dacc[0:8] + dacc[8:16]
    rowid = lax.broadcasted_iota(jnp.int32, (8, 128), 0)
    wave_row = dev + lax.rem(rowid, 3) - 1
    drift_ref[...] = jnp.where(wave_row >= 64, drift[:, 128:], drift[:, :128])

    top = grp == 0
    for k in range(SHARE):
        low = acc[k * 64 : (k + 1) * 64, 0:128]
        high = acc[k * 64 : (k + 1) * 64, 128:256]
        G[k, 8:72, :] = low
        G[k, 72:136, :] = high
        edge[0, k : k + 1, :] = jnp.where(top, high[63:64], low[0:1])
        edge[1, k : k + 1, :] = jnp.where(top, high[62:63], low[1:2])
    for q in range(2):
        for s in range(128):
            cur[q, 8 + s : 9 + s, :] = arr_ref[s : s + 1, 13 + q : 14 + q, :].reshape(1, 128)
        edge[0, SHARE + q : SHARE + q + 1, :] = jnp.where(top, cur[q, 135:136, :], cur[q, 8:9, :])
        edge[1, SHARE + q : SHARE + q + 1, :] = jnp.where(top, cur[q, 134:135, :], cur[q, 9:10, :])
    for r in range(2):
        edge[r, 13:16, :] = jnp.zeros((3, 128), F32)
    pl.semaphore_wait(barrier, 1)
    copy = pltpu.make_async_remote_copy(
        src_ref=edge, dst_ref=halo, send_sem=send_sem, recv_sem=recv_sem, device_id=(1 - grp, dev), device_id_type=MESH
    )
    copy.start()
    copy.wait()

    below_on = jnp.where(top, 1.0, 0.0)
    above_on = 1.0 - below_on
    blank = jnp.zeros((6, 128), F32)

    def pad(dst, k, index):
        h0 = halo[0, k : k + 1, :]
        h1 = halo[1, k : k + 1, :]
        dst[index, 0:8, :] = jnp.concatenate([blank, h1, h0], axis=0) * above_on
        dst[index, 136:144, :] = jnp.concatenate([h0, h1, blank], axis=0) * below_on

    for k in range(SHARE):
        pad(G, k, k)
    for q in range(2):
        pad(cur, SHARE + q, q)
    lane = lax.broadcasted_iota(jnp.int32, (144, 128), 1)
    line = lax.broadcasted_iota(jnp.int32, (144, 128), 0)
    first_lane, last_lane = lane == 0, lane == 127
    keep = jnp.where(line < 8, above_on, jnp.where(line >= 136, below_on, 1.0))

    def propagate(k, _):
        cx = cur[0] + speed_ref[0, k]
        cy = cur[1] + speed_ref[1, k]
        f = substep(G[k], cx, cy, first_lane, last_lane) * keep
        f = substep(f, cx, cy, first_lane, last_lane)
        hi, lo = split(f[8:136])
        r = pl.multiple_of(k * 64, 64)
        for h in range(2):
            LH[pl.ds(r, 64), h * 128 : (h + 1) * 128] = hi[h * 64 : (h + 1) * 64]
            LH[pl.ds(R + r, 64), h * 128 : (h + 1) * 128] = lo[h * 64 : (h + 1) * 64]
        return 0

    lax.fori_loop(0, SHARE, propagate, 0)

    def backward(i, _):
        c = CT[:, pl.ds(pl.multiple_of(i * (S * 128), 128), S * 128)]
        T[...] = jnp.dot(LH[:R, 0:256], c, preferred_element_type=F32) + jnp.dot(
            LH[R:, 0:256], c, preferred_element_type=F32
        )
        for j in range(S):
            m = MF[:, pl.ds(pl.multiple_of(i * (S * 128) + j * 128, 128), 128)]
            for k in range(SHARE):
                r = jnp.sum(T[k * 64 : (k + 1) * 64, j * 128 : (j + 1) * 128] * m, axis=0, keepdims=True)
                out_ref[pl.ds(i * S + j, 1), k : k + 1, :] = r.reshape(1, 1, 128)
            out_ref[pl.ds(i * S + j, 1), SHARE:16, :] = jnp.zeros((1, 16 - SHARE, 128), F32)
        return 0

    lax.fori_loop(0, 128 // S, backward, 0)


def cells_kernel(drift_ref, cp_ref, out_ref):
    masks = couple_masks(cp_ref[...], lax.axis_index("dev"))
    wide = jnp.dot(drift_ref[...], spread_matrix(), precision=HIGH, preferred_element_type=F32)
    for q in range(2):
        total = jnp.zeros((8, 256), F32)
        for dr in range(3):
            for delta in range(3):
                total = total + masks[dr][delta] * wide[q * 3 + dr : q * 3 + dr + 1, delta * 256 : (delta + 1) * 256]
        out_ref[q * 8 : (q + 1) * 8, :] = total


def ocean_kernel(u_ref, v_ref, uh_ref, vh_ref, d_ref, dh_ref, mix_ref, prof_ref, ou_ref, ov_ref, A, B):
    grp = lax.axis_index("grp")
    dev = lax.axis_index("dev")
    start = (grp * 128 + dev) * 8
    line = lax.broadcasted_iota(jnp.int32, (24, 256), 0)
    lane = lax.broadcasted_iota(jnp.int32, (24, 256), 1)
    world = start + line - 8
    keep = jnp.where((world >= 0) & (world < 2048), 1.0, 0.0)
    f = 0.5 + world.astype(F32) / 2048.0
    first_lane, last_lane = lane == 0, lane == 255
    blank = jnp.zeros((6, 256), F32)

    def drift_block(q):
        return jnp.concatenate(
            [blank, dh_ref[0, q], d_ref[q * 8 : (q + 1) * 8, :], dh_ref[1, q], blank], axis=0
        )

    us, vs = drift_block(0), drift_block(1)

    def load(z, _):
        A[0, z] = jnp.concatenate([blank, uh_ref[0, z], u_ref[z], uh_ref[1, z], blank], axis=0)
        A[1, z] = jnp.concatenate([blank, vh_ref[0, z], v_ref[z], vh_ref[1, z], blank], axis=0)
        return 0

    lax.fori_loop(0, NZ, load, 0)

    def lap(a):
        r = jnp.where(last_lane, 0.0, pltpu.roll(a, 255, 1)) + jnp.where(first_lane, 0.0, pltpu.roll(a, 1, 1))
        return r + pltpu.roll(a, 1, 0) + pltpu.roll(a, 23, 0) - 4.0 * a

    def step(src, emit):
        def level(z, carry):
            pu, pv = carry
            u, v = src[0, z], src[1, z]
            last = z == NZ - 1
            zn = jnp.minimum(z + 1, NZ - 1)
            m0 = mix_ref[0, z]
            m1 = jnp.where(last, 0.0, mix_ref[0, zn])
            nu, nv = src[0, zn], src[1, zn]
            p = prof_ref[0, z]
            wu = m1 * (nu - u) - m0 * (u - pu)
            wv = m1 * (nv - v) - m0 * (v - pv)
            emit(z, u + 0.2 * (0.2 * lap(u) + wu + f * (v + p * vs)), v + 0.2 * (0.2 * lap(v) + wv - f * (u + p * us)))
            return u, v

        zero = jnp.zeros((24, 256), F32)
        lax.fori_loop(0, NZ, level, (zero, zero))

    def emit1(z, u, v):
        B[0, z] = u * keep
        B[1, z] = v * keep

    def emit2(z, u, v):
        ou_ref[z] = u[8:16]
        ov_ref[z] = v[8:16]

    step(A, emit1)
    step(B, emit2)


def neighbours(x, axis):
    n = lax.axis_size(axis)
    up = [(i, i + 1) for i in range(n - 1)]
    return lambda last, first: (lax.ppermute(last, axis, up), lax.ppermute(first, axis, [(b, a) for a, b in up]))


def params(**kw):
    return pltpu.CompilerParams(vmem_limit_bytes=VMEM_LIMIT, **kw)


def body(spectra, sea_mask, card_map, dia_table, dia_coef, speed, stokes_weight, couple_point, ocean_u, ocean_v, mixing):
    group = lax.axis_index("grp")
    device = lax.axis_index("dev")
    sds = jax.ShapeDtypeStruct
    both = ("grp", "dev")
    swap = neighbours(None, both)
    uh = jnp.stack(swap(ocean_u[:, 6:8], ocean_u[:, 0:2]))
    vh = jnp.stack(swap(ocean_v[:, 6:8], ocean_v[:, 0:2]))
    part = pl.pallas_call(partial_kernel, out_shape=sds((16, 128), F32), name="partials")(
        couple_point, ocean_u[0], ocean_v[0]
    )
    before, after = neighbours(None, "dev")(part[6:9], part[0:3])
    totals = part[3:6] + before + after
    cur = 0.3 * totals[:2] / (totals[2] + 1.0)
    cur = jnp.pad(cur, ((0, 6), (0, 0)))
    cosine, sine = direction_cosines(jnp.arange(KC, dtype=jnp.int32))
    weights = jnp.pad(jnp.stack([stokes_weight * cosine, stokes_weight * sine]), ((0, 6), (0, KP - KC)))
    trow = jnp.pad(dia_table, ((0, 4), (0, KP - KC)), constant_values=-1)
    col = jnp.concatenate([dia_table.T.astype(F32), dia_coef[:, None], jnp.zeros((KC, 3), F32)], axis=1)
    mask = sea_mask.astype(F32)[None, :]
    payload = pl.pallas_call(
        dia_kernel,
        out_shape=sds((128, 16, 128), F32),
        scratch_shapes=[pltpu.VMEM((KP, 256), BF16)] * 3 + [pltpu.VMEM((4 * 432, KP), BF16), pltpu.VMEM((KP, 128), F32)],
        compiler_params=params(),
        name="sources",
    )(spectra, mask, trow, col, weights, cur)
    arrived = lax.all_to_all(payload, "dev", split_axis=0, concat_axis=0, tiled=True)
    map2d = lax.dynamic_slice_in_dim(card_map, group * 16384, 16384, 0).reshape(128, 128)
    speeds = jnp.pad(jnp.stack([speed * cosine, speed * sine]), ((0, 0), (0, KP - KC)))
    speeds = jnp.pad(lax.dynamic_slice_in_dim(speeds, device * SHARE, SHARE, 1), ((0, 0), (0, 16 - SHARE)))
    vmem = pl.BlockSpec(memory_space=pltpu.VMEM)
    smem = pl.BlockSpec(memory_space=pltpu.SMEM)
    leaving, drift = pl.pallas_call(
        grid_kernel,
        out_shape=(sds((128, 16, 128), F32), sds((8, 128), F32)),
        in_specs=[vmem, vmem, smem],
        out_specs=(vmem, vmem),
        scratch_shapes=[
            pltpu.VMEM((256, 16384), BF16),
            pltpu.VMEM((64, 16384), BF16),
            pltpu.VMEM((64, 16384), F32),
            pltpu.VMEM((2 * R, S * 128), BF16),
            pltpu.VMEM((R, 256), F32),
            pltpu.VMEM((16, 256), F32),
            pltpu.VMEM((R, S * 128), F32),
            pltpu.VMEM((SHARE, 144, 128), F32),
            pltpu.VMEM((2, 144, 128), F32),
            pltpu.VMEM((2, 16, 128), F32),
            pltpu.VMEM((2, 16, 128), F32),
            pltpu.SemaphoreType.DMA,
            pltpu.SemaphoreType.DMA,
        ],
        compiler_params=params(collective_id=0, has_side_effects=True),
        name="grid",
    )(arrived, map2d, speeds)
    returned = lax.all_to_all(leaving, "dev", split_axis=0, concat_axis=0, tiled=True)
    new_spectra = returned[:, :SHARE].reshape(KP, 128)[:KC] * mask
    cells = pl.pallas_call(cells_kernel, out_shape=sds((16, 256), F32), name="cells")(drift, couple_point)
    cells3 = cells.reshape(2, 8, 256)
    dh = jnp.stack(swap(cells3[:, 6:8], cells3[:, 0:2]))
    profile = jnp.exp(-3.0 * (jnp.arange(NZ, dtype=jnp.int32).astype(F32) + 0.5) / NZ)[None, :]
    new_u, new_v = pl.pallas_call(
        ocean_kernel,
        out_shape=(sds((NZ, 8, 256), F32), sds((NZ, 8, 256), F32)),
        in_specs=[vmem] * 6 + [smem, smem],
        out_specs=(vmem, vmem),
        scratch_shapes=[pltpu.VMEM((2, NZ, 24, 256), F32)] * 2,
        compiler_params=params(),
        name="ocean",
    )(ocean_u, ocean_v, uh, vh, cells, dh, mixing[None, :], profile)
    return (new_spectra, new_u, new_v)


def solution(mesh):
    both = ("grp", "dev")
    in_specs = (P(None, both), P(both), P(), P(), P(), P(), P(), P(both, None), P(None, both, None), P(None, both, None), P())
    out_specs = (P(None, both), P(None, both, None), P(None, both, None))
    return jax.shard_map(body, mesh=mesh, in_specs=in_specs, out_specs=out_specs, check_vma=False)
```

```python
import jax
import jax.numpy as jnp
from jax import lax
from jax.experimental import pallas as pl
from jax.experimental.pallas import tpu as pltpu
from jax.sharding import PartitionSpec as P

ND = 36
NZ = 40
KC = 1296
KP = 1408
SHARE = 11
F32, BF16 = jnp.float32, jnp.bfloat16
NT = (((1,), (1,)), ((), ()))
HIGH = lax.Precision.HIGHEST
MESH = pl.DeviceIdType.MESH
VMEM_LIMIT = 56 << 20


def direction_cosines(index):
    theta = ((index % ND).astype(jnp.float32) + 0.5) * (2.0 * jnp.pi / ND)
    return (jnp.cos(theta), jnp.sin(theta))


def split(x):
    hi = x.astype(BF16)
    return hi, (x - hi.astype(F32)).astype(BF16)


def spread_matrix():
    wide = lax.broadcasted_iota(jnp.int32, (128, 768), 1)
    target = ((wide & 255) >> 1) + (wide >> 8) - 1
    return jnp.where(lax.broadcasted_iota(jnp.int32, (128, 768), 0) == target, 1.0, 0.0)


def couple_masks(cp, dev):
    row = (cp >> 7) - dev
    col = (cp & 127) - (lax.broadcasted_iota(jnp.int32, (8, 256), 1) >> 1)
    valid = cp >= 0
    return [
        [jnp.where(valid & (row == dr - 1) & (col == delta - 1), 1.0, 0.0) for delta in range(3)]
        for dr in range(3)
    ]


def build_maps(map_ref, CT, M, MF):
    def step(s, _):
        row = map_ref[pl.ds(s, 1), :]
        n = ((row >> 13) << 7) | (row & 127)
        rl = (row >> 7) & 63
        col = pl.ds(pl.multiple_of(s * 128, 128), 128)
        CT[:, col] = jnp.where(lax.broadcasted_iota(jnp.int32, (256, 128), 0) == n, 1.0, 0.0).astype(BF16)
        mf = jnp.where(lax.broadcasted_iota(jnp.int32, (64, 128), 0) == rl, 1.0, 0.0)
        MF[:, col] = mf
        M[:, col] = mf.astype(BF16)
        return 0

    lax.fori_loop(0, 128, step, 0)


def substep(f, cx, cy, first_lane, last_lane):
    ox = jnp.maximum(cx, 0.0) * f
    ix = jnp.minimum(cx, 0.0) * f
    oy = jnp.maximum(cy, 0.0) * f
    iy = jnp.minimum(cy, 0.0) * f
    rows = f.shape[0]
    nx = jnp.where(last_lane, 0.0, pltpu.roll(ix, 127, 1))
    px = jnp.where(first_lane, 0.0, pltpu.roll(ox, 1, 1))
    ny = pltpu.roll(iy, rows - 1, 0)
    py = pltpu.roll(oy, 1, 0)
    return f - (ox - ix + nx - px) - (oy - iy + ny - py)


S = 8
R = SHARE * 64
ROWS = SHARE + 2
CH = 432


def chunk_offset(i):
    return jnp.where(i % 2 == 1, (i + 1) // 2, 16 - i // 2)


def wait_for(ref, sem):
    pltpu.make_async_copy(ref, ref, sem).wait()


def step_kernel(
    e_ref, mask_ref, trow_ref, col_ref, w_ref, map_ref, speed_ref, cp_ref, u_ref, v_ref, mix_ref, prof_ref,
    ret, ou_ref, ov_ref,
    E, F1, F2, OH, forced_ref, payload, arr, outb, CT, M, MF, LH, acc, dacc, T, G, cur, edge, halo,
    part, pin, cb, curb, ostage, ohalo, B,
    o_send, o_recv, p_send, p_recv, c_send, c_recv, a_send, a_recv, h_send, h_recv, r_send, r_recv,
):
    grp = lax.axis_index("grp")
    dev = lax.axis_index("dev")
    q16 = dev // 8
    linear = grp * 128 + dev
    has_up = linear > 0
    has_down = linear < 255
    up = linear + 255
    up_id = ((up // 128) % 2, up % 128)
    down = linear + 1
    down_id = ((down // 128) % 2, down % 128)

    barrier = pltpu.get_barrier_semaphore()

    def greet(i, _):
        pl.semaphore_signal(barrier, inc=1, device_id=(grp, (dev + i) % 128), device_id_type=MESH)
        return 0

    lax.fori_loop(1, 128, greet, 0)
    pl.semaphore_signal(barrier, inc=1, device_id=(1 - grp, dev), device_id_type=MESH)
    crosses_down = (grp == 0) & (dev == 127)
    crosses_up = (grp == 1) & (dev == 0)

    @pl.when(crosses_down)
    def _():
        pl.semaphore_signal(barrier, inc=1, device_id=down_id, device_id_type=MESH)

    @pl.when(crosses_up)
    def _():
        pl.semaphore_signal(barrier, inc=1, device_id=up_id, device_id_type=MESH)

    masks = couple_masks(cp_ref[...], dev)
    surface = [u_ref[0], v_ref[0]]
    rows = []
    for dr in range(3):
        for q in range(3):
            pieces = []
            for delta in range(3):
                m = masks[dr][delta]
                pieces.append(jnp.sum(m if q == 2 else m * surface[q], axis=0, keepdims=True))
            rows.append(jnp.concatenate(pieces, axis=1))
        rows.append(jnp.zeros((5, 768), F32))
    sums = lax.dot_general(
        jnp.concatenate(rows, axis=0), spread_matrix(), NT, precision=HIGH, preferred_element_type=F32
    )
    for dr in range(3):
        part[dr] = sums[dr * 8 : (dr + 1) * 8]

    def stage_ocean(slot, a, b):
        def level(z, _):
            for side, line in ((0, 0), (1, 7)):
                ostage[slot, side, 0, pl.ds(z, 1), :] = a(z)[line : line + 1]
                ostage[slot, side, 1, pl.ds(z, 1), :] = b(z)[line : line + 1]
            return 0

        lax.fori_loop(0, NZ, level, 0)

    stage_ocean(0, lambda z: u_ref[z], lambda z: v_ref[z])
    build_maps(map_ref, CT, M, MF)

    pl.semaphore_wait(barrier, 128 + jnp.where(crosses_down | crosses_up, 1, 0))

    def ocean_copy(slot, side):
        return pltpu.make_async_remote_copy(
            src_ref=ostage.at[slot, side],
            dst_ref=ohalo.at[slot, 1 - side],
            send_sem=o_send.at[slot, side],
            recv_sem=o_recv.at[slot, 1 - side],
            device_id=up_id if side == 0 else down_id,
            device_id_type=MESH,
        )

    def ocean_start(slot):
        for side, there in ((0, has_up), (1, has_down)):
            @pl.when(there)
            def _(side=side):
                ocean_copy(slot, side).start()

    def ocean_wait(slot):
        for side, there in ((0, has_up), (1, has_down)):
            @pl.when(there)
            def _(side=side):
                wait_for(ostage.at[slot, side], o_send.at[slot, side])
                wait_for(ohalo.at[slot, side], o_recv.at[slot, side])

    def part_copy(side):
        return pltpu.make_async_remote_copy(
            src_ref=part.at[2 * side],
            dst_ref=pin.at[1 - side],
            send_sem=p_send.at[side],
            recv_sem=p_recv.at[1 - side],
            device_id=(grp, (dev + 127 + 2 * side) % 128),
            device_id_type=MESH,
        )

    for side, there in ((0, dev > 0), (1, dev < 127)):
        @pl.when(there)
        def _(side=side):
            part_copy(side).start()

    ocean_start(0)

    tail = jnp.zeros((KP - KC, 256), BF16)
    E[KC:, :] = tail
    F1[KC:, :] = tail
    F2[KC:, :] = tail
    hi, lo = split(e_ref[...])
    E[:KC, :128] = hi
    E[:KC, 128:] = lo

    def gather(i, _):
        rows = pl.ds(pl.multiple_of(i * CH, 16), CH)
        lanes = lax.broadcasted_iota(jnp.int32, (CH, KP), 1).astype(F32)
        e = e_ref[rows, :]
        cols = col_ref[rows, :]
        for m in range(4):
            OH[m * CH : (m + 1) * CH, :] = jnp.where(lanes == cols[:, m : m + 1], 1.0, 0.0).astype(BF16)
        p = jnp.dot(OH[...], E[...], preferred_element_type=F32)
        p = p[:, :128] + p[:, 128:]
        g = [p[m * CH : (m + 1) * CH] for m in range(4)]
        s = cols[:, 4:5]
        ee = e * e
        e2 = 2.0 * e
        a = s * (ee * (g[0] + g[1]) - e2 * g[0] * g[1])
        b = s * (ee * (g[2] + g[3]) - e2 * g[2] * g[3])
        forced_ref[rows, :] = e - (a + b)
        ah, al = split(a)
        bh, bl = split(b)
        F1[rows, :128] = ah
        F1[rows, 128:] = al
        F2[rows, :128] = bh
        F2[rows, 128:] = bl
        return 0

    lax.fori_loop(0, KC // CH, gather, 0)

    for side, there in ((0, dev > 0), (1, dev < 127)):
        @pl.when(there)
        def _(side=side):
            wait_for(part.at[2 * side], p_send.at[side])
            wait_for(pin.at[side], p_recv.at[side])

    total = part[1] + jnp.where(dev > 0, pin[0], 0.0) + jnp.where(dev < 127, pin[1], 0.0)
    speeds = 0.3 * total[0:2] / (total[2:3] + 1.0)
    for q in range(2):
        cb[q] = speeds[q : q + 1]
        curb[dev, q] = speeds[q : q + 1]

    def tell(i, _):
        pltpu.make_async_remote_copy(
            src_ref=cb,
            dst_ref=curb.at[dev],
            send_sem=c_send,
            recv_sem=c_recv,
            device_id=(grp, (dev + i) % 128),
            device_id_type=MESH,
        ).start()
        return 0

    lax.fori_loop(1, 128, tell, 0)

    def scatter(i, _):
        rows = pl.ds(pl.multiple_of(i * CH, 16), CH)
        b = lax.broadcasted_iota(jnp.int32, (CH, KP), 0) + i * CH

        def onehot(m):
            return jnp.where(b == trow_ref[m : m + 1, :], 1.0, 0.0)

        p = jnp.dot((onehot(0) + onehot(1)).astype(BF16), F1[...], preferred_element_type=F32)
        p = p + jnp.dot((onehot(2) + onehot(3)).astype(BF16), F2[...], preferred_element_type=F32)
        forced_ref[rows, :] = mask_ref[...] * (forced_ref[rows, :] + 0.5 * (p[:, :128] + p[:, 128:]))
        return 0

    lax.fori_loop(0, KC // CH, scatter, 0)
    forced_ref[KC:, :] = jnp.zeros((KP - KC, 128), F32)
    drift_own = jnp.dot(w_ref[...], forced_ref[...], precision=HIGH, preferred_element_type=F32)

    def fill(d, _):
        for k in range(SHARE):
            payload[d, k] = forced_ref[pl.ds(d * SHARE + k, 1), :]
        for q in range(2):
            payload[d, SHARE + q] = drift_own[q : q + 1]
        return 0

    lax.fori_loop(0, 128, fill, 0)

    pltpu.make_async_copy(payload.at[dev], arr.at[dev], a_recv.at[q16]).start()

    def send(n, _):
        dest = ((q16 + 16 - chunk_offset(n // 8)) % 16) * 8 + (dev + n) % 8
        pltpu.make_async_remote_copy(
            src_ref=payload.at[dest],
            dst_ref=arr.at[dev],
            send_sem=a_send,
            recv_sem=a_recv.at[q16],
            device_id=(grp, dest),
            device_id_type=MESH,
        ).start()
        return 0

    lax.fori_loop(1, 128, send, 0)

    wait_for(curb.at[pl.ds(0, 127)], c_send)
    wait_for(curb.at[pl.ds(0, 127)], c_recv)

    def place(s, _):
        for q in range(2):
            cur[q, pl.ds(8 + s, 1), :] = curb[s, q]
        return 0

    lax.fori_loop(0, 128, place, 0)
    acc[...] = jnp.zeros_like(acc)
    dacc[...] = jnp.zeros_like(dacc)
    zero_row = jnp.zeros((1, 128), F32)

    def forward(i, _):
        chunk = (q16 + chunk_offset(i)) % 16
        wait_for(arr.at[pl.ds(chunk * S, S)], a_recv.at[chunk])
        drift_rows = []
        for j in range(S):
            s = chunk * S + j
            cols = pl.ds(pl.multiple_of(s * 128, 128), 128)
            c = slice(j * 128, (j + 1) * 128)
            for k in range(SHARE):
                x = jnp.broadcast_to(arr[s, k], (16, 128))
                hi, lo = split(x)
                for q in range(4):
                    m = M[q * 16 : (q + 1) * 16, cols]
                    r = k * 64 + q * 16
                    LH[r : r + 16, c] = m * hi
                    LH[R + r : R + r + 16, c] = m * lo
            row = map_ref[pl.ds(s, 1), :] >> 7
            pieces = []
            for q in range(2):
                x = arr[s, SHARE + q]
                for dr in range(3):
                    pieces.append(jnp.where(row == dev + (dr - 1), x, zero_row))
            pieces += [zero_row, zero_row]
            piece = jnp.concatenate(pieces, axis=0)
            hi = piece.astype(BF16).astype(F32)
            drift_rows.append(jnp.concatenate([hi, piece - hi], axis=0).astype(BF16))
        c = CT[:, pl.ds(pl.multiple_of(chunk * (S * 128), 128), S * 128)]
        acc[...] += lax.dot_general(LH[:R], c, NT, preferred_element_type=F32) + lax.dot_general(
            LH[R:], c, NT, preferred_element_type=F32
        )
        dacc[...] += lax.dot_general(jnp.concatenate(drift_rows, axis=1), c, NT, preferred_element_type=F32)
        return 0

    lax.fori_loop(0, 128 // S, forward, 0)

    top = grp == 0
    for k in range(SHARE):
        low = acc[k * 64 : (k + 1) * 64, 0:128]
        high = acc[k * 64 : (k + 1) * 64, 128:256]
        G[k, 8:72, :] = low
        G[k, 72:136, :] = high
        edge[0, k : k + 1, :] = jnp.where(top, high[63:64], low[0:1])
        edge[1, k : k + 1, :] = jnp.where(top, high[62:63], low[1:2])
    for q in range(2):
        edge[0, SHARE + q : SHARE + q + 1, :] = jnp.where(top, cur[q, 135:136, :], cur[q, 8:9, :])
        edge[1, SHARE + q : SHARE + q + 1, :] = jnp.where(top, cur[q, 134:135, :], cur[q, 9:10, :])
    for r in range(2):
        edge[r, 13:16, :] = jnp.zeros((3, 128), F32)
    exchange = pltpu.make_async_remote_copy(
        src_ref=edge, dst_ref=halo, send_sem=h_send, recv_sem=h_recv, device_id=(1 - grp, dev), device_id_type=MESH
    )
    exchange.start()

    drift = dacc[0:8] + dacc[8:16]
    wave_row = dev + lax.rem(lax.broadcasted_iota(jnp.int32, (8, 128), 0), 3) - 1
    drift = jnp.where(wave_row >= 64, drift[:, 128:], drift[:, :128])
    wide = jnp.dot(drift, spread_matrix(), precision=HIGH, preferred_element_type=F32)
    masks = couple_masks(cp_ref[...], dev)
    cells = []
    for q in range(2):
        sum_q = jnp.zeros((8, 256), F32)
        for dr in range(3):
            for delta in range(3):
                sum_q = sum_q + masks[dr][delta] * wide[q * 3 + dr : q * 3 + dr + 1, delta * 256 : (delta + 1) * 256]
        cells.append(sum_q)
    us, vs = cells

    oline = lax.broadcasted_iota(jnp.int32, (8, 256), 0)
    olane = lax.broadcasted_iota(jnp.int32, (8, 256), 1)
    coriolis = 0.5 + (linear * 8 + oline).astype(F32) / 2048.0
    fvs, fus = coriolis * vs, coriolis * us

    def ocean_step(slot, source, emit):
        def lap(a, z, q):
            above = jnp.where(has_up, ohalo[slot, 0, q, pl.ds(z, 1), :], 0.0)
            below = jnp.where(has_down, ohalo[slot, 1, q, pl.ds(z, 1), :], 0.0)
            r = jnp.where(olane == 255, 0.0, pltpu.roll(a, 255, 1)) + jnp.where(olane == 0, 0.0, pltpu.roll(a, 1, 1))
            r = r + jnp.where(oline == 0, above, pltpu.roll(a, 1, 0)) + jnp.where(oline == 7, below, pltpu.roll(a, 7, 0))
            return r - 4.0 * a

        def level(z, carry):
            pu, pv = carry
            u, v = source(0, z), source(1, z)
            zn = jnp.minimum(z + 1, NZ - 1)
            m0 = mix_ref[0, z]
            m1 = jnp.where(z == NZ - 1, 0.0, mix_ref[0, zn])
            nu, nv = source(0, zn), source(1, zn)
            p = prof_ref[0, z]
            wu = m1 * (nu - u) - m0 * (u - pu)
            wv = m1 * (nv - v) - m0 * (v - pv)
            emit(
                z,
                u + 0.2 * (0.2 * lap(u, z, 0) + wu + coriolis * v + p * fvs),
                v + 0.2 * (0.2 * lap(v, z, 1) + wv - coriolis * u - p * fus),
            )
            return u, v

        zero = jnp.zeros((8, 256), F32)
        lax.fori_loop(0, NZ, level, (zero, zero))

    def emit1(z, u, v):
        B[0, z] = u
        B[1, z] = v

    def emit2(z, u, v):
        ou_ref[z] = u
        ov_ref[z] = v

    ocean_wait(0)
    ocean_step(0, lambda q, z: (u_ref, v_ref)[q][z], emit1)
    stage_ocean(1, lambda z: B[0, z], lambda z: B[1, z])
    ocean_start(1)

    exchange.wait()
    below_on = jnp.where(top, 1.0, 0.0)
    above_on = 1.0 - below_on
    blank = jnp.zeros((6, 128), F32)

    def pad(dst, k, index):
        h0 = halo[0, k : k + 1, :]
        h1 = halo[1, k : k + 1, :]
        dst[index, 0:8, :] = jnp.concatenate([blank, h1, h0], axis=0) * above_on
        dst[index, 136:144, :] = jnp.concatenate([h0, h1, blank], axis=0) * below_on

    for k in range(SHARE):
        pad(G, k, k)
    for q in range(2):
        pad(cur, SHARE + q, q)
    lane = lax.broadcasted_iota(jnp.int32, (144, 128), 1)
    line = lax.broadcasted_iota(jnp.int32, (144, 128), 0)
    first_lane, last_lane = lane == 0, lane == 127
    keep = jnp.where(line < 8, above_on, jnp.where(line >= 136, below_on, 1.0))

    def propagate(k, _):
        cx = cur[0] + speed_ref[0, k]
        cy = cur[1] + speed_ref[1, k]
        f = substep(G[k], cx, cy, first_lane, last_lane) * keep
        f = substep(f, cx, cy, first_lane, last_lane)
        hi, lo = split(f[8:136])
        r = pl.multiple_of(k * 64, 64)
        for h in range(2):
            LH[pl.ds(r, 64), h * 128 : (h + 1) * 128] = hi[h * 64 : (h + 1) * 64]
            LH[pl.ds(R + r, 64), h * 128 : (h + 1) * 128] = lo[h * 64 : (h + 1) * 64]
        return 0

    lax.fori_loop(0, SHARE, propagate, 0)

    def backward(t, _):
        i = 15 - t
        chunk = (q16 + 16 - chunk_offset(i)) % 16
        c = CT[:, pl.ds(pl.multiple_of(chunk * (S * 128), 128), S * 128)]
        T[...] = jnp.dot(LH[:R, 0:256], c, preferred_element_type=F32) + jnp.dot(
            LH[R:, 0:256], c, preferred_element_type=F32
        )
        for j in range(S):
            s = chunk * S + j
            m = MF[:, pl.ds(pl.multiple_of(s * 128, 128), 128)]
            for k in range(SHARE):
                outb[s, k] = jnp.sum(T[k * 64 : (k + 1) * 64, j * 128 : (j + 1) * 128] * m, axis=0, keepdims=True)

        def post(j, _):
            s = chunk * S + j

            @pl.when(s != dev)
            def _():
                pltpu.make_async_remote_copy(
                    src_ref=outb.at[s],
                    dst_ref=ret.at[pl.ds(dev * SHARE, SHARE)],
                    send_sem=r_send,
                    recv_sem=r_recv,
                    device_id=(grp, s),
                    device_id_type=MESH,
                ).start()

            return 0

        lax.fori_loop(0, S, post, 0)
        return 0

    lax.fori_loop(0, 128 // S, backward, 0)
    for k in range(SHARE):
        ret[dev * SHARE + k] = outb[dev, k]

    ocean_wait(1)
    ocean_step(1, lambda q, z: B[q, z], emit2)

    wait_for(payload.at[pl.ds(0, 127)], a_send)
    wait_for(outb.at[pl.ds(0, 127)], r_send)
    wait_for(ret.at[pl.ds(0, 127 * SHARE)], r_recv)


def body(spectra, sea_mask, card_map, dia_table, dia_coef, speed, stokes_weight, couple_point, ocean_u, ocean_v, mixing):
    group = lax.axis_index("grp")
    device = lax.axis_index("dev")
    sds = jax.ShapeDtypeStruct
    cosine, sine = direction_cosines(jnp.arange(KC, dtype=jnp.int32))
    weights = jnp.pad(jnp.stack([stokes_weight * cosine, stokes_weight * sine]), ((0, 6), (0, KP - KC)))
    trow = jnp.pad(dia_table, ((0, 4), (0, KP - KC)), constant_values=-1)
    col = jnp.concatenate([dia_table.T.astype(F32), dia_coef[:, None], jnp.zeros((KC, 3), F32)], axis=1)
    mask = sea_mask.astype(F32)[None, :]
    map2d = lax.dynamic_slice_in_dim(card_map, group * 16384, 16384, 0).reshape(128, 128)
    speeds = jnp.pad(jnp.stack([speed * cosine, speed * sine]), ((0, 0), (0, KP - KC)))
    speeds = jnp.pad(lax.dynamic_slice_in_dim(speeds, device * SHARE, SHARE, 1), ((0, 0), (0, 16 - SHARE)))
    profile = jnp.exp(-3.0 * (jnp.arange(NZ, dtype=jnp.int32).astype(F32) + 0.5) / NZ)[None, :]
    vmem = pl.BlockSpec(memory_space=pltpu.VMEM)
    smem = pl.BlockSpec(memory_space=pltpu.SMEM)
    dma = pltpu.SemaphoreType.DMA
    scratch = [
        pltpu.VMEM((KP, 256), BF16),
        pltpu.VMEM((KP, 256), BF16),
        pltpu.VMEM((KP, 256), BF16),
        pltpu.VMEM((4 * CH, KP), BF16),
        pltpu.VMEM((KP, 128), F32),
        pltpu.VMEM((128, ROWS, 1, 128), F32),
        pltpu.VMEM((128, ROWS, 1, 128), F32),
        pltpu.VMEM((128, SHARE, 1, 128), F32),
        pltpu.VMEM((256, 16384), BF16),
        pltpu.VMEM((64, 16384), BF16),
        pltpu.VMEM((64, 16384), F32),
        pltpu.VMEM((2 * R, S * 128), BF16),
        pltpu.VMEM((R, 256), F32),
        pltpu.VMEM((16, 256), F32),
        pltpu.VMEM((R, S * 128), F32),
        pltpu.VMEM((SHARE, 144, 128), F32),
        pltpu.VMEM((2, 144, 128), F32),
        pltpu.VMEM((2, 16, 128), F32),
        pltpu.VMEM((2, 16, 128), F32),
        pltpu.VMEM((3, 8, 128), F32),
        pltpu.VMEM((2, 8, 128), F32),
        pltpu.VMEM((2, 1, 128), F32),
        pltpu.VMEM((128, 2, 1, 128), F32),
        pltpu.VMEM((2, 2, 2, NZ, 256), F32),
        pltpu.VMEM((2, 2, 2, NZ, 256), F32),
        pltpu.VMEM((2, NZ, 8, 256), F32),
        dma((2, 2)), dma((2, 2)), dma((2,)), dma((2,)), dma, dma, dma, dma((16,)), dma, dma, dma, dma,
    ]
    ret, new_u, new_v = pl.pallas_call(
        step_kernel,
        out_shape=(sds((KP, 1, 128), F32), sds((NZ, 8, 256), F32), sds((NZ, 8, 256), F32)),
        in_specs=[vmem] * 6 + [smem] + [vmem] * 3 + [smem] * 2,
        out_specs=(vmem, vmem, vmem),
        scratch_shapes=scratch,
        compiler_params=pltpu.CompilerParams(
            vmem_limit_bytes=VMEM_LIMIT, collective_id=0, has_side_effects=True
        ),
        name="step",
    )(spectra, mask, trow, col, weights, map2d, speeds, couple_point, ocean_u, ocean_v, mixing[None, :], profile)
    new_spectra = ret.reshape(KP, 128)[:KC] * mask
    return (new_spectra, new_u, new_v)


def solution(mesh):
    both = ("grp", "dev")
    in_specs = (P(None, both), P(both), P(), P(), P(), P(), P(), P(both, None), P(None, both, None), P(None, both, None), P())
    out_specs = (P(None, both), P(None, both, None), P(None, both, None))
    return jax.shard_map(body, mesh=mesh, in_specs=in_specs, out_specs=out_specs, check_vma=False)
```

```python
import jax
import jax.numpy as jnp
import numpy as np
from jax import lax
from jax.experimental import pallas as pl
from jax.experimental.pallas import tpu as pltpu
from jax.sharding import PartitionSpec as P

ND = 36
NZ = 40
KC = 1296
KP = 1408
FIRST, SECOND = 5, 6
SHARE = FIRST + SECOND
F32, BF16 = jnp.float32, jnp.bfloat16
NT = (((1,), (1,)), ((), ()))
HIGH = lax.Precision.HIGHEST
MESH = pl.DeviceIdType.MESH
VMEM_LIMIT = 56 << 20


def direction_table():
    theta = (np.arange(ND) + 0.5) * (2.0 * np.pi / ND)
    return np.stack([np.cos(theta), np.sin(theta)]).astype(np.float32)


def split(x):
    hi = x.astype(BF16)
    return hi, (x - hi.astype(F32)).astype(BF16)


def spread_matrix():
    wide = lax.broadcasted_iota(jnp.int32, (128, 768), 1)
    target = ((wide & 255) >> 1) + (wide >> 8) - 1
    return jnp.where(lax.broadcasted_iota(jnp.int32, (128, 768), 0) == target, 1.0, 0.0)


def couple_masks(cp, dev):
    row = (cp >> 7) - dev
    col = (cp & 127) - (lax.broadcasted_iota(jnp.int32, (8, 256), 1) >> 1)
    valid = cp >= 0
    return [
        [jnp.where(valid & (row == dr - 1) & (col == delta - 1), 1.0, 0.0) for delta in range(3)]
        for dr in range(3)
    ]


def build_maps(map_ref, base, CT, M, MF):
    def step(s, _):
        row = map_ref[pl.ds(base + s, 1), :]
        n = ((row >> 13) << 7) | (row & 127)
        rl = (row >> 7) & 63
        col = pl.ds(pl.multiple_of(s * 128, 128), 128)
        CT[:, col] = jnp.where(lax.broadcasted_iota(jnp.int32, (256, 128), 0) == n, 1.0, 0.0).astype(BF16)
        mf = jnp.where(lax.broadcasted_iota(jnp.int32, (64, 128), 0) == rl, 1.0, 0.0)
        MF[:, col] = mf
        M[:, col] = mf.astype(BF16)
        return 0

    lax.fori_loop(0, 128, step, 0)


def substep(f, cx, cy, first_lane, last_lane):
    ox = jnp.maximum(cx, 0.0) * f
    ix = jnp.minimum(cx, 0.0) * f
    oy = jnp.maximum(cy, 0.0) * f
    iy = jnp.minimum(cy, 0.0) * f
    rows = f.shape[0]
    nx = jnp.where(last_lane, 0.0, pltpu.roll(ix, 127, 1))
    px = jnp.where(first_lane, 0.0, pltpu.roll(ox, 1, 1))
    ny = pltpu.roll(iy, rows - 1, 0)
    py = pltpu.roll(oy, 1, 0)
    return f - (ox - ix + nx - px) - (oy - iy + ny - py)


S = 8
ROWS = 10
CH = 432


def chunk_offset(i):
    return jnp.where((i & 1) == 1, (i + 1) >> 1, 16 - (i >> 1))


def wait_for(ref, sem):
    pltpu.make_async_copy(ref, ref, sem).wait()


def step_kernel(
    e_ref, mask_ref, table_ref, coef_ref, stokes_ref, trig_ref, map_ref, speed_ref, dirs_ref, cp_ref, u_ref, v_ref,
    mix_ref, prof_ref,
    ret, ret_last, ou_ref, ov_ref,
    E, F1, F2, OH, forced_ref, trow_ref, col_ref, pay1, pay2, arr1, arr2, out1, out2, CT, M, MF, LH, FF1, FF2, acc, dacc, T,
    G, cur, edge, halo, part, pin, ostage, ohalo, B,
    o_send, o_recv, p_send, p_recv, a1_send, a1_recv, a2_send, a2_recv, a3_send,
    h_send, h_recv, r_send, r_recv,
):
    grp = lax.axis_index("grp")
    dev = lax.axis_index("dev")
    q16 = dev >> 3
    owner = (dev & 7) == 0
    linear = grp * 128 + dev
    has_up = linear > 0
    has_down = linear < 255
    up = linear + 255
    up_id = ((up // 128) % 2, up % 128)
    down = linear + 1
    down_id = ((down // 128) % 2, down % 128)

    barrier = pltpu.get_barrier_semaphore()

    def greet(i, _):
        pl.semaphore_signal(barrier, inc=1, device_id=(grp, (dev + i) & 127), device_id_type=MESH)
        return 0

    lax.fori_loop(1, 128, greet, 0)
    pl.semaphore_signal(barrier, inc=1, device_id=(1 - grp, dev), device_id_type=MESH)
    crosses_down = (grp == 0) & (dev == 127)
    crosses_up = (grp == 1) & (dev == 0)

    @pl.when(crosses_down)
    def _():
        pl.semaphore_signal(barrier, inc=1, device_id=down_id, device_id_type=MESH)

    @pl.when(crosses_up)
    def _():
        pl.semaphore_signal(barrier, inc=1, device_id=up_id, device_id_type=MESH)

    masks = couple_masks(cp_ref[...], dev)
    surface = [u_ref[0], v_ref[0]]
    rows = []
    for dr in range(3):
        for q in range(3):
            pieces = []
            for delta in range(3):
                m = masks[dr][delta]
                pieces.append(jnp.sum(m if q == 2 else m * surface[q], axis=0, keepdims=True))
            rows.append(jnp.concatenate(pieces, axis=1))
        rows.append(jnp.zeros((5, 768), F32))
    sums = lax.dot_general(
        jnp.concatenate(rows, axis=0), spread_matrix(), NT, precision=HIGH, preferred_element_type=F32
    )
    for dr in range(3):
        part[dr] = sums[dr * 8 : (dr + 1) * 8]

    def stage_ocean(slot, a, b):
        def level(z, _):
            for side, line in ((0, 0), (1, 7)):
                ostage[slot, side, 0, pl.ds(z, 1), :] = a(z)[line : line + 1]
                ostage[slot, side, 1, pl.ds(z, 1), :] = b(z)[line : line + 1]
            return 0

        lax.fori_loop(0, NZ, level, 0)

    stage_ocean(0, lambda z: u_ref[z], lambda z: v_ref[z])
    build_maps(map_ref, grp * 128, CT, M, MF)

    trow_ref[...] = jnp.full((8, KP), -1, jnp.int32)
    trow_ref[0:4, :KC] = table_ref[...]
    OH_rows = trow_ref[...].astype(F32)
    line8 = lax.broadcasted_iota(jnp.int32, (8, KP), 0)
    wide_coef = jnp.concatenate([coef_ref[...], jnp.zeros((1, KP - KC), F32)], axis=1)
    col_ref[...] = jnp.transpose(jnp.where(line8 < 4, OH_rows, wide_coef))
    tail = jnp.zeros((KP - KC, 256), BF16)
    E[KC:, :] = tail
    F1[KC:, :] = tail
    F2[KC:, :] = tail
    hi, lo = split(e_ref[...])
    E[:KC, :128] = hi
    E[:KC, 128:] = lo

    def gather(i, _):
        rows = pl.ds(pl.multiple_of(i * CH, 16), CH)
        lanes = lax.broadcasted_iota(jnp.int32, (CH, KP), 1).astype(F32)
        e = e_ref[rows, :]
        cols = col_ref[rows, :]
        for m in range(4):
            OH[m * CH : (m + 1) * CH, :] = jnp.where(lanes == cols[:, m : m + 1], 1.0, 0.0).astype(BF16)
        p = jnp.dot(OH[...], E[...], preferred_element_type=F32)
        p = p[:, :128] + p[:, 128:]
        g = [p[m * CH : (m + 1) * CH] for m in range(4)]
        s = cols[:, 4:5]
        ee = e * e
        e2 = 2.0 * e
        a = s * (ee * (g[0] + g[1]) - e2 * g[0] * g[1])
        b = s * (ee * (g[2] + g[3]) - e2 * g[2] * g[3])
        forced_ref[rows, :] = e - (a + b)
        ah, al = split(a)
        bh, bl = split(b)
        F1[rows, :128] = ah
        F1[rows, 128:] = al
        F2[rows, :128] = bh
        F2[rows, 128:] = bl
        return 0

    lax.fori_loop(0, KC // CH, gather, 0)

    mask = mask_ref[...].astype(F32)

    def scatter(first, count):
        rows = slice(first, first + count)
        b = lax.broadcasted_iota(jnp.int32, (count, KP), 0) + first

        def onehot(m):
            return jnp.where(b == trow_ref[m : m + 1, :], 1.0, 0.0)

        p = jnp.dot((onehot(0) + onehot(1)).astype(BF16), F1[...], preferred_element_type=F32)
        p = p + jnp.dot((onehot(2) + onehot(3)).astype(BF16), F2[...], preferred_element_type=F32)
        forced_ref[rows, :] = mask * (forced_ref[rows, :] + 0.5 * (p[:, :128] + p[:, 128:]))

    def destination(n):
        return (((q16 - chunk_offset(n >> 3)) & 15) << 3) | ((dev + n) & 7)

    scatter(0, FIRST * 128)

    scatter(FIRST * 128, KC - FIRST * 128)
    forced_ref[KC:, :] = jnp.zeros((KP - KC, 128), F32)
    weights = trig_ref[...] * jnp.concatenate([stokes_ref[...], jnp.zeros((1, KP - KC), F32)], axis=1)
    drift_own = jnp.dot(weights, forced_ref[...], precision=HIGH, preferred_element_type=F32)

    def ocean_copy(slot, side):
        return pltpu.make_async_remote_copy(
            src_ref=ostage.at[slot, side],
            dst_ref=ohalo.at[slot, 1 - side],
            send_sem=o_send.at[slot, side],
            recv_sem=o_recv.at[slot, 1 - side],
            device_id=up_id if side == 0 else down_id,
            device_id_type=MESH,
        )

    def ocean_start(slot):
        for side, there in ((0, has_up), (1, has_down)):
            @pl.when(there)
            def _(side=side):
                ocean_copy(slot, side).start()

    def ocean_wait(slot):
        for side, there in ((0, has_up), (1, has_down)):
            @pl.when(there)
            def _(side=side):
                wait_for(ostage.at[slot, side], o_send.at[slot, side])
                wait_for(ohalo.at[slot, side], o_recv.at[slot, side])

    def part_copy(side):
        return pltpu.make_async_remote_copy(
            src_ref=part.at[2 * side],
            dst_ref=pin.at[1 - side],
            send_sem=p_send.at[side],
            recv_sem=p_recv.at[1 - side],
            device_id=(grp, (dev + 127 + 2 * side) & 127),
            device_id_type=MESH,
        )

    pl.semaphore_wait(barrier, 128 + jnp.where(crosses_down | crosses_up, 1, 0))

    for side, there in ((0, dev > 0), (1, dev < 127)):
        @pl.when(there)
        def _(side=side):
            part_copy(side).start()

    def fill1(t, _):
        for r in range(4):
            d = t * 4 + r
            for k in range(FIRST):
                pay1[d, k] = forced_ref[pl.ds(k * 128 + d, 1), :]
        return 0

    lax.fori_loop(0, 32, fill1, 0)
    pltpu.make_async_copy(pay1.at[dev], arr1.at[dev], a1_recv.at[q16]).start()

    def send1(n, _):
        dest = destination(n)
        pltpu.make_async_remote_copy(
            src_ref=pay1.at[dest],
            dst_ref=arr1.at[dev],
            send_sem=a1_send,
            recv_sem=a1_recv.at[q16],
            device_id=(grp, dest),
            device_id_type=MESH,
        ).start()
        return 0

    lax.fori_loop(1, 128, send1, 0)
    ocean_start(0)

    for side, there in ((0, dev > 0), (1, dev < 127)):
        @pl.when(there)
        def _(side=side):
            wait_for(part.at[2 * side], p_send.at[side])
            wait_for(pin.at[side], p_recv.at[side])

    total = part[1] + jnp.where(dev > 0, pin[0], 0.0) + jnp.where(dev < 127, pin[1], 0.0)
    speeds = 0.3 * total[0:2] / (total[2:3] + 1.0)

    def fill2(t, _):
        for r in range(8):
            d = t * 8 + r
            for k in range(5):
                pay2[d, k] = forced_ref[pl.ds((FIRST + k) * 128 + d, 1), :]
            for q in range(2):
                pay2[d, 5 + q] = drift_own[q : q + 1]
                pay2[d, 7 + q] = speeds[q : q + 1]
        pay2[t * 8, 9] = forced_ref[pl.ds(1280 + t, 1), :]
        return 0

    lax.fori_loop(0, 16, fill2, 0)

    @pl.when(owner)
    def _():
        pltpu.make_async_copy(pay2.at[dev], arr2.at[dev], a2_recv.at[q16]).start()

    @pl.when(jnp.logical_not(owner))
    def _():
        pltpu.make_async_copy(pay2.at[dev, pl.ds(0, 9)], arr2.at[dev, pl.ds(0, 9)], a2_recv.at[q16]).start()

    def send2(n, _):
        dest = destination(n)

        @pl.when((dest & 7) == 0)
        def _():
            pltpu.make_async_remote_copy(
                src_ref=pay2.at[dest],
                dst_ref=arr2.at[dev],
                send_sem=a3_send,
                recv_sem=a2_recv.at[q16],
                device_id=(grp, dest),
                device_id_type=MESH,
            ).start()

        @pl.when((dest & 7) != 0)
        def _():
            pltpu.make_async_remote_copy(
                src_ref=pay2.at[dest, pl.ds(0, 9)],
                dst_ref=arr2.at[dev, pl.ds(0, 9)],
                send_sem=a2_send,
                recv_sem=a2_recv.at[q16],
                device_id=(grp, dest),
                device_id_type=MESH,
            ).start()

        return 0

    lax.fori_loop(1, 128, send2, 0)

    zero_row = jnp.zeros((1, 128), F32)
    top = grp == 0

    def forward(count, arrived, target, extra):
        R = count * 64
        target[...] = jnp.zeros_like(target)

        def chunk_step(i, _):
            chunk = (q16 + chunk_offset(i)) & 15
            if extra:
                @pl.when(owner)
                def _():
                    wait_for(arr2.at[pl.ds(chunk * S, S)], a2_recv.at[chunk])

                @pl.when(jnp.logical_not(owner))
                def _():
                    wait_for(arr2.at[pl.ds(chunk * S, S), pl.ds(0, 9)], a2_recv.at[chunk])
            else:
                wait_for(arr1.at[pl.ds(chunk * S, S)], a1_recv.at[chunk])
            for j in range(S):
                s = chunk * S + j
                cols = pl.ds(pl.multiple_of(s * 128, 128), 128)
                c = slice(j * 128, (j + 1) * 128)
                for k in range(count):
                    slot = 9 if k == 5 else k
                    x = jnp.broadcast_to(arrived[s, slot], (16, 128))
                    hi, lo = split(x)
                    for q in range(4):
                        m = M[q * 16 : (q + 1) * 16, cols]
                        r = k * 64 + q * 16
                        LH[r : r + 16, c] = m * hi
                        LH[R + r : R + r + 16, c] = m * lo
                if extra:
                    row = map_ref[pl.ds(grp * 128 + s, 1), :] >> 7
                    pieces = []
                    for q in range(2):
                        cur[q, pl.ds(8 + s, 1), :] = arrived[s, 7 + q]
                        x = arrived[s, 5 + q]
                        for dr in range(3):
                            pieces.append(jnp.where(row == dev + (dr - 1), x, zero_row))
                    pieces += [zero_row, zero_row]
                    piece = jnp.concatenate(pieces, axis=0)
                    hi = piece.astype(BF16).astype(F32)
                    LH[2 * R : 2 * R + 16, c] = jnp.concatenate([hi, piece - hi], axis=0).astype(BF16)
            c = CT[:, pl.ds(pl.multiple_of(chunk * (S * 128), 128), S * 128)]
            d = lax.dot_general(LH[: 2 * R + (16 if extra else 0)], c, NT, preferred_element_type=F32)
            target[:R] += d[:R] + d[R : 2 * R]
            if extra:
                dacc[...] += d[2 * R :]
            return 0

        lax.fori_loop(0, 128 // S, chunk_step, 0)

    def boundary(part, first, count):
        for k in range(count):
            low = acc[k * 64 : (k + 1) * 64, 0:128]
            high = acc[k * 64 : (k + 1) * 64, 128:256]
            G[first + k, 8:72, :] = low
            G[first + k, 72:136, :] = high
            edge[part, 0, k : k + 1, :] = jnp.where(top, high[63:64], low[0:1])
            edge[part, 1, k : k + 1, :] = jnp.where(top, high[62:63], low[1:2])
        for r in range(2):
            if part == 0:
                edge[part, r, count:8, :] = jnp.zeros((8 - count, 128), F32)
            else:
                for q in range(2):
                    edge[part, r, 6 + q : 7 + q, :] = jnp.where(
                        top, cur[q, 135 - r : 136 - r, :], cur[q, 8 + r : 9 + r, :]
                    )
        exchange(part).start()

    def exchange(part):
        return pltpu.make_async_remote_copy(
            src_ref=edge.at[part],
            dst_ref=halo.at[part],
            send_sem=h_send.at[part],
            recv_sem=h_recv.at[part],
            device_id=(1 - grp, dev),
            device_id_type=MESH,
        )

    below_on = jnp.where(top, 1.0, 0.0)
    above_on = 1.0 - below_on
    blank = jnp.zeros((6, 128), F32)

    def pad(dst, index, part, k):
        h0 = halo[part, 0, k : k + 1, :]
        h1 = halo[part, 1, k : k + 1, :]
        dst[index, 0:8, :] = jnp.concatenate([blank, h1, h0], axis=0) * above_on
        dst[index, 136:144, :] = jnp.concatenate([h0, h1, blank], axis=0) * below_on

    lane = lax.broadcasted_iota(jnp.int32, (144, 128), 1)
    line = lax.broadcasted_iota(jnp.int32, (144, 128), 0)
    first_lane, last_lane = lane == 0, lane == 127
    keep = jnp.where(line < 8, above_on, jnp.where(line >= 136, below_on, 1.0))

    def propagate(part, first, count, FF):
        for k in range(count):
            pad(G, first + k, part, k)

        def one(k, _):
            comp = jnp.where(first + k == 10, 1280 + q16, (first + k) * 128 + dev)
            way = lax.rem(comp, ND)
            pace = speed_ref[comp]
            cx = cur[0] + pace * dirs_ref[0, way]
            cy = cur[1] + pace * dirs_ref[1, way]
            f = substep(G[first + k], cx, cy, first_lane, last_lane) * keep
            f = substep(f, cx, cy, first_lane, last_lane)
            hi, lo = split(f[8:136])
            r = pl.multiple_of(k * 64, 64)
            for h in range(2):
                FF[pl.ds(r, 64), h * 128 : (h + 1) * 128] = hi[h * 64 : (h + 1) * 64]
                FF[pl.ds(count * 64 + r, 64), h * 128 : (h + 1) * 128] = lo[h * 64 : (h + 1) * 64]
            return 0

        lax.fori_loop(0, count, one, 0)

    def backward(part, first, count, FF, out):
        R = count * 64

        def chunk_step(t, _):
            chunk = (q16 - chunk_offset(15 - t)) & 15
            c = CT[:, pl.ds(pl.multiple_of(chunk * (S * 128), 128), S * 128)]
            T[:R] = jnp.dot(FF[:R], c, preferred_element_type=F32) + jnp.dot(FF[R:], c, preferred_element_type=F32)
            for j in range(S):
                s = chunk * S + j
                m = MF[:, pl.ds(pl.multiple_of(s * 128, 128), 128)]
                for k in range(count):
                    out[s, k] = jnp.sum(T[k * 64 : (k + 1) * 64, j * 128 : (j + 1) * 128] * m, axis=0, keepdims=True)

            def post(j, _):
                s = chunk * S + j

                @pl.when(s != dev)
                def _():
                    pltpu.make_async_remote_copy(
                        src_ref=out.at[s, pl.ds(0, 5)],
                        dst_ref=ret.at[pl.ds(first, 5), dev],
                        send_sem=r_send.at[part],
                        recv_sem=r_recv.at[part],
                        device_id=(grp, s),
                        device_id_type=MESH,
                    ).start()

                if part == 1:
                    @pl.when((s != dev) & owner)
                    def _():
                        pltpu.make_async_remote_copy(
                            src_ref=out.at[s, 5],
                            dst_ref=ret_last.at[q16],
                            send_sem=r_send.at[2],
                            recv_sem=r_recv.at[2],
                            device_id=(grp, s),
                            device_id_type=MESH,
                        ).start()

                return 0

            lax.fori_loop(0, S, post, 0)
            return 0

        lax.fori_loop(0, 128 // S, chunk_step, 0)
        for k in range(5):
            ret[first + k, dev] = out[dev, k]

    dacc[...] = jnp.zeros_like(dacc)
    forward(FIRST, arr1, acc, False)
    boundary(0, 0, FIRST)
    forward(SECOND, arr2, acc, True)
    boundary(1, FIRST, SECOND)
    drift = dacc[0:8] + dacc[8:16]
    wave_row = dev + lax.rem(lax.broadcasted_iota(jnp.int32, (8, 128), 0), 3) - 1
    drift = jnp.where(wave_row >= 64, drift[:, 128:], drift[:, :128])
    wide = jnp.dot(drift, spread_matrix(), precision=HIGH, preferred_element_type=F32)
    masks = couple_masks(cp_ref[...], dev)
    cells = []
    for q in range(2):
        sum_q = jnp.zeros((8, 256), F32)
        for dr in range(3):
            for delta in range(3):
                sum_q = sum_q + masks[dr][delta] * wide[q * 3 + dr : q * 3 + dr + 1, delta * 256 : (delta + 1) * 256]
        cells.append(sum_q)
    us, vs = cells

    oline = lax.broadcasted_iota(jnp.int32, (8, 256), 0)
    olane = lax.broadcasted_iota(jnp.int32, (8, 256), 1)
    coriolis = 0.5 + (linear * 8 + oline).astype(F32) / 2048.0
    fvs, fus = coriolis * vs, coriolis * us

    def ocean_step(slot, source, emit):
        def lap(a, z, q):
            above = jnp.where(has_up, ohalo[slot, 0, q, pl.ds(z, 1), :], 0.0)
            below = jnp.where(has_down, ohalo[slot, 1, q, pl.ds(z, 1), :], 0.0)
            r = jnp.where(olane == 255, 0.0, pltpu.roll(a, 255, 1)) + jnp.where(olane == 0, 0.0, pltpu.roll(a, 1, 1))
            r = r + jnp.where(oline == 0, above, pltpu.roll(a, 1, 0)) + jnp.where(oline == 7, below, pltpu.roll(a, 7, 0))
            return r - 4.0 * a

        def level(z, carry):
            pu, pv = carry
            u, v = source(0, z), source(1, z)
            zn = jnp.minimum(z + 1, NZ - 1)
            m0 = mix_ref[z]
            m1 = jnp.where(z == NZ - 1, 0.0, mix_ref[zn])
            nu, nv = source(0, zn), source(1, zn)
            p = prof_ref[z]
            wu = m1 * (nu - u) - m0 * (u - pu)
            wv = m1 * (nv - v) - m0 * (v - pv)
            emit(
                z,
                u + 0.2 * (0.2 * lap(u, z, 0) + wu + coriolis * v + p * fvs),
                v + 0.2 * (0.2 * lap(v, z, 1) + wv - coriolis * u - p * fus),
            )
            return u, v

        zero = jnp.zeros((8, 256), F32)
        lax.fori_loop(0, NZ, level, (zero, zero))

    def emit1(z, u, v):
        B[0, z] = u
        B[1, z] = v

    def emit2(z, u, v):
        ou_ref[z] = u
        ov_ref[z] = v

    ocean_wait(0)
    ocean_step(0, lambda q, z: (u_ref, v_ref)[q][z], emit1)
    stage_ocean(1, lambda z: B[0, z], lambda z: B[1, z])
    ocean_start(1)

    exchange(0).wait()
    exchange(1).wait()
    for q in range(2):
        pad(cur, q, 1, 6 + q)
    propagate(0, 0, FIRST, FF1)
    backward(0, 0, FIRST, FF1, out1)
    propagate(1, FIRST, SECOND, FF2)
    backward(1, FIRST, SECOND, FF2, out2)

    @pl.when(owner)
    def _():
        ret_last[q16] = out2[dev, 5]

    ocean_wait(1)
    ocean_step(1, lambda q, z: B[q, z], emit2)

    wait_for(pay1.at[pl.ds(0, 127)], a1_send)

    @pl.when(owner)
    def _():
        wait_for(pay2.at[pl.ds(0, 112), pl.ds(0, 9)], a2_send)
        wait_for(pay2.at[pl.ds(0, 15)], a3_send)
        wait_for(out2.at[pl.ds(0, 127), 5], r_send.at[2])
        wait_for(ret_last.at[pl.ds(0, 15)], r_recv.at[2])

    @pl.when(jnp.logical_not(owner))
    def _():
        wait_for(pay2.at[pl.ds(0, 111), pl.ds(0, 9)], a2_send)
        wait_for(pay2.at[pl.ds(0, 16)], a3_send)
        wait_for(ret_last.at[pl.ds(0, 16)], r_recv.at[2])

    wait_for(out1.at[pl.ds(0, 127)], r_send.at[0])
    wait_for(out2.at[pl.ds(0, 127), pl.ds(0, 5)], r_send.at[1])
    wait_for(ret.at[pl.ds(0, 5), pl.ds(0, 127)], r_recv.at[0])
    wait_for(ret.at[pl.ds(0, 5), pl.ds(0, 127)], r_recv.at[1])


def body(spectra, sea_mask, card_map, dia_table, dia_coef, speed, stokes_weight, couple_point, ocean_u, ocean_v, mixing):
    sds = jax.ShapeDtypeStruct
    dirs = direction_table()
    trig = np.zeros((8, KP), np.float32)
    trig[:2, :KC] = np.tile(dirs, (1, KC // ND))
    profile = np.exp(-3.0 * (np.arange(NZ) + 0.5) / NZ).astype(np.float32)
    vmem = pl.BlockSpec(memory_space=pltpu.VMEM)
    smem = pl.BlockSpec(memory_space=pltpu.SMEM)
    dma = pltpu.SemaphoreType.DMA
    scratch = [
        pltpu.VMEM((KP, 256), BF16),
        pltpu.VMEM((KP, 256), BF16),
        pltpu.VMEM((KP, 256), BF16),
        pltpu.VMEM((4 * CH, KP), BF16),
        pltpu.VMEM((KP, 128), F32),
        pltpu.VMEM((8, KP), jnp.int32),
        pltpu.VMEM((KP, 8), F32),
        pltpu.VMEM((128, FIRST, 1, 128), F32),
        pltpu.VMEM((128, ROWS, 1, 128), F32),
        pltpu.VMEM((128, FIRST, 1, 128), F32),
        pltpu.VMEM((128, ROWS, 1, 128), F32),
        pltpu.VMEM((128, FIRST, 1, 128), F32),
        pltpu.VMEM((128, SECOND, 1, 128), F32),
        pltpu.VMEM((256, 16384), BF16),
        pltpu.VMEM((64, 16384), BF16),
        pltpu.VMEM((64, 16384), F32),
        pltpu.VMEM((128 * SECOND + 16, S * 128), BF16),
        pltpu.VMEM((128 * FIRST, 256), BF16),
        pltpu.VMEM((128 * SECOND, 256), BF16),
        pltpu.VMEM((64 * SECOND, 256), F32),
        pltpu.VMEM((16, 256), F32),
        pltpu.VMEM((64 * SECOND, S * 128), F32),
        pltpu.VMEM((SHARE, 144, 128), F32),
        pltpu.VMEM((2, 144, 128), F32),
        pltpu.VMEM((2, 2, 8, 128), F32),
        pltpu.VMEM((2, 2, 8, 128), F32),
        pltpu.VMEM((3, 8, 128), F32),
        pltpu.VMEM((2, 8, 128), F32),
        pltpu.VMEM((2, 2, 2, NZ, 256), F32),
        pltpu.VMEM((2, 2, 2, NZ, 256), F32),
        pltpu.VMEM((2, NZ, 8, 256), F32),
        dma((2, 2)), dma((2, 2)), dma((2,)), dma((2,)),
        dma, dma((16,)), dma, dma((16,)), dma, dma((2,)), dma((2,)), dma((3,)), dma((3,)),
    ]
    ret, ret_last, new_u, new_v = pl.pallas_call(
        step_kernel,
        out_shape=(
            sds((10, 128, 1, 128), F32), sds((16, 1, 128), F32), sds((NZ, 8, 256), F32), sds((NZ, 8, 256), F32)
        ),
        in_specs=[vmem] * 7 + [smem] * 2 + [vmem] * 3 + [smem] * 2,
        out_specs=(vmem,) * 4,
        scratch_shapes=scratch,
        compiler_params=pltpu.CompilerParams(
            vmem_limit_bytes=VMEM_LIMIT, collective_id=0, has_side_effects=True
        ),
        name="step",
    )(
        spectra, sea_mask.reshape(1, 128), dia_table, dia_coef.reshape(1, KC), stokes_weight.reshape(1, KC),
        jnp.asarray(trig), card_map.reshape(256, 128), speed, jnp.asarray(dirs), couple_point, ocean_u, ocean_v,
        mixing, jnp.asarray(profile),
    )
    new_spectra = jnp.concatenate([ret.reshape(1280, 128), ret_last.reshape(16, 128)]) * sea_mask.astype(F32)
    return (new_spectra, new_u, new_v)


def solution(mesh):
    both = ("grp", "dev")
    in_specs = (P(None, both), P(both), P(), P(), P(), P(), P(), P(both, None), P(None, both, None), P(None, both, None), P())
    out_specs = (P(None, both), P(None, both, None), P(None, both, None))
    return jax.shard_map(body, mesh=mesh, in_specs=in_specs, out_specs=out_specs, check_vma=False)
```

```python
import jax
import jax.numpy as jnp
import numpy as np
from jax import lax
from jax.experimental import pallas as pl
from jax.experimental.pallas import tpu as pltpu
from jax.sharding import PartitionSpec as P

ND = 36
NZ = 40
KC = 1296
KP = 1408
SHARE = 11
F32, BF16 = jnp.float32, jnp.bfloat16
NT = (((1,), (1,)), ((), ()))
HIGH = lax.Precision.HIGHEST
MESH = pl.DeviceIdType.MESH
VMEM_LIMIT = 56 << 20


def direction_table():
    theta = (np.arange(ND) + 0.5) * (2.0 * np.pi / ND)
    return np.stack([np.cos(theta), np.sin(theta)]).astype(np.float32)


def split(x):
    hi = x.astype(BF16)
    return hi, (x - hi.astype(F32)).astype(BF16)


def spread_matrix():
    wide = lax.broadcasted_iota(jnp.int32, (128, 768), 1)
    target = ((wide & 255) >> 1) + (wide >> 8) - 1
    return jnp.where(lax.broadcasted_iota(jnp.int32, (128, 768), 0) == target, 1.0, 0.0)


def couple_masks(cp, dev):
    row = (cp >> 7) - dev
    col = (cp & 127) - (lax.broadcasted_iota(jnp.int32, (8, 256), 1) >> 1)
    valid = cp >= 0
    return [
        [jnp.where(valid & (row == dr - 1) & (col == delta - 1), 1.0, 0.0) for delta in range(3)]
        for dr in range(3)
    ]


def build_maps(map_ref, base, CT, M, MF):
    def step(s, _):
        row = map_ref[pl.ds(base + s, 1), :]
        n = ((row >> 13) << 7) | (row & 127)
        rl = (row >> 7) & 63
        col = pl.ds(pl.multiple_of(s * 128, 128), 128)
        CT[:, col] = jnp.where(lax.broadcasted_iota(jnp.int32, (256, 128), 0) == n, 1.0, 0.0).astype(BF16)
        mf = jnp.where(lax.broadcasted_iota(jnp.int32, (64, 128), 0) == rl, 1.0, 0.0)
        MF[:, col] = mf
        M[:, col] = mf.astype(BF16)
        return 0

    lax.fori_loop(0, 128, step, 0)


def substep(f, cx, cy, first_lane, last_lane):
    ox = jnp.maximum(cx, 0.0) * f
    ix = jnp.minimum(cx, 0.0) * f
    oy = jnp.maximum(cy, 0.0) * f
    iy = jnp.minimum(cy, 0.0) * f
    rows = f.shape[0]
    nx = jnp.where(last_lane, 0.0, pltpu.roll(ix, 127, 1))
    px = jnp.where(first_lane, 0.0, pltpu.roll(ox, 1, 1))
    ny = pltpu.roll(iy, rows - 1, 0)
    py = pltpu.roll(oy, 1, 0)
    return f - (ox - ix + nx - px) - (oy - iy + ny - py)


S = 8
ROWS = 15
R = SHARE * 64
ONEHOT = 8
RB = ONEHOT * 64
CH = 432


def chunk_offset(i):
    return jnp.where((i & 1) == 1, (i + 1) >> 1, 16 - (i >> 1))


def start_of(dev):
    return dev * 10 + ((dev + 7) >> 3)


def wait_for(ref, sem):
    pltpu.make_async_copy(ref, ref, sem).wait()


def step_kernel(
    e_ref, mask_ref, table_ref, coef_ref, stokes_ref, trig_ref, map_ref, speed_ref, dirs_ref, cp_ref, u_ref, v_ref,
    mix_ref, prof_ref,
    ret, ou_ref, ov_ref,
    E, F1, F2, OH, forced_ref, trow_ref, col_ref, pay, arr, out, CT, M, MF, LH, FF, acc, dacc, T,
    G, cur, edge, halo, part, pin, ostage, ohalo, B,
    o_send, o_recv, p_send, p_recv, a_send, a_recv, b_send,
    h_send, h_recv, r_send, r_recv,
):
    grp = lax.axis_index("grp")
    dev = lax.axis_index("dev")
    q16 = dev >> 3
    owner = (dev & 7) == 0
    first = start_of(dev)
    linear = grp * 128 + dev
    has_up = linear > 0
    has_down = linear < 255
    up = linear + 255
    up_id = ((up // 128) % 2, up % 128)
    down = linear + 1
    down_id = ((down // 128) % 2, down % 128)

    barrier = pltpu.get_barrier_semaphore()

    def greet(i, _):
        pl.semaphore_signal(barrier, inc=1, device_id=(grp, (dev + i) & 127), device_id_type=MESH)
        return 0

    lax.fori_loop(1, 128, greet, 0)
    pl.semaphore_signal(barrier, inc=1, device_id=(1 - grp, dev), device_id_type=MESH)
    crosses_down = (grp == 0) & (dev == 127)
    crosses_up = (grp == 1) & (dev == 0)

    @pl.when(crosses_down)
    def _():
        pl.semaphore_signal(barrier, inc=1, device_id=down_id, device_id_type=MESH)

    @pl.when(crosses_up)
    def _():
        pl.semaphore_signal(barrier, inc=1, device_id=up_id, device_id_type=MESH)

    masks = couple_masks(cp_ref[...], dev)
    surface = [u_ref[0], v_ref[0]]
    rows = []
    for dr in range(3):
        for q in range(3):
            pieces = []
            for delta in range(3):
                m = masks[dr][delta]
                pieces.append(jnp.sum(m if q == 2 else m * surface[q], axis=0, keepdims=True))
            rows.append(jnp.concatenate(pieces, axis=1))
        rows.append(jnp.zeros((5, 768), F32))
    sums = lax.dot_general(
        jnp.concatenate(rows, axis=0), spread_matrix(), NT, precision=HIGH, preferred_element_type=F32
    )
    for dr in range(3):
        part[dr] = sums[dr * 8 : (dr + 1) * 8]

    def stage_ocean(slot, a, b):
        def level(z, _):
            for side, line in ((0, 0), (1, 7)):
                ostage[slot, side, 0, pl.ds(z, 1), :] = a(z)[line : line + 1]
                ostage[slot, side, 1, pl.ds(z, 1), :] = b(z)[line : line + 1]
            return 0

        lax.fori_loop(0, NZ, level, 0, unroll=8)

    stage_ocean(0, lambda z: u_ref[z], lambda z: v_ref[z])
    build_maps(map_ref, grp * 128, CT, M, MF)

    trow_ref[...] = jnp.full((8, KP), -1, jnp.int32)
    trow_ref[0:4, :KC] = table_ref[...]
    OH_rows = trow_ref[...].astype(F32)
    line8 = lax.broadcasted_iota(jnp.int32, (8, KP), 0)
    wide_coef = jnp.concatenate([coef_ref[...].reshape(1, KC), jnp.zeros((1, KP - KC), F32)], axis=1)
    col_ref[...] = jnp.transpose(jnp.where(line8 < 4, OH_rows, wide_coef))
    tail = jnp.zeros((KP - KC, 256), BF16)
    E[KC:, :] = tail
    F1[KC:, :] = tail
    F2[KC:, :] = tail
    hi, lo = split(e_ref[...])
    E[:KC, :128] = hi
    E[:KC, 128:] = lo

    def gather(i, _):
        rows = pl.ds(pl.multiple_of(i * CH, 16), CH)
        lanes = lax.broadcasted_iota(jnp.int32, (CH, KP), 1).astype(F32)
        e = e_ref[rows, :]
        cols = col_ref[rows, :]
        for m in range(4):
            OH[m * CH : (m + 1) * CH, :] = jnp.where(lanes == cols[:, m : m + 1], 1.0, 0.0).astype(BF16)
        p = jnp.dot(OH[...], E[...], preferred_element_type=F32)
        p = p[:, :128] + p[:, 128:]
        g = [p[m * CH : (m + 1) * CH] for m in range(4)]
        s = cols[:, 4:5]
        ee = e * e
        e2 = 2.0 * e
        a = s * (ee * (g[0] + g[1]) - e2 * g[0] * g[1])
        b = s * (ee * (g[2] + g[3]) - e2 * g[2] * g[3])
        forced_ref[rows, :] = e - (a + b)
        ah, al = split(a)
        bh, bl = split(b)
        F1[rows, :128] = ah
        F1[rows, 128:] = al
        F2[rows, :128] = bh
        F2[rows, 128:] = bl
        return 0

    lax.fori_loop(0, KC // CH, gather, 0)

    mask = mask_ref[...].astype(F32)

    def scatter(i, _):
        rows = pl.ds(pl.multiple_of(i * CH, 16), CH)
        b = lax.broadcasted_iota(jnp.int32, (CH, KP), 0) + i * CH

        def onehot(m):
            return jnp.where(b == trow_ref[m : m + 1, :], 1.0, 0.0)

        p = jnp.dot((onehot(0) + onehot(1)).astype(BF16), F1[...], preferred_element_type=F32)
        p = p + jnp.dot((onehot(2) + onehot(3)).astype(BF16), F2[...], preferred_element_type=F32)
        forced_ref[rows, :] = mask * (forced_ref[rows, :] + 0.5 * (p[:, :128] + p[:, 128:]))
        return 0

    lax.fori_loop(0, KC // CH, scatter, 0)

    def destination(n):
        return (((q16 - chunk_offset(n >> 3)) & 15) << 3) | ((dev + n) & 7)

    forced_ref[KC:, :] = jnp.zeros((KP - KC, 128), F32)
    weights = trig_ref[...] * jnp.concatenate([stokes_ref[...].reshape(1, KC), jnp.zeros((1, KP - KC), F32)], axis=1)
    drift_own = jnp.dot(weights, forced_ref[...], precision=HIGH, preferred_element_type=F32)

    def ocean_copy(slot, side):
        return pltpu.make_async_remote_copy(
            src_ref=ostage.at[slot, side],
            dst_ref=ohalo.at[slot, 1 - side],
            send_sem=o_send.at[slot, side],
            recv_sem=o_recv.at[slot, 1 - side],
            device_id=up_id if side == 0 else down_id,
            device_id_type=MESH,
        )

    def ocean_start(slot):
        for side, there in ((0, has_up), (1, has_down)):
            @pl.when(there)
            def _(side=side):
                ocean_copy(slot, side).start()

    def ocean_wait(slot):
        for side, there in ((0, has_up), (1, has_down)):
            @pl.when(there)
            def _(side=side):
                wait_for(ostage.at[slot, side], o_send.at[slot, side])
                wait_for(ohalo.at[slot, side], o_recv.at[slot, side])

    def part_copy(side):
        return pltpu.make_async_remote_copy(
            src_ref=part.at[2 * side],
            dst_ref=pin.at[1 - side],
            send_sem=p_send.at[side],
            recv_sem=p_recv.at[1 - side],
            device_id=(grp, (dev + 127 + 2 * side) & 127),
            device_id_type=MESH,
        )

    def fill(t, _):
        for r in range(4):
            d = t * 4 + r
            base = start_of(d)
            for k in range(10):
                pay[d, k] = forced_ref[pl.ds(base + k, 1), :]
            for q in range(2):
                pay[d, 10 + q] = drift_own[q : q + 1]
            pay[d, 14] = forced_ref[pl.ds(base + 10, 1), :]
        return 0

    lax.fori_loop(0, 32, fill, 0)

    pl.semaphore_wait(barrier, 128 + jnp.where(crosses_down | crosses_up, 1, 0))

    for side, there in ((0, dev > 0), (1, dev < 127)):
        @pl.when(there)
        def _(side=side):
            part_copy(side).start()

    for side, there in ((0, dev > 0), (1, dev < 127)):
        @pl.when(there)
        def _(side=side):
            wait_for(part.at[2 * side], p_send.at[side])
            wait_for(pin.at[side], p_recv.at[side])

    total = part[1] + jnp.where(dev > 0, pin[0], 0.0) + jnp.where(dev < 127, pin[1], 0.0)
    speeds = 0.3 * total[0:2] / (total[2:3] + 1.0)

    def fill_currents(t, _):
        for r in range(8):
            for q in range(2):
                pay[t * 8 + r, 12 + q] = speeds[q : q + 1]
        return 0

    lax.fori_loop(0, 16, fill_currents, 0)

    @pl.when(owner)
    def _():
        pltpu.make_async_copy(pay.at[dev], arr.at[dev], a_recv.at[q16]).start()

    @pl.when(jnp.logical_not(owner))
    def _():
        pltpu.make_async_copy(pay.at[dev, pl.ds(0, 14)], arr.at[dev, pl.ds(0, 14)], a_recv.at[q16]).start()

    def send(n, _):
        dest = destination(n)

        @pl.when((dest & 7) == 0)
        def _():
            pltpu.make_async_remote_copy(
                src_ref=pay.at[dest],
                dst_ref=arr.at[dev],
                send_sem=b_send,
                recv_sem=a_recv.at[q16],
                device_id=(grp, dest),
                device_id_type=MESH,
            ).start()

        @pl.when((dest & 7) != 0)
        def _():
            pltpu.make_async_remote_copy(
                src_ref=pay.at[dest, pl.ds(0, 14)],
                dst_ref=arr.at[dev, pl.ds(0, 14)],
                send_sem=a_send,
                recv_sem=a_recv.at[q16],
                device_id=(grp, dest),
                device_id_type=MESH,
            ).start()

        return 0

    lax.fori_loop(1, 128, send, 0)
    ocean_start(0)

    zero_row = jnp.zeros((1, 128), F32)
    top = grp == 0

    acc[...] = jnp.zeros_like(acc)
    dacc[...] = jnp.zeros_like(dacc)

    def forward(i, _):
        chunk = (q16 + chunk_offset(i)) & 15

        @pl.when(owner)
        def _():
            wait_for(arr.at[pl.ds(chunk * S, S)], a_recv.at[chunk])

        @pl.when(jnp.logical_not(owner))
        def _():
            wait_for(arr.at[pl.ds(chunk * S, S), pl.ds(0, 14)], a_recv.at[chunk])

        for j in range(S):
            s = chunk * S + j
            cols = pl.ds(pl.multiple_of(s * 128, 128), 128)
            c = slice(j * 128, (j + 1) * 128)
            for k in range(SHARE):
                x = jnp.broadcast_to(arr[s, 14 if k == 10 else k], (16, 128))
                hi, lo = split(x)
                for q in range(4):
                    m = M[q * 16 : (q + 1) * 16, cols]
                    r = k * 64 + q * 16
                    LH[r : r + 16, c] = m * hi
                    LH[R + r : R + r + 16, c] = m * lo
            row = map_ref[pl.ds(grp * 128 + s, 1), :] >> 7
            pieces = []
            for q in range(2):
                cur[q, pl.ds(8 + s, 1), :] = arr[s, 12 + q]
                x = arr[s, 10 + q]
                for dr in range(3):
                    pieces.append(jnp.where(row == dev + (dr - 1), x, zero_row))
            pieces += [zero_row, zero_row]
            piece = jnp.concatenate(pieces, axis=0)
            hi = piece.astype(BF16).astype(F32)
            LH[2 * R : 2 * R + 16, c] = jnp.concatenate([hi, piece - hi], axis=0).astype(BF16)
        c = CT[:, pl.ds(pl.multiple_of(chunk * (S * 128), 128), S * 128)]
        d = lax.dot_general(LH[...], c, NT, preferred_element_type=F32)
        acc[...] += d[:R] + d[R : 2 * R]
        dacc[...] += d[2 * R :]
        return 0

    lax.fori_loop(0, 128 // S, forward, 0)

    for k in range(SHARE):
        low = acc[k * 64 : (k + 1) * 64, 0:128]
        high = acc[k * 64 : (k + 1) * 64, 128:256]
        G[k, 8:72, :] = low
        G[k, 72:136, :] = high
        edge[0, k : k + 1, :] = jnp.where(top, high[63:64], low[0:1])
        edge[1, k : k + 1, :] = jnp.where(top, high[62:63], low[1:2])
    for r in range(2):
        for q in range(2):
            edge[r, SHARE + q : SHARE + q + 1, :] = jnp.where(
                top, cur[q, 135 - r : 136 - r, :], cur[q, 8 + r : 9 + r, :]
            )
        edge[r, 13:16, :] = jnp.zeros((3, 128), F32)
    exchange = pltpu.make_async_remote_copy(
        src_ref=edge, dst_ref=halo, send_sem=h_send, recv_sem=h_recv, device_id=(1 - grp, dev), device_id_type=MESH
    )
    exchange.start()

    below_on = jnp.where(top, 1.0, 0.0)
    above_on = 1.0 - below_on
    blank = jnp.zeros((6, 128), F32)

    def pad(dst, index, k):
        h0 = halo[0, k : k + 1, :]
        h1 = halo[1, k : k + 1, :]
        dst[index, 0:8, :] = jnp.concatenate([blank, h1, h0], axis=0) * above_on
        dst[index, 136:144, :] = jnp.concatenate([h0, h1, blank], axis=0) * below_on

    lane = lax.broadcasted_iota(jnp.int32, (144, 128), 1)
    line = lax.broadcasted_iota(jnp.int32, (144, 128), 0)
    first_lane, last_lane = lane == 0, lane == 127
    keep = jnp.where(line < 8, above_on, jnp.where(line >= 136, below_on, 1.0))

    def propagate(k, _):
        comp = jnp.minimum(first + k, KC - 1)
        way = lax.rem(comp, ND)
        pace = speed_ref[comp]
        cx = cur[0] + pace * dirs_ref[0, way]
        cy = cur[1] + pace * dirs_ref[1, way]
        f = substep(G[k], cx, cy, first_lane, last_lane) * keep
        f = substep(f, cx, cy, first_lane, last_lane)
        G[k] = f
        return 0

    def backward(t, _):
        chunk = (q16 - chunk_offset(15 - t)) & 15
        c = CT[:, pl.ds(pl.multiple_of(chunk * (S * 128), 128), S * 128)]
        T[...] = jnp.dot(FF[:RB], c, preferred_element_type=F32) + jnp.dot(FF[RB:], c, preferred_element_type=F32)
        where = map_ref[pl.ds(pl.multiple_of(grp * 128 + chunk * S, 8), S), :]
        row, col = where >> 7, where & 127
        taken = [jnp.zeros((S, 128), F32) for _ in range(SHARE - ONEHOT)]
        for r in range(128):
            hit = row == r
            for k in range(SHARE - ONEHOT):
                x = jnp.broadcast_to(G[ONEHOT + k, 8 + r : 9 + r, :], (S, 128))
                y = jnp.take_along_axis(x, col, axis=1, mode="promise_in_bounds")
                taken[k] = jnp.where(hit, y, taken[k])
        for j in range(S):
            s = chunk * S + j
            for k in range(SHARE - ONEHOT):
                out[s, ONEHOT + k] = taken[k][j : j + 1]
            m = MF[:, pl.ds(pl.multiple_of(s * 128, 128), 128)]
            for k in range(ONEHOT):
                out[s, k] = jnp.sum(T[k * 64 : (k + 1) * 64, j * 128 : (j + 1) * 128] * m, axis=0, keepdims=True)

        def post(j, _):
            s = chunk * S + j

            @pl.when((s != dev) & owner)
            def _():
                pltpu.make_async_remote_copy(
                    src_ref=out.at[s],
                    dst_ref=ret.at[pl.ds(first, 11)],
                    send_sem=r_send,
                    recv_sem=r_recv,
                    device_id=(grp, s),
                    device_id_type=MESH,
                ).start()

            @pl.when((s != dev) & jnp.logical_not(owner))
            def _():
                pltpu.make_async_remote_copy(
                    src_ref=out.at[s, pl.ds(0, 10)],
                    dst_ref=ret.at[pl.ds(first, 10)],
                    send_sem=r_send,
                    recv_sem=r_recv,
                    device_id=(grp, s),
                    device_id_type=MESH,
                ).start()

            return 0

        lax.fori_loop(0, S, post, 0)
        return 0

    drift = dacc[0:8] + dacc[8:16]
    wave_row = dev + lax.rem(lax.broadcasted_iota(jnp.int32, (8, 128), 0), 3) - 1
    drift = jnp.where(wave_row >= 64, drift[:, 128:], drift[:, :128])
    wide = jnp.dot(drift, spread_matrix(), precision=HIGH, preferred_element_type=F32)
    masks = couple_masks(cp_ref[...], dev)
    cells = []
    for q in range(2):
        sum_q = jnp.zeros((8, 256), F32)
        for dr in range(3):
            for delta in range(3):
                sum_q = sum_q + masks[dr][delta] * wide[q * 3 + dr : q * 3 + dr + 1, delta * 256 : (delta + 1) * 256]
        cells.append(sum_q)
    us, vs = cells

    oline = lax.broadcasted_iota(jnp.int32, (8, 256), 0)
    olane = lax.broadcasted_iota(jnp.int32, (8, 256), 1)
    coriolis = 0.5 + (linear * 8 + oline).astype(F32) / 2048.0
    fvs, fus = coriolis * vs, coriolis * us

    def ocean_step(slot, source, emit):
        def lap(a, z, q):
            above = jnp.where(has_up, ohalo[slot, 0, q, pl.ds(z, 1), :], 0.0)
            below = jnp.where(has_down, ohalo[slot, 1, q, pl.ds(z, 1), :], 0.0)
            r = jnp.where(olane == 255, 0.0, pltpu.roll(a, 255, 1)) + jnp.where(olane == 0, 0.0, pltpu.roll(a, 1, 1))
            r = r + jnp.where(oline == 0, above, pltpu.roll(a, 1, 0)) + jnp.where(oline == 7, below, pltpu.roll(a, 7, 0))
            return r - 4.0 * a

        def level(z, carry):
            pu, pv = carry
            u, v = source(0, z), source(1, z)
            zn = jnp.minimum(z + 1, NZ - 1)
            m0 = mix_ref[z]
            m1 = jnp.where(z == NZ - 1, 0.0, mix_ref[zn])
            nu, nv = source(0, zn), source(1, zn)
            p = prof_ref[z]
            wu = m1 * (nu - u) - m0 * (u - pu)
            wv = m1 * (nv - v) - m0 * (v - pv)
            emit(
                z,
                u + 0.2 * (0.2 * lap(u, z, 0) + wu + coriolis * v + p * fvs),
                v + 0.2 * (0.2 * lap(v, z, 1) + wv - coriolis * u - p * fus),
            )
            return u, v

        zero = jnp.zeros((8, 256), F32)
        lax.fori_loop(0, NZ, level, (zero, zero), unroll=8)

    def emit1(z, u, v):
        B[0, z] = u
        B[1, z] = v

    def emit2(z, u, v):
        ou_ref[z] = u
        ov_ref[z] = v

    ocean_wait(0)
    ocean_step(0, lambda q, z: (u_ref, v_ref)[q][z], emit1)
    stage_ocean(1, lambda z: B[0, z], lambda z: B[1, z])
    ocean_start(1)

    exchange.wait()
    for k in range(SHARE):
        pad(G, k, k)
    for q in range(2):
        pad(cur, q, SHARE + q)
    lax.fori_loop(0, SHARE, propagate, 0)
    for k in range(ONEHOT):
        for h in range(2):
            hi, lo = split(G[k, 8 + h * 64 : 72 + h * 64, :])
            FF[k * 64 : (k + 1) * 64, h * 128 : (h + 1) * 128] = hi
            FF[RB + k * 64 : RB + (k + 1) * 64, h * 128 : (h + 1) * 128] = lo
    lax.fori_loop(0, 128 // S, backward, 0)
    for k in range(10):
        ret[first + k] = out[dev, k]

    @pl.when(owner)
    def _():
        ret[first + 10] = out[dev, 10]

    ocean_wait(1)
    ocean_step(1, lambda q, z: B[q, z], emit2)

    @pl.when(owner)
    def _():
        wait_for(pay.at[pl.ds(0, 112), pl.ds(0, 14)], a_send)
        wait_for(pay.at[pl.ds(0, 15)], b_send)
        wait_for(out.at[pl.ds(0, 127)], r_send)
        wait_for(ret.at[pl.ds(0, KC - 11)], r_recv)

    @pl.when(jnp.logical_not(owner))
    def _():
        wait_for(pay.at[pl.ds(0, 111), pl.ds(0, 14)], a_send)
        wait_for(pay.at[pl.ds(0, 16)], b_send)
        wait_for(out.at[pl.ds(0, 127), pl.ds(0, 10)], r_send)
        wait_for(ret.at[pl.ds(0, KC - 10)], r_recv)


def body(spectra, sea_mask, card_map, dia_table, dia_coef, speed, stokes_weight, couple_point, ocean_u, ocean_v, mixing):
    sds = jax.ShapeDtypeStruct
    dirs = direction_table()
    trig = np.zeros((8, KP), np.float32)
    trig[:2, :KC] = np.tile(dirs, (1, KC // ND))
    profile = np.exp(-3.0 * (np.arange(NZ) + 0.5) / NZ).astype(np.float32)
    vmem = pl.BlockSpec(memory_space=pltpu.VMEM)
    smem = pl.BlockSpec(memory_space=pltpu.SMEM)
    dma = pltpu.SemaphoreType.DMA
    scratch = [
        pltpu.VMEM((KP, 256), BF16),
        pltpu.VMEM((KP, 256), BF16),
        pltpu.VMEM((KP, 256), BF16),
        pltpu.VMEM((4 * CH, KP), BF16),
        pltpu.VMEM((KP, 128), F32),
        pltpu.VMEM((8, KP), jnp.int32),
        pltpu.VMEM((KP, 8), F32),
        pltpu.VMEM((128, ROWS, 1, 128), F32),
        pltpu.VMEM((128, ROWS, 1, 128), F32),
        pltpu.VMEM((128, SHARE, 1, 128), F32),
        pltpu.VMEM((256, 16384), BF16),
        pltpu.VMEM((64, 16384), BF16),
        pltpu.VMEM((64, 16384), F32),
        pltpu.VMEM((2 * R + 16, S * 128), BF16),
        pltpu.VMEM((2 * RB, 256), BF16),
        pltpu.VMEM((R, 256), F32),
        pltpu.VMEM((16, 256), F32),
        pltpu.VMEM((RB, S * 128), F32),
        pltpu.VMEM((SHARE, 144, 128), F32),
        pltpu.VMEM((2, 144, 128), F32),
        pltpu.VMEM((2, 16, 128), F32),
        pltpu.VMEM((2, 16, 128), F32),
        pltpu.VMEM((3, 8, 128), F32),
        pltpu.VMEM((2, 8, 128), F32),
        pltpu.VMEM((2, 2, 2, NZ, 256), F32),
        pltpu.VMEM((2, 2, 2, NZ, 256), F32),
        pltpu.VMEM((2, NZ, 8, 256), F32),
        dma((2, 2)), dma((2, 2)), dma((2,)), dma((2,)), dma, dma((16,)), dma, dma, dma, dma, dma,
    ]
    ret, new_u, new_v = pl.pallas_call(
        step_kernel,
        out_shape=(sds((KC, 1, 128), F32), sds((NZ, 8, 256), F32), sds((NZ, 8, 256), F32)),
        in_specs=[vmem] * 7 + [smem] * 2 + [vmem] * 3 + [smem] * 2,
        out_specs=(vmem,) * 3,
        scratch_shapes=scratch,
        compiler_params=pltpu.CompilerParams(
            vmem_limit_bytes=VMEM_LIMIT, collective_id=0, has_side_effects=True
        ),
        name="step",
    )(
        spectra, sea_mask.reshape(1, 128), dia_table, dia_coef, stokes_weight,
        jnp.asarray(trig), card_map.reshape(256, 128), speed, jnp.asarray(dirs), couple_point, ocean_u, ocean_v,
        mixing, jnp.asarray(profile),
    )
    new_spectra = ret.reshape(KC, 128) * sea_mask.astype(F32)
    return (new_spectra, new_u, new_v)


def solution(mesh):
    both = ("grp", "dev")
    in_specs = (P(None, both), P(both), P(), P(), P(), P(), P(), P(both, None), P(None, both, None), P(None, both, None), P())
    out_specs = (P(None, both), P(None, both, None), P(None, both, None))
    return jax.shard_map(body, mesh=mesh, in_specs=in_specs, out_specs=out_specs, check_vma=False)
```

```python
import jax
import jax.numpy as jnp
import numpy as np
from jax import lax
from jax.experimental import pallas as pl
from jax.experimental.pallas import tpu as pltpu
from jax.sharding import PartitionSpec as P

ND = 36
NZ = 40
KC = 1296
KP = 1408
SHARE = 11
F32, BF16 = jnp.float32, jnp.bfloat16
NT = (((1,), (1,)), ((), ()))
HIGH = lax.Precision.HIGHEST
MESH = pl.DeviceIdType.MESH
VMEM_LIMIT = 56 << 20


def direction_table():
    theta = (np.arange(ND) + 0.5) * (2.0 * np.pi / ND)
    return np.stack([np.cos(theta), np.sin(theta)]).astype(np.float32)


def split(x):
    hi = x.astype(BF16)
    return hi, (x - hi.astype(F32)).astype(BF16)


def spread_matrix():
    wide = lax.broadcasted_iota(jnp.int32, (128, 768), 1)
    target = ((wide & 255) >> 1) + (wide >> 8) - 1
    return jnp.where(lax.broadcasted_iota(jnp.int32, (128, 768), 0) == target, 1.0, 0.0)


def couple_masks(cp, dev):
    row = (cp >> 7) - dev
    col = (cp & 127) - (lax.broadcasted_iota(jnp.int32, (8, 256), 1) >> 1)
    valid = cp >= 0
    return [
        [jnp.where(valid & (row == dr - 1) & (col == delta - 1), 1.0, 0.0) for delta in range(3)]
        for dr in range(3)
    ]


def build_maps(map_ref, base, CT, M, MF):
    def step(s, _):
        row = map_ref[pl.ds(base + s, 1), :]
        n = ((row >> 13) << 7) | (row & 127)
        rl = (row >> 7) & 63
        col = pl.ds(pl.multiple_of(s * 128, 128), 128)
        CT[:, col] = jnp.where(lax.broadcasted_iota(jnp.int32, (256, 128), 0) == n, 1.0, 0.0).astype(BF16)
        mf = jnp.where(lax.broadcasted_iota(jnp.int32, (64, 128), 0) == rl, 1.0, 0.0)
        MF[:, col] = mf
        M[:, col] = mf.astype(BF16)
        return 0

    lax.fori_loop(0, 128, step, 0)


def substep(f, cx, cy, first_lane, last_lane):
    ox = jnp.maximum(cx, 0.0) * f
    ix = jnp.minimum(cx, 0.0) * f
    oy = jnp.maximum(cy, 0.0) * f
    iy = jnp.minimum(cy, 0.0) * f
    rows = f.shape[0]
    nx = jnp.where(last_lane, 0.0, pltpu.roll(ix, 127, 1))
    px = jnp.where(first_lane, 0.0, pltpu.roll(ox, 1, 1))
    ny = pltpu.roll(iy, rows - 1, 0)
    py = pltpu.roll(oy, 1, 0)
    return f - (ox - ix + nx - px) - (oy - iy + ny - py)


S = 8
HEAD, TAIL = 7, 4
R = SHARE * 64
ONEHOT = 8
RB = ONEHOT * 64
CH = 432


def chunk_offset(i):
    return jnp.where((i & 1) == 1, (i + 1) >> 1, 16 - (i >> 1))


def start_of(dev):
    return dev * 10 + ((dev + 7) >> 3)


def wait_for(ref, sem):
    pltpu.make_async_copy(ref, ref, sem).wait()


def step_kernel(
    e_ref, mask_ref, table_ref, coef_ref, stokes_ref, trig_ref, map_ref, speed_ref, dirs_ref, cp_ref, u_ref, v_ref,
    mix_ref, prof_ref,
    ret, ou_ref, ov_ref,
    E, F1, F2, OH, forced_ref, trow_ref, col_ref, pay1, pay2, arr1, arr2, out, CT, M, MF, LH, FF, acc, dacc, T,
    G, H, cur, edge, halo, part, pin, ostage, ohalo, B,
    o_send, o_recv, p_send, p_recv, a1_send, a1_recv, a2_send, a2_recv, b_send,
    h_send, h_recv, r_send, r_recv,
):
    grp = lax.axis_index("grp")
    dev = lax.axis_index("dev")
    q16 = dev >> 3
    owner = (dev & 7) == 0
    first = start_of(dev)
    linear = grp * 128 + dev
    has_up = linear > 0
    has_down = linear < 255
    up = linear + 255
    up_id = ((up // 128) % 2, up % 128)
    down = linear + 1
    down_id = ((down // 128) % 2, down % 128)

    barrier = pltpu.get_barrier_semaphore()

    def greet(i, _):
        pl.semaphore_signal(barrier, inc=1, device_id=(grp, (dev + i) & 127), device_id_type=MESH)
        return 0

    lax.fori_loop(1, 128, greet, 0)
    pl.semaphore_signal(barrier, inc=1, device_id=(1 - grp, dev), device_id_type=MESH)
    crosses_down = (grp == 0) & (dev == 127)
    crosses_up = (grp == 1) & (dev == 0)

    @pl.when(crosses_down)
    def _():
        pl.semaphore_signal(barrier, inc=1, device_id=down_id, device_id_type=MESH)

    @pl.when(crosses_up)
    def _():
        pl.semaphore_signal(barrier, inc=1, device_id=up_id, device_id_type=MESH)

    masks = couple_masks(cp_ref[...], dev)
    surface = [u_ref[0], v_ref[0]]
    rows = []
    for dr in range(3):
        for q in range(3):
            pieces = []
            for delta in range(3):
                m = masks[dr][delta]
                pieces.append(jnp.sum(m if q == 2 else m * surface[q], axis=0, keepdims=True))
            rows.append(jnp.concatenate(pieces, axis=1))
        rows.append(jnp.zeros((5, 768), F32))
    sums = lax.dot_general(
        jnp.concatenate(rows, axis=0), spread_matrix(), NT, precision=HIGH, preferred_element_type=F32
    )
    for dr in range(3):
        part[dr] = sums[dr * 8 : (dr + 1) * 8]

    def stage_ocean(slot, a, b):
        def level(z, _):
            for side, line in ((0, 0), (1, 7)):
                ostage[slot, side, 0, pl.ds(z, 1), :] = a(z)[line : line + 1]
                ostage[slot, side, 1, pl.ds(z, 1), :] = b(z)[line : line + 1]
            return 0

        lax.fori_loop(0, NZ, level, 0, unroll=8)

    stage_ocean(0, lambda z: u_ref[z], lambda z: v_ref[z])
    build_maps(map_ref, grp * 128, CT, M, MF)

    trow_ref[...] = jnp.full((8, KP), -1, jnp.int32)
    trow_ref[0:4, :KC] = table_ref[...]
    OH_rows = trow_ref[...].astype(F32)
    line8 = lax.broadcasted_iota(jnp.int32, (8, KP), 0)
    wide_coef = jnp.concatenate([coef_ref[...].reshape(1, KC), jnp.zeros((1, KP - KC), F32)], axis=1)
    col_ref[...] = jnp.transpose(jnp.where(line8 < 4, OH_rows, wide_coef))
    tail = jnp.zeros((KP - KC, 256), BF16)
    E[KC:, :] = tail
    F1[KC:, :] = tail
    F2[KC:, :] = tail
    hi, lo = split(e_ref[...])
    E[:KC, :128] = hi
    E[:KC, 128:] = lo

    def gather(i, _):
        rows = pl.ds(pl.multiple_of(i * CH, 16), CH)
        lanes = lax.broadcasted_iota(jnp.int32, (CH, KP), 1).astype(F32)
        e = e_ref[rows, :]
        cols = col_ref[rows, :]
        for m in range(4):
            OH[m * CH : (m + 1) * CH, :] = jnp.where(lanes == cols[:, m : m + 1], 1.0, 0.0).astype(BF16)
        p = jnp.dot(OH[...], E[...], preferred_element_type=F32)
        p = p[:, :128] + p[:, 128:]
        g = [p[m * CH : (m + 1) * CH] for m in range(4)]
        s = cols[:, 4:5]
        ee = e * e
        e2 = 2.0 * e
        a = s * (ee * (g[0] + g[1]) - e2 * g[0] * g[1])
        b = s * (ee * (g[2] + g[3]) - e2 * g[2] * g[3])
        forced_ref[rows, :] = e - (a + b)
        ah, al = split(a)
        bh, bl = split(b)
        F1[rows, :128] = ah
        F1[rows, 128:] = al
        F2[rows, :128] = bh
        F2[rows, 128:] = bl
        return 0

    lax.fori_loop(0, KC // CH, gather, 0)

    mask = mask_ref[...].astype(F32)

    def scatter(i, _):
        rows = pl.ds(pl.multiple_of(i * CH, 16), CH)
        b = lax.broadcasted_iota(jnp.int32, (CH, KP), 0) + i * CH

        def onehot(m):
            return jnp.where(b == trow_ref[m : m + 1, :], 1.0, 0.0)

        p = jnp.dot((onehot(0) + onehot(1)).astype(BF16), F1[...], preferred_element_type=F32)
        p = p + jnp.dot((onehot(2) + onehot(3)).astype(BF16), F2[...], preferred_element_type=F32)
        forced_ref[rows, :] = mask * (forced_ref[rows, :] + 0.5 * (p[:, :128] + p[:, 128:]))
        return 0

    lax.fori_loop(0, KC // CH, scatter, 0)

    def destination(n):
        return (((q16 - chunk_offset(n >> 3)) & 15) << 3) | ((dev + n) & 7)

    forced_ref[KC:, :] = jnp.zeros((KP - KC, 128), F32)
    weights = trig_ref[...] * jnp.concatenate([stokes_ref[...].reshape(1, KC), jnp.zeros((1, KP - KC), F32)], axis=1)
    drift_own = jnp.dot(weights, forced_ref[...], precision=HIGH, preferred_element_type=F32)

    def ocean_copy(slot, side):
        return pltpu.make_async_remote_copy(
            src_ref=ostage.at[slot, side],
            dst_ref=ohalo.at[slot, 1 - side],
            send_sem=o_send.at[slot, side],
            recv_sem=o_recv.at[slot, 1 - side],
            device_id=up_id if side == 0 else down_id,
            device_id_type=MESH,
        )

    def ocean_start(slot):
        for side, there in ((0, has_up), (1, has_down)):
            @pl.when(there)
            def _(side=side):
                ocean_copy(slot, side).start()

    def ocean_wait(slot):
        for side, there in ((0, has_up), (1, has_down)):
            @pl.when(there)
            def _(side=side):
                wait_for(ostage.at[slot, side], o_send.at[slot, side])
                wait_for(ohalo.at[slot, side], o_recv.at[slot, side])

    def part_copy(side):
        return pltpu.make_async_remote_copy(
            src_ref=part.at[2 * side],
            dst_ref=pin.at[1 - side],
            send_sem=p_send.at[side],
            recv_sem=p_recv.at[1 - side],
            device_id=(grp, (dev + 127 + 2 * side) & 127),
            device_id_type=MESH,
        )

    def fill(t, _):
        for r in range(4):
            d = t * 4 + r
            base = start_of(d)
            for k in range(HEAD):
                pay1[d, k] = forced_ref[pl.ds(base + k, 1), :]
            for k in range(3):
                pay2[d, k] = forced_ref[pl.ds(base + HEAD + k, 1), :]
            for q in range(2):
                pay2[d, 3 + q] = drift_own[q : q + 1]
            pay2[d, 7] = forced_ref[pl.ds(base + 10, 1), :]
        return 0

    lax.fori_loop(0, 32, fill, 0)

    pl.semaphore_wait(barrier, 128 + jnp.where(crosses_down | crosses_up, 1, 0))

    for side, there in ((0, dev > 0), (1, dev < 127)):
        @pl.when(there)
        def _(side=side):
            part_copy(side).start()

    pltpu.make_async_copy(pay1.at[dev], arr1.at[dev], a1_recv.at[q16]).start()

    def send1(n, _):
        dest = destination(n)
        pltpu.make_async_remote_copy(
            src_ref=pay1.at[dest],
            dst_ref=arr1.at[dev],
            send_sem=a1_send,
            recv_sem=a1_recv.at[q16],
            device_id=(grp, dest),
            device_id_type=MESH,
        ).start()
        return 0

    lax.fori_loop(1, 128, send1, 0)

    for side, there in ((0, dev > 0), (1, dev < 127)):
        @pl.when(there)
        def _(side=side):
            wait_for(part.at[2 * side], p_send.at[side])
            wait_for(pin.at[side], p_recv.at[side])

    total = part[1] + jnp.where(dev > 0, pin[0], 0.0) + jnp.where(dev < 127, pin[1], 0.0)
    speeds = 0.3 * total[0:2] / (total[2:3] + 1.0)

    def fill_currents(t, _):
        for r in range(8):
            for q in range(2):
                pay2[t * 8 + r, 5 + q] = speeds[q : q + 1]
        return 0

    lax.fori_loop(0, 16, fill_currents, 0)

    @pl.when(owner)
    def _():
        pltpu.make_async_copy(pay2.at[dev], arr2.at[dev], a2_recv.at[q16]).start()

    @pl.when(jnp.logical_not(owner))
    def _():
        pltpu.make_async_copy(pay2.at[dev, pl.ds(0, 7)], arr2.at[dev, pl.ds(0, 7)], a2_recv.at[q16]).start()

    def send2(n, _):
        dest = destination(n)

        @pl.when((dest & 7) == 0)
        def _():
            pltpu.make_async_remote_copy(
                src_ref=pay2.at[dest],
                dst_ref=arr2.at[dev],
                send_sem=b_send,
                recv_sem=a2_recv.at[q16],
                device_id=(grp, dest),
                device_id_type=MESH,
            ).start()

        @pl.when((dest & 7) != 0)
        def _():
            pltpu.make_async_remote_copy(
                src_ref=pay2.at[dest, pl.ds(0, 7)],
                dst_ref=arr2.at[dev, pl.ds(0, 7)],
                send_sem=a2_send,
                recv_sem=a2_recv.at[q16],
                device_id=(grp, dest),
                device_id_type=MESH,
            ).start()

        return 0

    lax.fori_loop(1, 128, send2, 0)
    zero_row = jnp.zeros((1, 128), F32)
    top = grp == 0

    acc[...] = jnp.zeros_like(acc)
    dacc[...] = jnp.zeros_like(dacc)

    def forward(low, count, last):
        n = count * 64

        def chunk_step(i, _):
            chunk = (q16 + chunk_offset(i)) & 15
            if last:
                @pl.when(owner)
                def _():
                    wait_for(arr2.at[pl.ds(chunk * S, S)], a2_recv.at[chunk])

                @pl.when(jnp.logical_not(owner))
                def _():
                    wait_for(arr2.at[pl.ds(chunk * S, S), pl.ds(0, 7)], a2_recv.at[chunk])
            else:
                wait_for(arr1.at[pl.ds(chunk * S, S)], a1_recv.at[chunk])

            for j in range(S):
                s = chunk * S + j
                cols = pl.ds(pl.multiple_of(s * 128, 128), 128)
                c = slice(j * 128, (j + 1) * 128)
                for k in range(count):
                    x = (arr2[s, 7 if k == 3 else k]) if last else arr1[s, k]
                    hi, lo = split(jnp.broadcast_to(x, (16, 128)))
                    for q in range(4):
                        m = M[q * 16 : (q + 1) * 16, cols]
                        r = k * 64 + q * 16
                        LH[r : r + 16, c] = m * hi
                        LH[n + r : n + r + 16, c] = m * lo
                if last:
                    row = map_ref[pl.ds(grp * 128 + s, 1), :] >> 7
                    pieces = []
                    for q in range(2):
                        cur[q, pl.ds(8 + s, 1), :] = arr2[s, 5 + q]
                        x = arr2[s, 3 + q]
                        for dr in range(3):
                            pieces.append(jnp.where(row == dev + (dr - 1), x, zero_row))
                    pieces += [zero_row, zero_row]
                    piece = jnp.concatenate(pieces, axis=0)
                    hi = piece.astype(BF16).astype(F32)
                    LH[2 * n : 2 * n + 16, c] = jnp.concatenate([hi, piece - hi], axis=0).astype(BF16)
            c = CT[:, pl.ds(pl.multiple_of(chunk * (S * 128), 128), S * 128)]
            d = lax.dot_general(LH[: 2 * n + (16 if last else 0)], c, NT, preferred_element_type=F32)
            acc[low : low + n] += d[:n] + d[n : 2 * n]
            if last:
                dacc[...] += d[2 * n :]
            return 0

        lax.fori_loop(0, 128 // S, chunk_step, 0)

    forward(0, HEAD, False)
    forward(HEAD * 64, TAIL, True)

    for k in range(SHARE):
        low = acc[k * 64 : (k + 1) * 64, 0:128]
        high = acc[k * 64 : (k + 1) * 64, 128:256]
        G[k, 8:72, :] = low
        G[k, 72:136, :] = high
        edge[0, k : k + 1, :] = jnp.where(top, high[63:64], low[0:1])
        edge[1, k : k + 1, :] = jnp.where(top, high[62:63], low[1:2])
    for r in range(2):
        for q in range(2):
            edge[r, SHARE + q : SHARE + q + 1, :] = jnp.where(
                top, cur[q, 135 - r : 136 - r, :], cur[q, 8 + r : 9 + r, :]
            )
        edge[r, 13:16, :] = jnp.zeros((3, 128), F32)
    exchange = pltpu.make_async_remote_copy(
        src_ref=edge, dst_ref=halo, send_sem=h_send, recv_sem=h_recv, device_id=(1 - grp, dev), device_id_type=MESH
    )
    exchange.start()
    ocean_start(0)

    below_on = jnp.where(top, 1.0, 0.0)
    above_on = 1.0 - below_on
    blank = jnp.zeros((6, 128), F32)

    def pad(dst, index, k):
        h0 = halo[0, k : k + 1, :]
        h1 = halo[1, k : k + 1, :]
        dst[index, 0:8, :] = jnp.concatenate([blank, h1, h0], axis=0) * above_on
        dst[index, 136:144, :] = jnp.concatenate([h0, h1, blank], axis=0) * below_on

    lane = lax.broadcasted_iota(jnp.int32, (144, 128), 1)
    line = lax.broadcasted_iota(jnp.int32, (144, 128), 0)
    first_lane, last_lane = lane == 0, lane == 127
    keep = jnp.where(line < 8, above_on, jnp.where(line >= 136, below_on, 1.0))

    def pace_of(k):
        comp = jnp.minimum(first + k, KC - 1)
        way = lax.rem(comp, ND)
        pace = speed_ref[comp]
        return pace * dirs_ref[0, way], pace * dirs_ref[1, way]

    def propagate(k, _):
        pace_x, pace_y = pace_of(k)
        cx = cur[0] + pace_x
        cy = cur[1] + pace_y
        f = substep(G[k], cx, cy, first_lane, last_lane) * keep
        f = substep(f, cx, cy, first_lane, last_lane)
        H[k] = f[8:136]
        return 0

    def backward(t, _):
        chunk = (q16 - chunk_offset(15 - t)) & 15
        c = CT[:, pl.ds(pl.multiple_of(chunk * (S * 128), 128), S * 128)]
        T[...] = jnp.dot(FF[:RB], c, preferred_element_type=F32) + jnp.dot(FF[RB:], c, preferred_element_type=F32)
        where = map_ref[pl.ds(pl.multiple_of(grp * 128 + chunk * S, 8), S), :]
        row, col = where >> 7, where & 127
        taken = [jnp.zeros((S, 128), F32) for _ in range(SHARE - ONEHOT)]
        for r in range(128):
            hit = row == r
            for k in range(SHARE - ONEHOT):
                x = jnp.broadcast_to(H[ONEHOT + k, r : r + 1, :], (S, 128))
                y = jnp.take_along_axis(x, col, axis=1, mode="promise_in_bounds")
                taken[k] = jnp.where(hit, y, taken[k])
        for j in range(S):
            s = chunk * S + j
            for k in range(SHARE - ONEHOT):
                out[s, ONEHOT + k] = taken[k][j : j + 1]
            m = MF[:, pl.ds(pl.multiple_of(s * 128, 128), 128)]
            for k in range(ONEHOT):
                out[s, k] = jnp.sum(T[k * 64 : (k + 1) * 64, j * 128 : (j + 1) * 128] * m, axis=0, keepdims=True)

        def post(j, _):
            s = chunk * S + j

            @pl.when((s != dev) & owner)
            def _():
                pltpu.make_async_remote_copy(
                    src_ref=out.at[s],
                    dst_ref=ret.at[pl.ds(first, 11)],
                    send_sem=r_send,
                    recv_sem=r_recv,
                    device_id=(grp, s),
                    device_id_type=MESH,
                ).start()

            @pl.when((s != dev) & jnp.logical_not(owner))
            def _():
                pltpu.make_async_remote_copy(
                    src_ref=out.at[s, pl.ds(0, 10)],
                    dst_ref=ret.at[pl.ds(first, 10)],
                    send_sem=r_send,
                    recv_sem=r_recv,
                    device_id=(grp, s),
                    device_id_type=MESH,
                ).start()

            return 0

        lax.fori_loop(0, S, post, 0)
        return 0

    none = jnp.zeros((8, 128), F32)
    for k in range(SHARE):
        G[k, 0:8, :] = none
        G[k, 136:144, :] = none
    for q in range(2):
        cur[q, 0:8, :] = none
        cur[q, 136:144, :] = none

    lax.fori_loop(0, SHARE, propagate, 0)
    exchange.wait()
    for k in range(SHARE):
        pad(G, k, k)
    for q in range(2):
        pad(cur, q, SHARE + q)
    strip = pl.multiple_of(jnp.where(top, 112, 0), 8)
    strip_lane = lax.broadcasted_iota(jnp.int32, (32, 128), 1)
    strip_line = lax.broadcasted_iota(jnp.int32, (32, 128), 0) + strip
    strip_keep = jnp.where(strip_line < 8, above_on, jnp.where(strip_line >= 136, below_on, 1.0))
    strip_u, strip_v = cur[0, pl.ds(strip, 32), :], cur[1, pl.ds(strip, 32), :]
    for k in range(SHARE):
        pace_x, pace_y = pace_of(k)
        cx, cy = strip_u + pace_x, strip_v + pace_y
        f = substep(G[k, pl.ds(strip, 32), :], cx, cy, strip_lane == 0, strip_lane == 127) * strip_keep
        f = substep(f, cx, cy, strip_lane == 0, strip_lane == 127)
        H[k, pl.ds(pl.multiple_of(jnp.where(top, 120, 0), 8), 8), :] = jnp.where(top, f[16:24], f[8:16])
    for k in range(ONEHOT):
        for h in range(2):
            hi, lo = split(H[k, h * 64 : 64 + h * 64, :])
            FF[k * 64 : (k + 1) * 64, h * 128 : (h + 1) * 128] = hi
            FF[RB + k * 64 : RB + (k + 1) * 64, h * 128 : (h + 1) * 128] = lo
    lax.fori_loop(0, 5, backward, 0)

    drift = dacc[0:8] + dacc[8:16]
    wave_row = dev + lax.rem(lax.broadcasted_iota(jnp.int32, (8, 128), 0), 3) - 1
    drift = jnp.where(wave_row >= 64, drift[:, 128:], drift[:, :128])
    wide = jnp.dot(drift, spread_matrix(), precision=HIGH, preferred_element_type=F32)
    masks = couple_masks(cp_ref[...], dev)
    cells = []
    for q in range(2):
        sum_q = jnp.zeros((8, 256), F32)
        for dr in range(3):
            for delta in range(3):
                sum_q = sum_q + masks[dr][delta] * wide[q * 3 + dr : q * 3 + dr + 1, delta * 256 : (delta + 1) * 256]
        cells.append(sum_q)
    us, vs = cells

    oline = lax.broadcasted_iota(jnp.int32, (8, 256), 0)
    olane = lax.broadcasted_iota(jnp.int32, (8, 256), 1)
    coriolis = 0.5 + (linear * 8 + oline).astype(F32) / 2048.0
    fvs, fus = coriolis * vs, coriolis * us

    def ocean_step(slot, source, emit):
        def lap(a, z, q):
            above = jnp.where(has_up, ohalo[slot, 0, q, pl.ds(z, 1), :], 0.0)
            below = jnp.where(has_down, ohalo[slot, 1, q, pl.ds(z, 1), :], 0.0)
            r = jnp.where(olane == 255, 0.0, pltpu.roll(a, 255, 1)) + jnp.where(olane == 0, 0.0, pltpu.roll(a, 1, 1))
            r = r + jnp.where(oline == 0, above, pltpu.roll(a, 1, 0)) + jnp.where(oline == 7, below, pltpu.roll(a, 7, 0))
            return r - 4.0 * a

        def level(z, carry):
            pu, pv = carry
            u, v = source(0, z), source(1, z)
            zn = jnp.minimum(z + 1, NZ - 1)
            m0 = mix_ref[z]
            m1 = jnp.where(z == NZ - 1, 0.0, mix_ref[zn])
            nu, nv = source(0, zn), source(1, zn)
            p = prof_ref[z]
            wu = m1 * (nu - u) - m0 * (u - pu)
            wv = m1 * (nv - v) - m0 * (v - pv)
            emit(
                z,
                u + 0.2 * (0.2 * lap(u, z, 0) + wu + coriolis * v + p * fvs),
                v + 0.2 * (0.2 * lap(v, z, 1) + wv - coriolis * u - p * fus),
            )
            return u, v

        zero = jnp.zeros((8, 256), F32)
        lax.fori_loop(0, NZ, level, (zero, zero), unroll=8)

    def emit1(z, u, v):
        B[0, z] = u
        B[1, z] = v

    def emit2(z, u, v):
        ou_ref[z] = u
        ov_ref[z] = v

    ocean_wait(0)
    ocean_step(0, lambda q, z: (u_ref, v_ref)[q][z], emit1)
    stage_ocean(1, lambda z: B[0, z], lambda z: B[1, z])
    ocean_start(1)

    lax.fori_loop(5, 128 // S, backward, 0)
    for k in range(10):
        ret[first + k] = out[dev, k]

    @pl.when(owner)
    def _():
        ret[first + 10] = out[dev, 10]

    ocean_wait(1)
    ocean_step(1, lambda q, z: B[q, z], emit2)

    wait_for(pay1.at[pl.ds(0, 127)], a1_send)

    @pl.when(owner)
    def _():
        wait_for(pay2.at[pl.ds(0, 112), pl.ds(0, 7)], a2_send)
        wait_for(pay2.at[pl.ds(0, 15)], b_send)
        wait_for(out.at[pl.ds(0, 127)], r_send)
        wait_for(ret.at[pl.ds(0, KC - 11)], r_recv)

    @pl.when(jnp.logical_not(owner))
    def _():
        wait_for(pay2.at[pl.ds(0, 111), pl.ds(0, 7)], a2_send)
        wait_for(pay2.at[pl.ds(0, 16)], b_send)
        wait_for(out.at[pl.ds(0, 127), pl.ds(0, 10)], r_send)
        wait_for(ret.at[pl.ds(0, KC - 10)], r_recv)


def finish_kernel(r_ref, mask_ref, u_ref, v_ref, o_ref, ou_ref, ov_ref, sem):
    copies = [pltpu.make_async_copy(u_ref, ou_ref, sem.at[0]), pltpu.make_async_copy(v_ref, ov_ref, sem.at[1])]
    for copy in copies:
        copy.start()
    o_ref[...] = r_ref[...] * mask_ref[...].astype(F32)
    for copy in copies:
        copy.wait()


def body(spectra, sea_mask, card_map, dia_table, dia_coef, speed, stokes_weight, couple_point, ocean_u, ocean_v, mixing):
    sds = jax.ShapeDtypeStruct
    dirs = direction_table()
    trig = np.zeros((8, KP), np.float32)
    trig[:2, :KC] = np.tile(dirs, (1, KC // ND))
    profile = np.exp(-3.0 * (np.arange(NZ) + 0.5) / NZ).astype(np.float32)
    vmem = pl.BlockSpec(memory_space=pltpu.VMEM)
    smem = pl.BlockSpec(memory_space=pltpu.SMEM)
    dma = pltpu.SemaphoreType.DMA
    scratch = [
        pltpu.VMEM((KP, 256), BF16),
        pltpu.VMEM((KP, 256), BF16),
        pltpu.VMEM((KP, 256), BF16),
        pltpu.VMEM((4 * CH, KP), BF16),
        pltpu.VMEM((KP, 128), F32),
        pltpu.VMEM((8, KP), jnp.int32),
        pltpu.VMEM((KP, 8), F32),
        pltpu.VMEM((128, HEAD, 1, 128), F32),
        pltpu.VMEM((128, 8, 1, 128), F32),
        pltpu.VMEM((128, HEAD, 1, 128), F32),
        pltpu.VMEM((128, 8, 1, 128), F32),
        pltpu.VMEM((128, SHARE, 1, 128), F32),
        pltpu.VMEM((256, 16384), BF16),
        pltpu.VMEM((64, 16384), BF16),
        pltpu.VMEM((64, 16384), F32),
        pltpu.VMEM((128 * HEAD, S * 128), BF16),
        pltpu.VMEM((2 * RB, 256), BF16),
        pltpu.VMEM((R, 256), F32),
        pltpu.VMEM((16, 256), F32),
        pltpu.VMEM((RB, S * 128), F32),
        pltpu.VMEM((SHARE, 144, 128), F32),
        pltpu.VMEM((SHARE, 128, 128), F32),
        pltpu.VMEM((2, 144, 128), F32),
        pltpu.VMEM((2, 16, 128), F32),
        pltpu.VMEM((2, 16, 128), F32),
        pltpu.VMEM((3, 8, 128), F32),
        pltpu.VMEM((2, 8, 128), F32),
        pltpu.VMEM((2, 2, 2, NZ, 256), F32),
        pltpu.VMEM((2, 2, 2, NZ, 256), F32),
        pltpu.VMEM((2, NZ, 8, 256), F32),
        dma((2, 2)), dma((2, 2)), dma((2,)), dma((2,)),
        dma, dma((16,)), dma, dma((16,)), dma, dma, dma, dma, dma,
    ]
    ret, new_u, new_v = pl.pallas_call(
        step_kernel,
        out_shape=(sds((KC, 1, 128), F32), sds((NZ, 8, 256), F32), sds((NZ, 8, 256), F32)),
        in_specs=[vmem] * 7 + [smem] * 2 + [vmem] * 3 + [smem] * 2,
        out_specs=(vmem,) * 3,
        scratch_shapes=scratch,
        compiler_params=pltpu.CompilerParams(
            vmem_limit_bytes=VMEM_LIMIT, collective_id=0, has_side_effects=True
        ),
        name="step",
    )(
        spectra, sea_mask.reshape(1, 128), dia_table, dia_coef, stokes_weight,
        jnp.asarray(trig), card_map.reshape(256, 128), speed, jnp.asarray(dirs), couple_point, ocean_u, ocean_v,
        mixing, jnp.asarray(profile),
    )
    hbm = pl.BlockSpec(memory_space=pl.ANY)
    return pl.pallas_call(
        finish_kernel,
        out_shape=(sds((KC, 128), F32), sds((NZ, 8, 256), F32), sds((NZ, 8, 256), F32)),
        in_specs=[vmem, vmem, hbm, hbm],
        out_specs=(vmem, hbm, hbm),
        scratch_shapes=[dma((2,))],
        name="finish",
    )(ret.reshape(KC, 128), sea_mask.reshape(1, 128), new_u, new_v)


def solution(mesh):
    both = ("grp", "dev")
    in_specs = (P(None, both), P(both), P(), P(), P(), P(), P(), P(both, None), P(None, both, None), P(None, both, None), P())
    out_specs = (P(None, both), P(None, both, None), P(None, both, None))
    return jax.shard_map(body, mesh=mesh, in_specs=in_specs, out_specs=out_specs, check_vma=False)
```

```python
import jax
import jax.numpy as jnp
import numpy as np
from jax import lax
from jax.experimental import pallas as pl
from jax.experimental.pallas import tpu as pltpu
from jax.sharding import PartitionSpec as P

ND = 36
NZ = 40
KC = 1296
KP = 1408
SHARE = 11
F32, BF16 = jnp.float32, jnp.bfloat16
NT = (((1,), (1,)), ((), ()))
HIGH = lax.Precision.HIGHEST
MESH = pl.DeviceIdType.MESH
VMEM_LIMIT = 56 << 20


def direction_table():
    theta = (np.arange(ND) + 0.5) * (2.0 * np.pi / ND)
    return np.stack([np.cos(theta), np.sin(theta)]).astype(np.float32)


def split(x):
    hi = x.astype(BF16)
    return hi, (x - hi.astype(F32)).astype(BF16)


def spread_matrix():
    wide = lax.broadcasted_iota(jnp.int32, (128, 768), 1)
    target = ((wide & 255) >> 1) + (wide >> 8) - 1
    return jnp.where(lax.broadcasted_iota(jnp.int32, (128, 768), 0) == target, 1.0, 0.0)


def couple_masks(cp, dev):
    row = (cp >> 7) - dev
    col = (cp & 127) - (lax.broadcasted_iota(jnp.int32, (8, 256), 1) >> 1)
    valid = cp >= 0
    return [
        [jnp.where(valid & (row == dr - 1) & (col == delta - 1), 1.0, 0.0) for delta in range(3)]
        for dr in range(3)
    ]


def build_maps(map_ref, base, CT, M, MF):
    def step(s, _):
        row = map_ref[pl.ds(base + s, 1), :]
        n = ((row >> 13) << 7) | (row & 127)
        rl = (row >> 7) & 63
        col = pl.ds(pl.multiple_of(s * 128, 128), 128)
        CT[:, col] = jnp.where(lax.broadcasted_iota(jnp.int32, (256, 128), 0) == n, 1.0, 0.0).astype(BF16)
        mf = jnp.where(lax.broadcasted_iota(jnp.int32, (64, 128), 0) == rl, 1.0, 0.0)
        MF[:, col] = mf
        M[:, col] = mf.astype(BF16)
        return 0

    lax.fori_loop(0, 128, step, 0)


def substep(f, cx, cy, first_lane, last_lane):
    ox = jnp.maximum(cx, 0.0) * f
    ix = jnp.minimum(cx, 0.0) * f
    oy = jnp.maximum(cy, 0.0) * f
    iy = jnp.minimum(cy, 0.0) * f
    rows = f.shape[0]
    nx = jnp.where(last_lane, 0.0, pltpu.roll(ix, 127, 1))
    px = jnp.where(first_lane, 0.0, pltpu.roll(ox, 1, 1))
    ny = pltpu.roll(iy, rows - 1, 0)
    py = pltpu.roll(oy, 1, 0)
    return f - (ox - ix + nx - px) - (oy - iy + ny - py)


S = 8
HEAD, TAIL = 7, 4
R = SHARE * 64
ONEHOT = 8
RB = ONEHOT * 64
CH = 432


def chunk_offset(i):
    return jnp.where((i & 1) == 1, (i + 1) >> 1, 16 - (i >> 1))


def start_of(dev):
    return dev * 10 + ((dev + 7) >> 3)


def wait_for(ref, sem):
    pltpu.make_async_copy(ref, ref, sem).wait()


def step_kernel(
    e_ref, mask_ref, table_ref, coef_ref, stokes_ref, trig_ref, map_ref, speed_ref, dirs_ref, cp_ref, u_ref, v_ref,
    mix_ref, prof_ref,
    ret, ou_ref, ov_ref,
    E, F1, F2, OH, forced_ref, trow_ref, col_ref, pay1, pay2, arr1, arr2, out, CT, M, MF, LH, FF, acc, dacc, T,
    G, H, cur, edge, halo, part, pin, ostage, ohalo, B,
    o_send, o_recv, p_send, p_recv, a1_send, a1_recv, a2_send, a2_recv, b_send,
    h_send, h_recv, r_send, r_recv,
):
    grp = lax.axis_index("grp")
    dev = lax.axis_index("dev")
    q16 = dev >> 3
    owner = (dev & 7) == 0
    first = start_of(dev)
    linear = grp * 128 + dev
    has_up = linear > 0
    has_down = linear < 255
    up = linear + 255
    up_id = ((up // 128) % 2, up % 128)
    down = linear + 1
    down_id = ((down // 128) % 2, down % 128)

    barrier = pltpu.get_barrier_semaphore()

    def greet(i, _):
        pl.semaphore_signal(barrier, inc=1, device_id=(grp, (dev + i) & 127), device_id_type=MESH)
        return 0

    lax.fori_loop(1, 128, greet, 0)
    pl.semaphore_signal(barrier, inc=1, device_id=(1 - grp, dev), device_id_type=MESH)
    crosses_down = (grp == 0) & (dev == 127)
    crosses_up = (grp == 1) & (dev == 0)

    @pl.when(crosses_down)
    def _():
        pl.semaphore_signal(barrier, inc=1, device_id=down_id, device_id_type=MESH)

    @pl.when(crosses_up)
    def _():
        pl.semaphore_signal(barrier, inc=1, device_id=up_id, device_id_type=MESH)

    masks = couple_masks(cp_ref[...], dev)
    surface = [u_ref[0], v_ref[0]]
    rows = []
    for dr in range(3):
        for q in range(3):
            pieces = []
            for delta in range(3):
                m = masks[dr][delta]
                pieces.append(jnp.sum(m if q == 2 else m * surface[q], axis=0, keepdims=True))
            rows.append(jnp.concatenate(pieces, axis=1))
        rows.append(jnp.zeros((5, 768), F32))
    sums = lax.dot_general(
        jnp.concatenate(rows, axis=0), spread_matrix(), NT, precision=HIGH, preferred_element_type=F32
    )
    for dr in range(3):
        part[dr] = sums[dr * 8 : (dr + 1) * 8]

    def stage_ocean(slot, a, b):
        def level(z, _):
            for side, line in ((0, 0), (1, 7)):
                ostage[slot, side, 0, pl.ds(z, 1), :] = a(z)[line : line + 1]
                ostage[slot, side, 1, pl.ds(z, 1), :] = b(z)[line : line + 1]
            return 0

        lax.fori_loop(0, NZ, level, 0, unroll=8)

    stage_ocean(0, lambda z: u_ref[z], lambda z: v_ref[z])
    build_maps(map_ref, grp * 128, CT, M, MF)

    trow_ref[...] = jnp.full((8, KP), -1, jnp.int32)
    trow_ref[0:4, :KC] = table_ref[...]
    OH_rows = trow_ref[...].astype(F32)
    line8 = lax.broadcasted_iota(jnp.int32, (8, KP), 0)
    wide_coef = jnp.concatenate([coef_ref[...].reshape(1, KC), jnp.zeros((1, KP - KC), F32)], axis=1)
    col_ref[...] = jnp.transpose(jnp.where(line8 < 4, OH_rows, wide_coef))
    tail = jnp.zeros((KP - KC, 256), BF16)
    E[KC:, :] = tail
    F1[KC:, :] = tail
    F2[KC:, :] = tail
    hi, lo = split(e_ref[...])
    E[:KC, :128] = hi
    E[:KC, 128:] = lo

    def gather(i, _):
        rows = pl.ds(pl.multiple_of(i * CH, 16), CH)
        lanes = lax.broadcasted_iota(jnp.int32, (CH, KP), 1).astype(F32)
        e = e_ref[rows, :]
        cols = col_ref[rows, :]
        for m in range(4):
            OH[m * CH : (m + 1) * CH, :] = jnp.where(lanes == cols[:, m : m + 1], 1.0, 0.0).astype(BF16)
        p = jnp.dot(OH[...], E[...], preferred_element_type=F32)
        p = p[:, :128] + p[:, 128:]
        g = [p[m * CH : (m + 1) * CH] for m in range(4)]
        s = cols[:, 4:5]
        ee = e * e
        e2 = 2.0 * e
        a = s * (ee * (g[0] + g[1]) - e2 * g[0] * g[1])
        b = s * (ee * (g[2] + g[3]) - e2 * g[2] * g[3])
        forced_ref[rows, :] = e - (a + b)
        ah, al = split(a)
        bh, bl = split(b)
        F1[rows, :128] = ah
        F1[rows, 128:] = al
        F2[rows, :128] = bh
        F2[rows, 128:] = bl
        return 0

    lax.fori_loop(0, KC // CH, gather, 0)

    mask = mask_ref[...].astype(F32)

    def scatter(i, _):
        rows = pl.ds(pl.multiple_of(i * CH, 16), CH)
        b = lax.broadcasted_iota(jnp.int32, (CH, KP), 0) + i * CH

        def onehot(m):
            return jnp.where(b == trow_ref[m : m + 1, :], 1.0, 0.0)

        p = jnp.dot((onehot(0) + onehot(1)).astype(BF16), F1[...], preferred_element_type=F32)
        p = p + jnp.dot((onehot(2) + onehot(3)).astype(BF16), F2[...], preferred_element_type=F32)
        forced_ref[rows, :] = mask * (forced_ref[rows, :] + 0.5 * (p[:, :128] + p[:, 128:]))
        return 0

    lax.fori_loop(0, KC // CH, scatter, 0)

    def destination(n):
        return (((q16 - chunk_offset(n >> 3)) & 15) << 3) | ((dev + n) & 7)

    forced_ref[KC:, :] = jnp.zeros((KP - KC, 128), F32)
    weights = trig_ref[...] * jnp.concatenate([stokes_ref[...].reshape(1, KC), jnp.zeros((1, KP - KC), F32)], axis=1)
    drift_own = jnp.dot(weights, forced_ref[...], precision=HIGH, preferred_element_type=F32)

    def ocean_copy(slot, side):
        return pltpu.make_async_remote_copy(
            src_ref=ostage.at[slot, side],
            dst_ref=ohalo.at[slot, 1 - side],
            send_sem=o_send.at[slot, side],
            recv_sem=o_recv.at[slot, 1 - side],
            device_id=up_id if side == 0 else down_id,
            device_id_type=MESH,
        )

    def ocean_start(slot):
        for side, there in ((0, has_up), (1, has_down)):
            @pl.when(there)
            def _(side=side):
                ocean_copy(slot, side).start()

    def ocean_wait(slot):
        for side, there in ((0, has_up), (1, has_down)):
            @pl.when(there)
            def _(side=side):
                wait_for(ostage.at[slot, side], o_send.at[slot, side])
                wait_for(ohalo.at[slot, side], o_recv.at[slot, side])

    def part_copy(side):
        return pltpu.make_async_remote_copy(
            src_ref=part.at[2 * side],
            dst_ref=pin.at[1 - side],
            send_sem=p_send.at[side],
            recv_sem=p_recv.at[1 - side],
            device_id=(grp, (dev + 127 + 2 * side) & 127),
            device_id_type=MESH,
        )

    def fill(t, _):
        for r in range(4):
            d = t * 4 + r
            base = start_of(d)
            for k in range(HEAD):
                pay1[d, k] = forced_ref[pl.ds(base + k, 1), :]
            for k in range(3):
                pay2[d, k] = forced_ref[pl.ds(base + HEAD + k, 1), :]
            for q in range(2):
                pay2[d, 3 + q] = drift_own[q : q + 1]
            pay2[d, 7] = forced_ref[pl.ds(base + 10, 1), :]
        return 0

    lax.fori_loop(0, 32, fill, 0)

    pl.semaphore_wait(barrier, 128 + jnp.where(crosses_down | crosses_up, 1, 0))

    for side, there in ((0, dev > 0), (1, dev < 127)):
        @pl.when(there)
        def _(side=side):
            part_copy(side).start()

    pltpu.make_async_copy(pay1.at[dev], arr1.at[dev], a1_recv.at[q16]).start()

    def send1(n, _):
        dest = destination(n)
        pltpu.make_async_remote_copy(
            src_ref=pay1.at[dest],
            dst_ref=arr1.at[dev],
            send_sem=a1_send,
            recv_sem=a1_recv.at[q16],
            device_id=(grp, dest),
            device_id_type=MESH,
        ).start()
        return 0

    lax.fori_loop(1, 128, send1, 0)

    for side, there in ((0, dev > 0), (1, dev < 127)):
        @pl.when(there)
        def _(side=side):
            wait_for(part.at[2 * side], p_send.at[side])
            wait_for(pin.at[side], p_recv.at[side])

    total = part[1] + jnp.where(dev > 0, pin[0], 0.0) + jnp.where(dev < 127, pin[1], 0.0)
    speeds = 0.3 * total[0:2] / (total[2:3] + 1.0)

    def fill_currents(t, _):
        for r in range(8):
            for q in range(2):
                pay2[t * 8 + r, 5 + q] = speeds[q : q + 1]
        return 0

    lax.fori_loop(0, 16, fill_currents, 0)

    @pl.when(owner)
    def _():
        pltpu.make_async_copy(pay2.at[dev], arr2.at[dev], a2_recv.at[q16]).start()

    @pl.when(jnp.logical_not(owner))
    def _():
        pltpu.make_async_copy(pay2.at[dev, pl.ds(0, 7)], arr2.at[dev, pl.ds(0, 7)], a2_recv.at[q16]).start()

    def send2(n, _):
        dest = destination(n)

        @pl.when((dest & 7) == 0)
        def _():
            pltpu.make_async_remote_copy(
                src_ref=pay2.at[dest],
                dst_ref=arr2.at[dev],
                send_sem=b_send,
                recv_sem=a2_recv.at[q16],
                device_id=(grp, dest),
                device_id_type=MESH,
            ).start()

        @pl.when((dest & 7) != 0)
        def _():
            pltpu.make_async_remote_copy(
                src_ref=pay2.at[dest, pl.ds(0, 7)],
                dst_ref=arr2.at[dev, pl.ds(0, 7)],
                send_sem=a2_send,
                recv_sem=a2_recv.at[q16],
                device_id=(grp, dest),
                device_id_type=MESH,
            ).start()

        return 0

    lax.fori_loop(1, 128, send2, 0)
    zero_row = jnp.zeros((1, 128), F32)
    top = grp == 0

    acc[...] = jnp.zeros_like(acc)
    dacc[...] = jnp.zeros_like(dacc)

    def forward(low, count, last):
        n = count * 64

        def chunk_step(i, _):
            chunk = (q16 + chunk_offset(i)) & 15
            if last:
                @pl.when(owner)
                def _():
                    wait_for(arr2.at[pl.ds(chunk * S, S)], a2_recv.at[chunk])

                @pl.when(jnp.logical_not(owner))
                def _():
                    wait_for(arr2.at[pl.ds(chunk * S, S), pl.ds(0, 7)], a2_recv.at[chunk])
            else:
                wait_for(arr1.at[pl.ds(chunk * S, S)], a1_recv.at[chunk])

            for j in range(S):
                s = chunk * S + j
                cols = pl.ds(pl.multiple_of(s * 128, 128), 128)
                c = slice(j * 128, (j + 1) * 128)
                for k in range(count):
                    x = (arr2[s, 7 if k == 3 else k]) if last else arr1[s, k]
                    hi, lo = split(jnp.broadcast_to(x, (16, 128)))
                    for q in range(4):
                        m = M[q * 16 : (q + 1) * 16, cols]
                        r = k * 64 + q * 16
                        LH[r : r + 16, c] = m * hi
                        LH[n + r : n + r + 16, c] = m * lo
                if last:
                    row = map_ref[pl.ds(grp * 128 + s, 1), :] >> 7
                    pieces = []
                    for q in range(2):
                        cur[q, pl.ds(8 + s, 1), :] = arr2[s, 5 + q]
                        x = arr2[s, 3 + q]
                        for dr in range(3):
                            pieces.append(jnp.where(row == dev + (dr - 1), x, zero_row))
                    pieces += [zero_row, zero_row]
                    piece = jnp.concatenate(pieces, axis=0)
                    hi = piece.astype(BF16).astype(F32)
                    LH[2 * n : 2 * n + 16, c] = jnp.concatenate([hi, piece - hi], axis=0).astype(BF16)
            c = CT[:, pl.ds(pl.multiple_of(chunk * (S * 128), 128), S * 128)]
            d = lax.dot_general(LH[: 2 * n + (16 if last else 0)], c, NT, preferred_element_type=F32)
            acc[low : low + n] += d[:n] + d[n : 2 * n]
            if last:
                dacc[...] += d[2 * n :]
            return 0

        lax.fori_loop(0, 128 // S, chunk_step, 0)

    forward(0, HEAD, False)
    forward(HEAD * 64, TAIL, True)

    for k in range(SHARE):
        low = acc[k * 64 : (k + 1) * 64, 0:128]
        high = acc[k * 64 : (k + 1) * 64, 128:256]
        G[k, 8:72, :] = low
        G[k, 72:136, :] = high
        edge[0, k : k + 1, :] = jnp.where(top, high[63:64], low[0:1])
        edge[1, k : k + 1, :] = jnp.where(top, high[62:63], low[1:2])
    for r in range(2):
        for q in range(2):
            edge[r, SHARE + q : SHARE + q + 1, :] = jnp.where(
                top, cur[q, 135 - r : 136 - r, :], cur[q, 8 + r : 9 + r, :]
            )
        edge[r, 13:16, :] = jnp.zeros((3, 128), F32)
    exchange = pltpu.make_async_remote_copy(
        src_ref=edge, dst_ref=halo, send_sem=h_send, recv_sem=h_recv, device_id=(1 - grp, dev), device_id_type=MESH
    )
    exchange.start()
    ocean_start(0)

    below_on = jnp.where(top, 1.0, 0.0)
    above_on = 1.0 - below_on
    blank = jnp.zeros((6, 128), F32)

    def pad(dst, index, k):
        h0 = halo[0, k : k + 1, :]
        h1 = halo[1, k : k + 1, :]
        dst[index, 0:8, :] = jnp.concatenate([blank, h1, h0], axis=0) * above_on
        dst[index, 136:144, :] = jnp.concatenate([h0, h1, blank], axis=0) * below_on

    lane = lax.broadcasted_iota(jnp.int32, (144, 128), 1)
    line = lax.broadcasted_iota(jnp.int32, (144, 128), 0)
    first_lane, last_lane = lane == 0, lane == 127
    keep = jnp.where(line < 8, above_on, jnp.where(line >= 136, below_on, 1.0))

    def pace_of(k):
        comp = jnp.minimum(first + k, KC - 1)
        way = lax.rem(comp, ND)
        pace = speed_ref[comp]
        return pace * dirs_ref[0, way], pace * dirs_ref[1, way]

    def propagate(k, _):
        pace_x, pace_y = pace_of(k)
        cx = cur[0] + pace_x
        cy = cur[1] + pace_y
        f = substep(G[k], cx, cy, first_lane, last_lane) * keep
        f = substep(f, cx, cy, first_lane, last_lane)
        H[k] = f[8:136]
        return 0

    def backward(t, _):
        chunk = (q16 - chunk_offset(15 - t)) & 15
        c = CT[:, pl.ds(pl.multiple_of(chunk * (S * 128), 128), S * 128)]
        T[...] = jnp.dot(FF[:RB], c, preferred_element_type=F32) + jnp.dot(FF[RB:], c, preferred_element_type=F32)
        where = map_ref[pl.ds(pl.multiple_of(grp * 128 + chunk * S, 8), S), :]
        row, col = where >> 7, where & 127
        taken = [jnp.zeros((S, 128), F32) for _ in range(SHARE - ONEHOT)]
        for r in range(128):
            hit = row == r
            for k in range(SHARE - ONEHOT):
                x = jnp.broadcast_to(H[ONEHOT + k, r : r + 1, :], (S, 128))
                y = jnp.take_along_axis(x, col, axis=1, mode="promise_in_bounds")
                taken[k] = jnp.where(hit, y, taken[k])
        for j in range(S):
            s = chunk * S + j
            for k in range(SHARE - ONEHOT):
                out[s, ONEHOT + k] = taken[k][j : j + 1]
            m = MF[:, pl.ds(pl.multiple_of(s * 128, 128), 128)]
            for k in range(ONEHOT):
                out[s, k] = jnp.sum(T[k * 64 : (k + 1) * 64, j * 128 : (j + 1) * 128] * m, axis=0, keepdims=True)

        def post(j, _):
            s = chunk * S + j

            @pl.when((s != dev) & owner)
            def _():
                pltpu.make_async_remote_copy(
                    src_ref=out.at[s],
                    dst_ref=ret.at[pl.ds(first, 11)],
                    send_sem=r_send,
                    recv_sem=r_recv,
                    device_id=(grp, s),
                    device_id_type=MESH,
                ).start()

            @pl.when((s != dev) & jnp.logical_not(owner))
            def _():
                pltpu.make_async_remote_copy(
                    src_ref=out.at[s, pl.ds(0, 10)],
                    dst_ref=ret.at[pl.ds(first, 10)],
                    send_sem=r_send,
                    recv_sem=r_recv,
                    device_id=(grp, s),
                    device_id_type=MESH,
                ).start()

            return 0

        lax.fori_loop(0, S, post, 0)
        return 0

    none = jnp.zeros((8, 128), F32)
    for k in range(SHARE):
        G[k, 0:8, :] = none
        G[k, 136:144, :] = none
    for q in range(2):
        cur[q, 0:8, :] = none
        cur[q, 136:144, :] = none

    lax.fori_loop(0, SHARE, propagate, 0)
    exchange.wait()
    for k in range(SHARE):
        pad(G, k, k)
    for q in range(2):
        pad(cur, q, SHARE + q)
    strip = pl.multiple_of(jnp.where(top, 112, 0), 8)
    strip_lane = lax.broadcasted_iota(jnp.int32, (32, 128), 1)
    strip_line = lax.broadcasted_iota(jnp.int32, (32, 128), 0) + strip
    strip_keep = jnp.where(strip_line < 8, above_on, jnp.where(strip_line >= 136, below_on, 1.0))
    strip_u, strip_v = cur[0, pl.ds(strip, 32), :], cur[1, pl.ds(strip, 32), :]
    for k in range(SHARE):
        pace_x, pace_y = pace_of(k)
        cx, cy = strip_u + pace_x, strip_v + pace_y
        f = substep(G[k, pl.ds(strip, 32), :], cx, cy, strip_lane == 0, strip_lane == 127) * strip_keep
        f = substep(f, cx, cy, strip_lane == 0, strip_lane == 127)
        H[k, pl.ds(pl.multiple_of(jnp.where(top, 120, 0), 8), 8), :] = jnp.where(top, f[16:24], f[8:16])
    for k in range(ONEHOT):
        for h in range(2):
            hi, lo = split(H[k, h * 64 : 64 + h * 64, :])
            FF[k * 64 : (k + 1) * 64, h * 128 : (h + 1) * 128] = hi
            FF[RB + k * 64 : RB + (k + 1) * 64, h * 128 : (h + 1) * 128] = lo
    lax.fori_loop(0, 5, backward, 0)

    drift = dacc[0:8] + dacc[8:16]
    wave_row = dev + lax.rem(lax.broadcasted_iota(jnp.int32, (8, 128), 0), 3) - 1
    drift = jnp.where(wave_row >= 64, drift[:, 128:], drift[:, :128])
    wide = jnp.dot(drift, spread_matrix(), precision=HIGH, preferred_element_type=F32)
    masks = couple_masks(cp_ref[...], dev)
    cells = []
    for q in range(2):
        sum_q = jnp.zeros((8, 256), F32)
        for dr in range(3):
            for delta in range(3):
                sum_q = sum_q + masks[dr][delta] * wide[q * 3 + dr : q * 3 + dr + 1, delta * 256 : (delta + 1) * 256]
        cells.append(sum_q)
    us, vs = cells

    oline = lax.broadcasted_iota(jnp.int32, (8, 256), 0)
    olane = lax.broadcasted_iota(jnp.int32, (8, 256), 1)
    coriolis = 0.5 + (linear * 8 + oline).astype(F32) / 2048.0
    fvs, fus = coriolis * vs, coriolis * us

    def ocean_step(slot, source, emit):
        def lap(a, z, q):
            above = jnp.where(has_up, ohalo[slot, 0, q, pl.ds(z, 1), :], 0.0)
            below = jnp.where(has_down, ohalo[slot, 1, q, pl.ds(z, 1), :], 0.0)
            r = jnp.where(olane == 255, 0.0, pltpu.roll(a, 255, 1)) + jnp.where(olane == 0, 0.0, pltpu.roll(a, 1, 1))
            r = r + jnp.where(oline == 0, above, pltpu.roll(a, 1, 0)) + jnp.where(oline == 7, below, pltpu.roll(a, 7, 0))
            return r - 4.0 * a

        def level(z, carry):
            pu, pv = carry
            u, v = source(0, z), source(1, z)
            zn = jnp.minimum(z + 1, NZ - 1)
            m0 = mix_ref[z]
            m1 = jnp.where(z == NZ - 1, 0.0, mix_ref[zn])
            nu, nv = source(0, zn), source(1, zn)
            p = prof_ref[z]
            wu = m1 * (nu - u) - m0 * (u - pu)
            wv = m1 * (nv - v) - m0 * (v - pv)
            emit(
                z,
                u + 0.2 * (0.2 * lap(u, z, 0) + wu + coriolis * v + p * fvs),
                v + 0.2 * (0.2 * lap(v, z, 1) + wv - coriolis * u - p * fus),
            )
            return u, v

        zero = jnp.zeros((8, 256), F32)
        lax.fori_loop(0, NZ, level, (zero, zero), unroll=8)

    def emit1(z, u, v):
        B[0, z] = u
        B[1, z] = v

    def emit2(z, u, v):
        ou_ref[z] = u
        ov_ref[z] = v

    ocean_wait(0)
    ocean_step(0, lambda q, z: (u_ref, v_ref)[q][z], emit1)
    stage_ocean(1, lambda z: B[0, z], lambda z: B[1, z])
    ocean_start(1)

    lax.fori_loop(5, 128 // S, backward, 0)
    for k in range(10):
        ret[first + k] = out[dev, k]

    @pl.when(owner)
    def _():
        ret[first + 10] = out[dev, 10]

    ocean_wait(1)
    ocean_step(1, lambda q, z: B[q, z], emit2)

    wait_for(pay1.at[pl.ds(0, 127)], a1_send)

    @pl.when(owner)
    def _():
        wait_for(pay2.at[pl.ds(0, 112), pl.ds(0, 7)], a2_send)
        wait_for(pay2.at[pl.ds(0, 15)], b_send)
        wait_for(out.at[pl.ds(0, 127)], r_send)
        wait_for(ret.at[pl.ds(0, KC - 11)], r_recv)

    @pl.when(jnp.logical_not(owner))
    def _():
        wait_for(pay2.at[pl.ds(0, 111), pl.ds(0, 7)], a2_send)
        wait_for(pay2.at[pl.ds(0, 16)], b_send)
        wait_for(out.at[pl.ds(0, 127), pl.ds(0, 10)], r_send)
        wait_for(ret.at[pl.ds(0, KC - 10)], r_recv)


def finish_kernel(r_ref, mask_ref, u_ref, v_ref, o_ref, ou_ref, ov_ref):
    ou_ref[...] = u_ref[...]
    ov_ref[...] = v_ref[...]
    o_ref[...] = r_ref[...] * mask_ref[...].astype(F32)


def body(spectra, sea_mask, card_map, dia_table, dia_coef, speed, stokes_weight, couple_point, ocean_u, ocean_v, mixing):
    sds = jax.ShapeDtypeStruct
    dirs = direction_table()
    trig = np.zeros((8, KP), np.float32)
    trig[:2, :KC] = np.tile(dirs, (1, KC // ND))
    profile = np.exp(-3.0 * (np.arange(NZ) + 0.5) / NZ).astype(np.float32)
    vmem = pl.BlockSpec(memory_space=pltpu.VMEM)
    smem = pl.BlockSpec(memory_space=pltpu.SMEM)
    dma = pltpu.SemaphoreType.DMA
    scratch = [
        pltpu.VMEM((KP, 256), BF16),
        pltpu.VMEM((KP, 256), BF16),
        pltpu.VMEM((KP, 256), BF16),
        pltpu.VMEM((4 * CH, KP), BF16),
        pltpu.VMEM((KP, 128), F32),
        pltpu.VMEM((8, KP), jnp.int32),
        pltpu.VMEM((KP, 8), F32),
        pltpu.VMEM((128, HEAD, 1, 128), F32),
        pltpu.VMEM((128, 8, 1, 128), F32),
        pltpu.VMEM((128, HEAD, 1, 128), F32),
        pltpu.VMEM((128, 8, 1, 128), F32),
        pltpu.VMEM((128, SHARE, 1, 128), F32),
        pltpu.VMEM((256, 16384), BF16),
        pltpu.VMEM((64, 16384), BF16),
        pltpu.VMEM((64, 16384), F32),
        pltpu.VMEM((128 * HEAD, S * 128), BF16),
        pltpu.VMEM((2 * RB, 256), BF16),
        pltpu.VMEM((R, 256), F32),
        pltpu.VMEM((16, 256), F32),
        pltpu.VMEM((RB, S * 128), F32),
        pltpu.VMEM((SHARE, 144, 128), F32),
        pltpu.VMEM((SHARE, 128, 128), F32),
        pltpu.VMEM((2, 144, 128), F32),
        pltpu.VMEM((2, 16, 128), F32),
        pltpu.VMEM((2, 16, 128), F32),
        pltpu.VMEM((3, 8, 128), F32),
        pltpu.VMEM((2, 8, 128), F32),
        pltpu.VMEM((2, 2, 2, NZ, 256), F32),
        pltpu.VMEM((2, 2, 2, NZ, 256), F32),
        pltpu.VMEM((2, NZ, 8, 256), F32),
        dma((2, 2)), dma((2, 2)), dma((2,)), dma((2,)),
        dma, dma((16,)), dma, dma((16,)), dma, dma, dma, dma, dma,
    ]
    ret, new_u, new_v = pl.pallas_call(
        step_kernel,
        out_shape=(sds((KC, 1, 128), F32), sds((NZ, 8, 256), F32), sds((NZ, 8, 256), F32)),
        in_specs=[vmem] * 7 + [smem] * 2 + [vmem] * 3 + [smem] * 2,
        out_specs=(vmem,) * 3,
        scratch_shapes=scratch,
        compiler_params=pltpu.CompilerParams(
            vmem_limit_bytes=VMEM_LIMIT, collective_id=0, has_side_effects=True
        ),
        name="step",
    )(
        spectra, sea_mask.reshape(1, 128), dia_table, dia_coef, stokes_weight,
        jnp.asarray(trig), card_map.reshape(256, 128), speed, jnp.asarray(dirs), couple_point, ocean_u, ocean_v,
        mixing, jnp.asarray(profile),
    )
    return pl.pallas_call(
        finish_kernel,
        out_shape=(sds((KC, 128), F32), sds((NZ, 8, 256), F32), sds((NZ, 8, 256), F32)),
        in_specs=[vmem] * 4,
        out_specs=(vmem,) * 3,
        name="finish",
    )(ret.reshape(KC, 128), sea_mask.reshape(1, 128), new_u, new_v)


def solution(mesh):
    both = ("grp", "dev")
    in_specs = (P(None, both), P(both), P(), P(), P(), P(), P(), P(both, None), P(None, both, None), P(None, both, None), P())
    out_specs = (P(None, both), P(None, both, None), P(None, both, None))
    return jax.shard_map(body, mesh=mesh, in_specs=in_specs, out_specs=out_specs, check_vma=False)
```

```python
import jax
import jax.numpy as jnp
import numpy as np
from jax import lax
from jax.experimental import pallas as pl
from jax.experimental.pallas import tpu as pltpu
from jax.sharding import PartitionSpec as P

ND = 36
NZ = 40
KC = 1296
KP = 1408
SHARE = 11
F32, BF16 = jnp.float32, jnp.bfloat16
NT = (((1,), (1,)), ((), ()))
HIGH = lax.Precision.HIGHEST
MESH = pl.DeviceIdType.MESH
VMEM_LIMIT = 56 << 20


def direction_table():
    theta = (np.arange(ND) + 0.5) * (2.0 * np.pi / ND)
    return np.stack([np.cos(theta), np.sin(theta)]).astype(np.float32)


def split(x):
    hi = x.astype(BF16)
    return hi, (x - hi.astype(F32)).astype(BF16)


def spread_matrix():
    wide = lax.broadcasted_iota(jnp.int32, (128, 768), 1)
    target = ((wide & 255) >> 1) + (wide >> 8) - 1
    return jnp.where(lax.broadcasted_iota(jnp.int32, (128, 768), 0) == target, 1.0, 0.0)


def couple_masks(cp, dev):
    row = (cp >> 7) - dev
    col = (cp & 127) - (lax.broadcasted_iota(jnp.int32, (8, 256), 1) >> 1)
    valid = cp >= 0
    return [
        [jnp.where(valid & (row == dr - 1) & (col == delta - 1), 1.0, 0.0) for delta in range(3)]
        for dr in range(3)
    ]


def build_maps(map_ref, base, CT, M, MF):
    def step(s, _):
        row = map_ref[pl.ds(base + s, 1), :]
        n = ((row >> 13) << 7) | (row & 127)
        rl = (row >> 7) & 63
        col = pl.ds(pl.multiple_of(s * 128, 128), 128)
        CT[:, col] = jnp.where(lax.broadcasted_iota(jnp.int32, (256, 128), 0) == n, 1.0, 0.0).astype(BF16)
        mf = jnp.where(lax.broadcasted_iota(jnp.int32, (64, 128), 0) == rl, 1.0, 0.0)
        MF[:, col] = mf
        M[:, col] = mf.astype(BF16)
        return 0

    lax.fori_loop(0, 128, step, 0)


def substep(f, cx, cy, first_lane, last_lane):
    ox = jnp.maximum(cx, 0.0) * f
    ix = jnp.minimum(cx, 0.0) * f
    oy = jnp.maximum(cy, 0.0) * f
    iy = jnp.minimum(cy, 0.0) * f
    rows = f.shape[0]
    nx = jnp.where(last_lane, 0.0, pltpu.roll(ix, 127, 1))
    px = jnp.where(first_lane, 0.0, pltpu.roll(ox, 1, 1))
    ny = pltpu.roll(iy, rows - 1, 0)
    py = pltpu.roll(oy, 1, 0)
    return f - (ox - ix + nx - px) - (oy - iy + ny - py)


S = 8
HEAD, TAIL = 7, 4
R = SHARE * 64
ONEHOT = 8
RB = ONEHOT * 64
CH = 432


def chunk_offset(i):
    return jnp.where((i & 1) == 1, (i + 1) >> 1, 16 - (i >> 1))


def start_of(dev):
    return dev * 10 + ((dev + 7) >> 3)


def wait_for(ref, sem):
    pltpu.make_async_copy(ref, ref, sem).wait()


def step_kernel(
    e_ref, mask_ref, table_ref, coef_ref, stokes_ref, trig_ref, map_ref, speed_ref, dirs_ref, cp_ref, u_ref, v_ref,
    mix_ref, prof_ref,
    ret, ou_ref, ov_ref,
    E, F1, F2, OH, forced_ref, trow_ref, col_ref, pay1, pay2, arr1, arr2, out, CT, M, MF, LH, FF, acc, dacc, T,
    G, H, cur, edge, halo, part, pin, ostage, ohalo, B,
    o_send, o_recv, p_send, p_recv, a1_send, a1_recv, a2_send, a2_recv, b_send,
    h_send, h_recv, r_send, r_recv,
):
    grp = lax.axis_index("grp")
    dev = lax.axis_index("dev")
    q16 = dev >> 3
    owner = (dev & 7) == 0
    first = start_of(dev)
    linear = grp * 128 + dev
    has_up = linear > 0
    has_down = linear < 255
    up = linear + 255
    up_id = ((up // 128) % 2, up % 128)
    down = linear + 1
    down_id = ((down // 128) % 2, down % 128)

    barrier = pltpu.get_barrier_semaphore()

    def greet(i, _):
        pl.semaphore_signal(barrier, inc=1, device_id=(grp, (dev + i) & 127), device_id_type=MESH)
        return 0

    lax.fori_loop(1, 128, greet, 0)
    pl.semaphore_signal(barrier, inc=1, device_id=(1 - grp, dev), device_id_type=MESH)
    crosses_down = (grp == 0) & (dev == 127)
    crosses_up = (grp == 1) & (dev == 0)

    @pl.when(crosses_down)
    def _():
        pl.semaphore_signal(barrier, inc=1, device_id=down_id, device_id_type=MESH)

    @pl.when(crosses_up)
    def _():
        pl.semaphore_signal(barrier, inc=1, device_id=up_id, device_id_type=MESH)

    masks = couple_masks(cp_ref[...], dev)
    surface = [u_ref[0], v_ref[0]]
    rows = []
    for dr in range(3):
        for q in range(3):
            pieces = []
            for delta in range(3):
                m = masks[dr][delta]
                pieces.append(jnp.sum(m if q == 2 else m * surface[q], axis=0, keepdims=True))
            rows.append(jnp.concatenate(pieces, axis=1))
        rows.append(jnp.zeros((5, 768), F32))
    sums = lax.dot_general(
        jnp.concatenate(rows, axis=0), spread_matrix(), NT, precision=HIGH, preferred_element_type=F32
    )
    for dr in range(3):
        part[dr] = sums[dr * 8 : (dr + 1) * 8]

    trow_ref[...] = jnp.full((8, KP), -1, jnp.int32)
    trow_ref[0:4, :KC] = table_ref[...]
    OH_rows = trow_ref[...].astype(F32)
    line8 = lax.broadcasted_iota(jnp.int32, (8, KP), 0)
    wide_coef = jnp.concatenate([coef_ref[...].reshape(1, KC), jnp.zeros((1, KP - KC), F32)], axis=1)
    col_ref[...] = jnp.transpose(jnp.where(line8 < 4, OH_rows, wide_coef))
    tail = jnp.zeros((KP - KC, 256), BF16)
    E[KC:, :] = tail
    F1[KC:, :] = tail
    F2[KC:, :] = tail
    hi, lo = split(e_ref[...])
    E[:KC, :128] = hi
    E[:KC, 128:] = lo

    def gather(i, _):
        rows = pl.ds(pl.multiple_of(i * CH, 16), CH)
        lanes = lax.broadcasted_iota(jnp.int32, (CH, KP), 1).astype(F32)
        e = e_ref[rows, :]
        cols = col_ref[rows, :]
        for m in range(4):
            OH[m * CH : (m + 1) * CH, :] = jnp.where(lanes == cols[:, m : m + 1], 1.0, 0.0).astype(BF16)
        p = jnp.dot(OH[...], E[...], preferred_element_type=F32)
        p = p[:, :128] + p[:, 128:]
        g = [p[m * CH : (m + 1) * CH] for m in range(4)]
        s = cols[:, 4:5]
        ee = e * e
        e2 = 2.0 * e
        a = s * (ee * (g[0] + g[1]) - e2 * g[0] * g[1])
        b = s * (ee * (g[2] + g[3]) - e2 * g[2] * g[3])
        forced_ref[rows, :] = e - (a + b)
        ah, al = split(a)
        bh, bl = split(b)
        F1[rows, :128] = ah
        F1[rows, 128:] = al
        F2[rows, :128] = bh
        F2[rows, 128:] = bl
        return 0

    lax.fori_loop(0, KC // CH, gather, 0)

    mask = mask_ref[...].astype(F32)

    def scatter(i, _):
        rows = pl.ds(pl.multiple_of(i * CH, 16), CH)
        b = lax.broadcasted_iota(jnp.int32, (CH, KP), 0) + i * CH

        def onehot(m):
            return jnp.where(b == trow_ref[m : m + 1, :], 1.0, 0.0)

        p = jnp.dot((onehot(0) + onehot(1)).astype(BF16), F1[...], preferred_element_type=F32)
        p = p + jnp.dot((onehot(2) + onehot(3)).astype(BF16), F2[...], preferred_element_type=F32)
        forced_ref[rows, :] = mask * (forced_ref[rows, :] + 0.5 * (p[:, :128] + p[:, 128:]))
        return 0

    lax.fori_loop(0, KC // CH, scatter, 0)

    def destination(n):
        return (((q16 - chunk_offset(n >> 3)) & 15) << 3) | ((dev + n) & 7)

    def fill1(t, _):
        for r in range(4):
            d = t * 4 + r
            base = start_of(d)
            for k in range(HEAD):
                pay1[d, k] = forced_ref[pl.ds(base + k, 1), :]
        return 0

    lax.fori_loop(0, 32, fill1, 0)

    pl.semaphore_wait(barrier, 128 + jnp.where(crosses_down | crosses_up, 1, 0))

    def ocean_copy(slot, side):
        return pltpu.make_async_remote_copy(
            src_ref=ostage.at[slot, side],
            dst_ref=ohalo.at[slot, 1 - side],
            send_sem=o_send.at[slot, side],
            recv_sem=o_recv.at[slot, 1 - side],
            device_id=up_id if side == 0 else down_id,
            device_id_type=MESH,
        )

    def ocean_start(slot):
        for side, there in ((0, has_up), (1, has_down)):
            @pl.when(there)
            def _(side=side):
                ocean_copy(slot, side).start()

    def ocean_wait(slot):
        for side, there in ((0, has_up), (1, has_down)):
            @pl.when(there)
            def _(side=side):
                wait_for(ostage.at[slot, side], o_send.at[slot, side])
                wait_for(ohalo.at[slot, side], o_recv.at[slot, side])

    def part_copy(side):
        return pltpu.make_async_remote_copy(
            src_ref=part.at[2 * side],
            dst_ref=pin.at[1 - side],
            send_sem=p_send.at[side],
            recv_sem=p_recv.at[1 - side],
            device_id=(grp, (dev + 127 + 2 * side) & 127),
            device_id_type=MESH,
        )

    for side, there in ((0, dev > 0), (1, dev < 127)):
        @pl.when(there)
        def _(side=side):
            part_copy(side).start()

    pltpu.make_async_copy(pay1.at[dev], arr1.at[dev], a1_recv.at[q16]).start()

    def send1(n, _):
        dest = destination(n)
        pltpu.make_async_remote_copy(
            src_ref=pay1.at[dest],
            dst_ref=arr1.at[dev],
            send_sem=a1_send,
            recv_sem=a1_recv.at[q16],
            device_id=(grp, dest),
            device_id_type=MESH,
        ).start()
        return 0

    lax.fori_loop(1, 128, send1, 0)

    def stage_ocean(slot, a, b):
        def level(z, _):
            for side, line in ((0, 0), (1, 7)):
                ostage[slot, side, 0, pl.ds(z, 1), :] = a(z)[line : line + 1]
                ostage[slot, side, 1, pl.ds(z, 1), :] = b(z)[line : line + 1]
            return 0

        lax.fori_loop(0, NZ, level, 0, unroll=8)

    stage_ocean(0, lambda z: u_ref[z], lambda z: v_ref[z])
    forced_ref[KC:, :] = jnp.zeros((KP - KC, 128), F32)
    weights = trig_ref[...] * jnp.concatenate([stokes_ref[...].reshape(1, KC), jnp.zeros((1, KP - KC), F32)], axis=1)
    drift_own = jnp.dot(weights, forced_ref[...], precision=HIGH, preferred_element_type=F32)

    def fill2(t, _):
        for r in range(4):
            d = t * 4 + r
            base = start_of(d)
            for k in range(3):
                pay2[d, k] = forced_ref[pl.ds(base + HEAD + k, 1), :]
            for q in range(2):
                pay2[d, 3 + q] = drift_own[q : q + 1]
            pay2[d, 7] = forced_ref[pl.ds(base + 10, 1), :]
        return 0

    lax.fori_loop(0, 32, fill2, 0)

    build_maps(map_ref, grp * 128, CT, M, MF)

    for side, there in ((0, dev > 0), (1, dev < 127)):
        @pl.when(there)
        def _(side=side):
            wait_for(part.at[2 * side], p_send.at[side])
            wait_for(pin.at[side], p_recv.at[side])

    total = part[1] + jnp.where(dev > 0, pin[0], 0.0) + jnp.where(dev < 127, pin[1], 0.0)
    speeds = 0.3 * total[0:2] / (total[2:3] + 1.0)

    def fill_currents(t, _):
        for r in range(8):
            for q in range(2):
                pay2[t * 8 + r, 5 + q] = speeds[q : q + 1]
        return 0

    lax.fori_loop(0, 16, fill_currents, 0)

    @pl.when(owner)
    def _():
        pltpu.make_async_copy(pay2.at[dev], arr2.at[dev], a2_recv.at[q16]).start()

    @pl.when(jnp.logical_not(owner))
    def _():
        pltpu.make_async_copy(pay2.at[dev, pl.ds(0, 7)], arr2.at[dev, pl.ds(0, 7)], a2_recv.at[q16]).start()

    def send2(n, _):
        dest = destination(n)

        @pl.when((dest & 7) == 0)
        def _():
            pltpu.make_async_remote_copy(
                src_ref=pay2.at[dest],
                dst_ref=arr2.at[dev],
                send_sem=b_send,
                recv_sem=a2_recv.at[q16],
                device_id=(grp, dest),
                device_id_type=MESH,
            ).start()

        @pl.when((dest & 7) != 0)
        def _():
            pltpu.make_async_remote_copy(
                src_ref=pay2.at[dest, pl.ds(0, 7)],
                dst_ref=arr2.at[dev, pl.ds(0, 7)],
                send_sem=a2_send,
                recv_sem=a2_recv.at[q16],
                device_id=(grp, dest),
                device_id_type=MESH,
            ).start()

        return 0

    lax.fori_loop(1, 128, send2, 0)
    ocean_start(0)
    zero_row = jnp.zeros((1, 128), F32)
    top = grp == 0

    acc[...] = jnp.zeros_like(acc)
    dacc[...] = jnp.zeros_like(dacc)

    def forward(low, count, last):
        n = count * 64

        def chunk_step(i, _):
            chunk = (q16 + chunk_offset(i)) & 15
            if last:
                @pl.when(owner)
                def _():
                    wait_for(arr2.at[pl.ds(chunk * S, S)], a2_recv.at[chunk])

                @pl.when(jnp.logical_not(owner))
                def _():
                    wait_for(arr2.at[pl.ds(chunk * S, S), pl.ds(0, 7)], a2_recv.at[chunk])
            else:
                wait_for(arr1.at[pl.ds(chunk * S, S)], a1_recv.at[chunk])

            for j in range(S):
                s = chunk * S + j
                cols = pl.ds(pl.multiple_of(s * 128, 128), 128)
                c = slice(j * 128, (j + 1) * 128)
                for k in range(count):
                    x = (arr2[s, 7 if k == 3 else k]) if last else arr1[s, k]
                    hi, lo = split(jnp.broadcast_to(x, (16, 128)))
                    for q in range(4):
                        m = M[q * 16 : (q + 1) * 16, cols]
                        r = k * 64 + q * 16
                        LH[r : r + 16, c] = m * hi
                        LH[n + r : n + r + 16, c] = m * lo
                if last:
                    row = map_ref[pl.ds(grp * 128 + s, 1), :] >> 7
                    pieces = []
                    for q in range(2):
                        cur[q, pl.ds(8 + s, 1), :] = arr2[s, 5 + q]
                        x = arr2[s, 3 + q]
                        for dr in range(3):
                            pieces.append(jnp.where(row == dev + (dr - 1), x, zero_row))
                    pieces += [zero_row, zero_row]
                    piece = jnp.concatenate(pieces, axis=0)
                    hi = piece.astype(BF16).astype(F32)
                    LH[2 * n : 2 * n + 16, c] = jnp.concatenate([hi, piece - hi], axis=0).astype(BF16)
            c = CT[:, pl.ds(pl.multiple_of(chunk * (S * 128), 128), S * 128)]
            d = lax.dot_general(LH[: 2 * n + (16 if last else 0)], c, NT, preferred_element_type=F32)
            acc[low : low + n] += d[:n] + d[n : 2 * n]
            if last:
                dacc[...] += d[2 * n :]
            return 0

        lax.fori_loop(0, 128 // S, chunk_step, 0)

    oline = lax.broadcasted_iota(jnp.int32, (8, 256), 0)
    olane = lax.broadcasted_iota(jnp.int32, (8, 256), 1)
    coriolis = 0.5 + (linear * 8 + oline).astype(F32) / 2048.0

    def ocean_step(slot, source, emit, drift):
        def lap(a, z, q):
            above = jnp.where(has_up, ohalo[slot, 0, q, pl.ds(z, 1), :], 0.0)
            below = jnp.where(has_down, ohalo[slot, 1, q, pl.ds(z, 1), :], 0.0)
            r = jnp.where(olane == 255, 0.0, pltpu.roll(a, 255, 1)) + jnp.where(olane == 0, 0.0, pltpu.roll(a, 1, 1))
            r = r + jnp.where(oline == 0, above, pltpu.roll(a, 1, 0)) + jnp.where(oline == 7, below, pltpu.roll(a, 7, 0))
            return r - 4.0 * a

        def level(z, carry):
            pu, pv = carry
            u, v = source(0, z), source(1, z)
            zn = jnp.minimum(z + 1, NZ - 1)
            m0 = mix_ref[z]
            m1 = jnp.where(z == NZ - 1, 0.0, mix_ref[zn])
            nu, nv = source(0, zn), source(1, zn)
            p = prof_ref[z]
            wu = m1 * (nu - u) - m0 * (u - pu)
            wv = m1 * (nv - v) - m0 * (v - pv)
            emit(
                z,
                u + 0.2 * (0.2 * lap(u, z, 0) + wu + coriolis * v + (p * drift[0] if drift else 0.0)),
                v + 0.2 * (0.2 * lap(v, z, 1) + wv - coriolis * u + (p * drift[1] if drift else 0.0)),
            )
            return u, v

        zero = jnp.zeros((8, 256), F32)
        lax.fori_loop(0, NZ, level, (zero, zero), unroll=8)

    def emit1(z, u, v):
        B[0, z] = u
        B[1, z] = v

    def emit2(z, u, v):
        ou_ref[z] = u
        ov_ref[z] = v

    forward(0, HEAD, False)
    ocean_wait(0)
    ocean_step(0, lambda q, z: (u_ref, v_ref)[q][z], emit1, None)
    forward(HEAD * 64, TAIL, True)

    for k in range(SHARE):
        low = acc[k * 64 : (k + 1) * 64, 0:128]
        high = acc[k * 64 : (k + 1) * 64, 128:256]
        G[k, 8:72, :] = low
        G[k, 72:136, :] = high
        edge[0, k : k + 1, :] = jnp.where(top, high[63:64], low[0:1])
        edge[1, k : k + 1, :] = jnp.where(top, high[62:63], low[1:2])
    for r in range(2):
        for q in range(2):
            edge[r, SHARE + q : SHARE + q + 1, :] = jnp.where(
                top, cur[q, 135 - r : 136 - r, :], cur[q, 8 + r : 9 + r, :]
            )
        edge[r, 13:16, :] = jnp.zeros((3, 128), F32)
    exchange = pltpu.make_async_remote_copy(
        src_ref=edge, dst_ref=halo, send_sem=h_send, recv_sem=h_recv, device_id=(1 - grp, dev), device_id_type=MESH
    )
    exchange.start()

    drift = dacc[0:8] + dacc[8:16]
    wave_row = dev + lax.rem(lax.broadcasted_iota(jnp.int32, (8, 128), 0), 3) - 1
    drift = jnp.where(wave_row >= 64, drift[:, 128:], drift[:, :128])
    wide = jnp.dot(drift, spread_matrix(), precision=HIGH, preferred_element_type=F32)
    masks = couple_masks(cp_ref[...], dev)
    cells = []
    for q in range(2):
        sum_q = jnp.zeros((8, 256), F32)
        for dr in range(3):
            for delta in range(3):
                sum_q = sum_q + masks[dr][delta] * wide[q * 3 + dr : q * 3 + dr + 1, delta * 256 : (delta + 1) * 256]
        cells.append(sum_q)
    us, vs = cells

    drift_terms = (coriolis * vs, -coriolis * us)

    def add_drift(z, _):
        p = 0.2 * prof_ref[z]
        for q in range(2):
            b = B[q, z] + p * drift_terms[q]
            B[q, z] = b
            for side, line in ((0, 0), (1, 7)):
                ostage[1, side, q, pl.ds(z, 1), :] = b[line : line + 1]
        return 0

    lax.fori_loop(0, NZ, add_drift, 0, unroll=8)
    ocean_start(1)

    below_on = jnp.where(top, 1.0, 0.0)
    above_on = 1.0 - below_on
    blank = jnp.zeros((6, 128), F32)

    def pad(dst, index, k):
        h0 = halo[0, k : k + 1, :]
        h1 = halo[1, k : k + 1, :]
        dst[index, 0:8, :] = jnp.concatenate([blank, h1, h0], axis=0) * above_on
        dst[index, 136:144, :] = jnp.concatenate([h0, h1, blank], axis=0) * below_on

    lane = lax.broadcasted_iota(jnp.int32, (144, 128), 1)
    line = lax.broadcasted_iota(jnp.int32, (144, 128), 0)
    first_lane, last_lane = lane == 0, lane == 127
    keep = jnp.where(line < 8, above_on, jnp.where(line >= 136, below_on, 1.0))

    def pace_of(k):
        comp = jnp.minimum(first + k, KC - 1)
        way = lax.rem(comp, ND)
        pace = speed_ref[comp]
        return pace * dirs_ref[0, way], pace * dirs_ref[1, way]

    def propagate(k, _):
        pace_x, pace_y = pace_of(k)
        cx = cur[0] + pace_x
        cy = cur[1] + pace_y
        f = substep(G[k], cx, cy, first_lane, last_lane) * keep
        f = substep(f, cx, cy, first_lane, last_lane)
        H[k] = f[8:136]
        return 0

    def backward(t, _):
        chunk = (q16 - chunk_offset(15 - t)) & 15
        c = CT[:, pl.ds(pl.multiple_of(chunk * (S * 128), 128), S * 128)]
        T[...] = jnp.dot(FF[:RB], c, preferred_element_type=F32) + jnp.dot(FF[RB:], c, preferred_element_type=F32)
        where = map_ref[pl.ds(pl.multiple_of(grp * 128 + chunk * S, 8), S), :]
        row, col = where >> 7, where & 127
        taken = [jnp.zeros((S, 128), F32) for _ in range(SHARE - ONEHOT)]
        for r in range(128):
            hit = row == r
            for k in range(SHARE - ONEHOT):
                x = jnp.broadcast_to(H[ONEHOT + k, r : r + 1, :], (S, 128))
                y = jnp.take_along_axis(x, col, axis=1, mode="promise_in_bounds")
                taken[k] = jnp.where(hit, y, taken[k])
        for j in range(S):
            s = chunk * S + j
            for k in range(SHARE - ONEHOT):
                out[s, ONEHOT + k] = taken[k][j : j + 1]
            m = MF[:, pl.ds(pl.multiple_of(s * 128, 128), 128)]
            for k in range(ONEHOT):
                out[s, k] = jnp.sum(T[k * 64 : (k + 1) * 64, j * 128 : (j + 1) * 128] * m, axis=0, keepdims=True)

        def post(j, _):
            s = chunk * S + j

            @pl.when((s != dev) & owner)
            def _():
                pltpu.make_async_remote_copy(
                    src_ref=out.at[s],
                    dst_ref=ret.at[pl.ds(first, 11)],
                    send_sem=r_send,
                    recv_sem=r_recv,
                    device_id=(grp, s),
                    device_id_type=MESH,
                ).start()

            @pl.when((s != dev) & jnp.logical_not(owner))
            def _():
                pltpu.make_async_remote_copy(
                    src_ref=out.at[s, pl.ds(0, 10)],
                    dst_ref=ret.at[pl.ds(first, 10)],
                    send_sem=r_send,
                    recv_sem=r_recv,
                    device_id=(grp, s),
                    device_id_type=MESH,
                ).start()

            return 0

        lax.fori_loop(0, S, post, 0)
        return 0

    none = jnp.zeros((8, 128), F32)
    for k in range(SHARE):
        G[k, 0:8, :] = none
        G[k, 136:144, :] = none
    for q in range(2):
        cur[q, 0:8, :] = none
        cur[q, 136:144, :] = none

    lax.fori_loop(0, SHARE, propagate, 0)
    exchange.wait()
    for k in range(SHARE):
        pad(G, k, k)
    for q in range(2):
        pad(cur, q, SHARE + q)
    strip = pl.multiple_of(jnp.where(top, 112, 0), 8)
    strip_lane = lax.broadcasted_iota(jnp.int32, (32, 128), 1)
    strip_line = lax.broadcasted_iota(jnp.int32, (32, 128), 0) + strip
    strip_keep = jnp.where(strip_line < 8, above_on, jnp.where(strip_line >= 136, below_on, 1.0))
    strip_u, strip_v = cur[0, pl.ds(strip, 32), :], cur[1, pl.ds(strip, 32), :]
    for k in range(SHARE):
        pace_x, pace_y = pace_of(k)
        cx, cy = strip_u + pace_x, strip_v + pace_y
        f = substep(G[k, pl.ds(strip, 32), :], cx, cy, strip_lane == 0, strip_lane == 127) * strip_keep
        f = substep(f, cx, cy, strip_lane == 0, strip_lane == 127)
        H[k, pl.ds(pl.multiple_of(jnp.where(top, 120, 0), 8), 8), :] = jnp.where(top, f[16:24], f[8:16])
    for k in range(ONEHOT):
        for h in range(2):
            hi, lo = split(H[k, h * 64 : 64 + h * 64, :])
            FF[k * 64 : (k + 1) * 64, h * 128 : (h + 1) * 128] = hi
            FF[RB + k * 64 : RB + (k + 1) * 64, h * 128 : (h + 1) * 128] = lo
    lax.fori_loop(0, 128 // S, backward, 0)
    for k in range(10):
        ret[first + k] = out[dev, k]

    @pl.when(owner)
    def _():
        ret[first + 10] = out[dev, 10]

    ocean_wait(1)
    ocean_step(1, lambda q, z: B[q, z], emit2, drift_terms)

    wait_for(pay1.at[pl.ds(0, 127)], a1_send)

    @pl.when(owner)
    def _():
        wait_for(pay2.at[pl.ds(0, 112), pl.ds(0, 7)], a2_send)
        wait_for(pay2.at[pl.ds(0, 15)], b_send)
        wait_for(out.at[pl.ds(0, 127)], r_send)
        wait_for(ret.at[pl.ds(0, KC - 11)], r_recv)

    @pl.when(jnp.logical_not(owner))
    def _():
        wait_for(pay2.at[pl.ds(0, 111), pl.ds(0, 7)], a2_send)
        wait_for(pay2.at[pl.ds(0, 16)], b_send)
        wait_for(out.at[pl.ds(0, 127), pl.ds(0, 10)], r_send)
        wait_for(ret.at[pl.ds(0, KC - 10)], r_recv)


def finish_kernel(r_ref, mask_ref, u_ref, v_ref, o_ref, ou_ref, ov_ref):
    ou_ref[...] = u_ref[...]
    ov_ref[...] = v_ref[...]
    o_ref[...] = r_ref[...] * mask_ref[...].astype(F32)


def body(spectra, sea_mask, card_map, dia_table, dia_coef, speed, stokes_weight, couple_point, ocean_u, ocean_v, mixing):
    sds = jax.ShapeDtypeStruct
    dirs = direction_table()
    trig = np.zeros((8, KP), np.float32)
    trig[:2, :KC] = np.tile(dirs, (1, KC // ND))
    profile = np.exp(-3.0 * (np.arange(NZ) + 0.5) / NZ).astype(np.float32)
    vmem = pl.BlockSpec(memory_space=pltpu.VMEM)
    smem = pl.BlockSpec(memory_space=pltpu.SMEM)
    dma = pltpu.SemaphoreType.DMA
    scratch = [
        pltpu.VMEM((KP, 256), BF16),
        pltpu.VMEM((KP, 256), BF16),
        pltpu.VMEM((KP, 256), BF16),
        pltpu.VMEM((4 * CH, KP), BF16),
        pltpu.VMEM((KP, 128), F32),
        pltpu.VMEM((8, KP), jnp.int32),
        pltpu.VMEM((KP, 8), F32),
        pltpu.VMEM((128, HEAD, 1, 128), F32),
        pltpu.VMEM((128, 8, 1, 128), F32),
        pltpu.VMEM((128, HEAD, 1, 128), F32),
        pltpu.VMEM((128, 8, 1, 128), F32),
        pltpu.VMEM((128, SHARE, 1, 128), F32),
        pltpu.VMEM((256, 16384), BF16),
        pltpu.VMEM((64, 16384), BF16),
        pltpu.VMEM((64, 16384), F32),
        pltpu.VMEM((128 * HEAD, S * 128), BF16),
        pltpu.VMEM((2 * RB, 256), BF16),
        pltpu.VMEM((R, 256), F32),
        pltpu.VMEM((16, 256), F32),
        pltpu.VMEM((RB, S * 128), F32),
        pltpu.VMEM((SHARE, 144, 128), F32),
        pltpu.VMEM((SHARE, 128, 128), F32),
        pltpu.VMEM((2, 144, 128), F32),
        pltpu.VMEM((2, 16, 128), F32),
        pltpu.VMEM((2, 16, 128), F32),
        pltpu.VMEM((3, 8, 128), F32),
        pltpu.VMEM((2, 8, 128), F32),
        pltpu.VMEM((2, 2, 2, NZ, 256), F32),
        pltpu.VMEM((2, 2, 2, NZ, 256), F32),
        pltpu.VMEM((2, NZ, 8, 256), F32),
        dma((2, 2)), dma((2, 2)), dma((2,)), dma((2,)),
        dma, dma((16,)), dma, dma((16,)), dma, dma, dma, dma, dma,
    ]
    ret, new_u, new_v = pl.pallas_call(
        step_kernel,
        out_shape=(sds((KC, 1, 128), F32), sds((NZ, 8, 256), F32), sds((NZ, 8, 256), F32)),
        in_specs=[vmem] * 7 + [smem] * 2 + [vmem] * 3 + [smem] * 2,
        out_specs=(vmem,) * 3,
        scratch_shapes=scratch,
        compiler_params=pltpu.CompilerParams(
            vmem_limit_bytes=VMEM_LIMIT, collective_id=0, has_side_effects=True
        ),
        name="step",
    )(
        spectra, sea_mask.reshape(1, 128), dia_table, dia_coef, stokes_weight,
        jnp.asarray(trig), card_map.reshape(256, 128), speed, jnp.asarray(dirs), couple_point, ocean_u, ocean_v,
        mixing, jnp.asarray(profile),
    )
    return pl.pallas_call(
        finish_kernel,
        out_shape=(sds((KC, 128), F32), sds((NZ, 8, 256), F32), sds((NZ, 8, 256), F32)),
        in_specs=[vmem] * 4,
        out_specs=(vmem,) * 3,
        name="finish",
    )(ret.reshape(KC, 128), sea_mask.reshape(1, 128), new_u, new_v)


def solution(mesh):
    both = ("grp", "dev")
    in_specs = (P(None, both), P(both), P(), P(), P(), P(), P(), P(both, None), P(None, both, None), P(None, both, None), P())
    out_specs = (P(None, both), P(None, both, None), P(None, both, None))
    return jax.shard_map(body, mesh=mesh, in_specs=in_specs, out_specs=out_specs, check_vma=False)
```

```python
import jax
import jax.numpy as jnp
import numpy as np
from jax import lax
from jax.experimental import pallas as pl
from jax.experimental.pallas import tpu as pltpu
from jax.sharding import PartitionSpec as P

ND = 36
NZ = 40
KC = 1296
KP = 1408
SHARE = 11
F32, BF16 = jnp.float32, jnp.bfloat16
NT = (((1,), (1,)), ((), ()))
HIGH = lax.Precision.HIGHEST
MESH = pl.DeviceIdType.MESH
VMEM_LIMIT = 56 << 20


def direction_table():
    theta = (np.arange(ND) + 0.5) * (2.0 * np.pi / ND)
    return np.stack([np.cos(theta), np.sin(theta)]).astype(np.float32)


def split(x):
    hi = x.astype(BF16)
    return hi, (x - hi.astype(F32)).astype(BF16)


def spread_matrix():
    wide = lax.broadcasted_iota(jnp.int32, (128, 768), 1)
    target = ((wide & 255) >> 1) + (wide >> 8) - 1
    return jnp.where(lax.broadcasted_iota(jnp.int32, (128, 768), 0) == target, 1.0, 0.0)


def couple_masks(cp, dev):
    row = (cp >> 7) - dev
    col = (cp & 127) - (lax.broadcasted_iota(jnp.int32, (8, 256), 1) >> 1)
    valid = cp >= 0
    return [
        [jnp.where(valid & (row == dr - 1) & (col == delta - 1), 1.0, 0.0) for delta in range(3)]
        for dr in range(3)
    ]


def build_maps(map_ref, base, CT, M, MF):
    def step(s, _):
        row = map_ref[pl.ds(base + s, 1), :]
        n = ((row >> 13) << 7) | (row & 127)
        rl = (row >> 7) & 63
        col = pl.ds(pl.multiple_of(s * 128, 128), 128)
        CT[:, col] = jnp.where(lax.broadcasted_iota(jnp.int32, (256, 128), 0) == n, 1.0, 0.0).astype(BF16)
        mf = jnp.where(lax.broadcasted_iota(jnp.int32, (64, 128), 0) == rl, 1.0, 0.0)
        MF[:, col] = mf
        M[:, col] = mf.astype(BF16)
        return 0

    lax.fori_loop(0, 128, step, 0)


def substep(f, cx, cy, first_lane, last_lane):
    ox = jnp.maximum(cx, 0.0) * f
    ix = jnp.minimum(cx, 0.0) * f
    oy = jnp.maximum(cy, 0.0) * f
    iy = jnp.minimum(cy, 0.0) * f
    rows = f.shape[0]
    nx = jnp.where(last_lane, 0.0, pltpu.roll(ix, 127, 1))
    px = jnp.where(first_lane, 0.0, pltpu.roll(ox, 1, 1))
    ny = pltpu.roll(iy, rows - 1, 0)
    py = pltpu.roll(oy, 1, 0)
    return f - (ox - ix + nx - px) - (oy - iy + ny - py)


S = 8
HEAD, TAIL = 7, 4
R = SHARE * 64
ONEHOT = 8
RB = ONEHOT * 64
CH = 432


def chunk_offset(i):
    return jnp.where((i & 1) == 1, (i + 1) >> 1, 16 - (i >> 1))


def start_of(dev):
    return dev * 10 + ((dev + 7) >> 3)


def wait_for(ref, sem):
    pltpu.make_async_copy(ref, ref, sem).wait()


def step_kernel(
    e_ref, mask_ref, table_ref, coef_ref, stokes_ref, trig_ref, map_ref, speed_ref, dirs_ref, cp_ref, u_ref, v_ref,
    mix_ref, prof_ref,
    ret, ou_ref, ov_ref,
    E, F1, F2, OH, forced_ref, trow_ref, col_ref, pay1, pay2, arr1, arr2, out, CT, M, MF, LH, FF, acc, dacc, T,
    G, H, cur, edge, halo, part, pin, ostage, ohalo, B,
    o_send, o_recv, p_send, p_recv, a1_send, a1_recv, a2_send, a2_recv, b_send,
    h_send, h_recv, r_send, r_recv,
):
    grp = lax.axis_index("grp")
    dev = lax.axis_index("dev")
    q16 = dev >> 3
    owner = (dev & 7) == 0
    first = start_of(dev)
    linear = grp * 128 + dev
    has_up = linear > 0
    has_down = linear < 255
    up = linear + 255
    up_id = ((up // 128) % 2, up % 128)
    down = linear + 1
    down_id = ((down // 128) % 2, down % 128)

    barrier = pltpu.get_barrier_semaphore()

    def greet(i, _):
        pl.semaphore_signal(barrier, inc=1, device_id=(grp, (dev + i) & 127), device_id_type=MESH)
        return 0

    lax.fori_loop(1, 128, greet, 0)
    pl.semaphore_signal(barrier, inc=1, device_id=(1 - grp, dev), device_id_type=MESH)
    crosses_down = (grp == 0) & (dev == 127)
    crosses_up = (grp == 1) & (dev == 0)

    @pl.when(crosses_down)
    def _():
        pl.semaphore_signal(barrier, inc=1, device_id=down_id, device_id_type=MESH)

    @pl.when(crosses_up)
    def _():
        pl.semaphore_signal(barrier, inc=1, device_id=up_id, device_id_type=MESH)

    masks = couple_masks(cp_ref[...], dev)
    surface = [u_ref[0], v_ref[0]]
    rows = []
    for dr in range(3):
        for q in range(3):
            pieces = []
            for delta in range(3):
                m = masks[dr][delta]
                pieces.append(jnp.sum(m if q == 2 else m * surface[q], axis=0, keepdims=True))
            rows.append(jnp.concatenate(pieces, axis=1))
        rows.append(jnp.zeros((5, 768), F32))
    sums = lax.dot_general(
        jnp.concatenate(rows, axis=0), spread_matrix(), NT, precision=HIGH, preferred_element_type=F32
    )
    for dr in range(3):
        part[dr] = sums[dr * 8 : (dr + 1) * 8]

    trow_ref[...] = jnp.full((8, KP), -1, jnp.int32)
    trow_ref[0:4, :KC] = table_ref[...]
    OH_rows = trow_ref[...].astype(F32)
    line8 = lax.broadcasted_iota(jnp.int32, (8, KP), 0)
    wide_coef = jnp.concatenate([coef_ref[...].reshape(1, KC), jnp.zeros((1, KP - KC), F32)], axis=1)
    col_ref[...] = jnp.transpose(jnp.where(line8 < 4, OH_rows, wide_coef))
    tail = jnp.zeros((KP - KC, 256), BF16)
    E[KC:, :] = tail
    F1[KC:, :] = tail
    F2[KC:, :] = tail
    hi, lo = split(e_ref[...])
    E[:KC, :128] = hi
    E[:KC, 128:] = lo

    def gather(i, _):
        rows = pl.ds(pl.multiple_of(i * CH, 16), CH)
        lanes = lax.broadcasted_iota(jnp.int16, (CH, KP), 1)
        e = e_ref[rows, :]
        cols = col_ref[rows, :]
        one, nil = jnp.ones((), BF16), jnp.zeros((), BF16)
        for m in range(4):
            OH[m * CH : (m + 1) * CH, :] = jnp.where(
                lanes == jnp.broadcast_to(cols[:, m : m + 1].astype(jnp.int32), (CH, KP)).astype(jnp.int16), one, nil
            )
        p = jnp.dot(OH[...], E[...], preferred_element_type=F32)
        p = p[:, :128] + p[:, 128:]
        g = [p[m * CH : (m + 1) * CH] for m in range(4)]
        s = cols[:, 4:5]
        ee = e * e
        e2 = 2.0 * e
        a = s * (ee * (g[0] + g[1]) - e2 * g[0] * g[1])
        b = s * (ee * (g[2] + g[3]) - e2 * g[2] * g[3])
        forced_ref[rows, :] = e - (a + b)
        ah, al = split(a)
        bh, bl = split(b)
        F1[rows, :128] = ah
        F1[rows, 128:] = al
        F2[rows, :128] = bh
        F2[rows, 128:] = bl
        return 0

    lax.fori_loop(0, KC // CH, gather, 0)

    mask = mask_ref[...].astype(F32)

    def scatter(i, _):
        rows = pl.ds(pl.multiple_of(i * CH, 16), CH)
        b = lax.broadcasted_iota(jnp.int32, (CH, KP), 0) + i * CH

        def onehot(m):
            return jnp.where(b == trow_ref[m : m + 1, :], 1.0, 0.0)

        p = jnp.dot((onehot(0) + onehot(1)).astype(BF16), F1[...], preferred_element_type=F32)
        p = p + jnp.dot((onehot(2) + onehot(3)).astype(BF16), F2[...], preferred_element_type=F32)
        forced_ref[rows, :] = mask * (forced_ref[rows, :] + 0.5 * (p[:, :128] + p[:, 128:]))
        return 0

    lax.fori_loop(0, KC // CH, scatter, 0)

    def destination(n):
        return (((q16 - chunk_offset(n >> 3)) & 15) << 3) | ((dev + n) & 7)

    def fill1(t, _):
        for r in range(4):
            d = t * 4 + r
            base = start_of(d)
            for k in range(HEAD):
                pay1[d, k] = forced_ref[pl.ds(base + k, 1), :]
        return 0

    lax.fori_loop(0, 32, fill1, 0)

    pl.semaphore_wait(barrier, 128 + jnp.where(crosses_down | crosses_up, 1, 0))

    def ocean_copy(slot, side):
        return pltpu.make_async_remote_copy(
            src_ref=ostage.at[slot, side],
            dst_ref=ohalo.at[slot, 1 - side],
            send_sem=o_send.at[slot, side],
            recv_sem=o_recv.at[slot, 1 - side],
            device_id=up_id if side == 0 else down_id,
            device_id_type=MESH,
        )

    def ocean_start(slot):
        for side, there in ((0, has_up), (1, has_down)):
            @pl.when(there)
            def _(side=side):
                ocean_copy(slot, side).start()

    def ocean_wait(slot):
        for side, there in ((0, has_up), (1, has_down)):
            @pl.when(there)
            def _(side=side):
                wait_for(ostage.at[slot, side], o_send.at[slot, side])
                wait_for(ohalo.at[slot, side], o_recv.at[slot, side])

    def part_copy(side):
        return pltpu.make_async_remote_copy(
            src_ref=part.at[2 * side],
            dst_ref=pin.at[1 - side],
            send_sem=p_send.at[side],
            recv_sem=p_recv.at[1 - side],
            device_id=(grp, (dev + 127 + 2 * side) & 127),
            device_id_type=MESH,
        )

    for side, there in ((0, dev > 0), (1, dev < 127)):
        @pl.when(there)
        def _(side=side):
            part_copy(side).start()

    pltpu.make_async_copy(pay1.at[dev], arr1.at[dev], a1_recv.at[q16]).start()

    def send1(n, _):
        dest = destination(n)
        pltpu.make_async_remote_copy(
            src_ref=pay1.at[dest],
            dst_ref=arr1.at[dev],
            send_sem=a1_send,
            recv_sem=a1_recv.at[q16],
            device_id=(grp, dest),
            device_id_type=MESH,
        ).start()
        return 0

    lax.fori_loop(1, 128, send1, 0)

    def stage_ocean(slot, a, b):
        def level(z, _):
            for side, line in ((0, 0), (1, 7)):
                ostage[slot, side, 0, pl.ds(z, 1), :] = a(z)[line : line + 1]
                ostage[slot, side, 1, pl.ds(z, 1), :] = b(z)[line : line + 1]
            return 0

        lax.fori_loop(0, NZ, level, 0, unroll=8)

    stage_ocean(0, lambda z: u_ref[z], lambda z: v_ref[z])
    forced_ref[KC:, :] = jnp.zeros((KP - KC, 128), F32)
    weights = trig_ref[...] * jnp.concatenate([stokes_ref[...].reshape(1, KC), jnp.zeros((1, KP - KC), F32)], axis=1)
    drift_own = jnp.dot(weights, forced_ref[...], precision=HIGH, preferred_element_type=F32)

    def fill2(t, _):
        for r in range(4):
            d = t * 4 + r
            base = start_of(d)
            for k in range(3):
                pay2[d, k] = forced_ref[pl.ds(base + HEAD + k, 1), :]
            for q in range(2):
                pay2[d, 3 + q] = drift_own[q : q + 1]
            pay2[d, 7] = forced_ref[pl.ds(base + 10, 1), :]
        return 0

    lax.fori_loop(0, 32, fill2, 0)

    build_maps(map_ref, grp * 128, CT, M, MF)

    for side, there in ((0, dev > 0), (1, dev < 127)):
        @pl.when(there)
        def _(side=side):
            wait_for(part.at[2 * side], p_send.at[side])
            wait_for(pin.at[side], p_recv.at[side])

    total = part[1] + jnp.where(dev > 0, pin[0], 0.0) + jnp.where(dev < 127, pin[1], 0.0)
    speeds = 0.3 * total[0:2] / (total[2:3] + 1.0)

    def fill_currents(t, _):
        for r in range(8):
            for q in range(2):
                pay2[t * 8 + r, 5 + q] = speeds[q : q + 1]
        return 0

    lax.fori_loop(0, 16, fill_currents, 0)

    @pl.when(owner)
    def _():
        pltpu.make_async_copy(pay2.at[dev], arr2.at[dev], a2_recv.at[q16]).start()

    @pl.when(jnp.logical_not(owner))
    def _():
        pltpu.make_async_copy(pay2.at[dev, pl.ds(0, 7)], arr2.at[dev, pl.ds(0, 7)], a2_recv.at[q16]).start()

    def send2(n, _):
        dest = destination(n)

        @pl.when((dest & 7) == 0)
        def _():
            pltpu.make_async_remote_copy(
                src_ref=pay2.at[dest],
                dst_ref=arr2.at[dev],
                send_sem=b_send,
                recv_sem=a2_recv.at[q16],
                device_id=(grp, dest),
                device_id_type=MESH,
            ).start()

        @pl.when((dest & 7) != 0)
        def _():
            pltpu.make_async_remote_copy(
                src_ref=pay2.at[dest, pl.ds(0, 7)],
                dst_ref=arr2.at[dev, pl.ds(0, 7)],
                send_sem=a2_send,
                recv_sem=a2_recv.at[q16],
                device_id=(grp, dest),
                device_id_type=MESH,
            ).start()

        return 0

    lax.fori_loop(1, 128, send2, 0)
    ocean_start(0)
    zero_row = jnp.zeros((1, 128), F32)
    top = grp == 0

    acc[...] = jnp.zeros_like(acc)
    dacc[...] = jnp.zeros_like(dacc)

    def forward(low, count, last):
        n = count * 64

        def chunk_step(i, _):
            chunk = ((dev >> 4) + jnp.where((i & 1) == 1, (i + 1) >> 1, 8 - (i >> 1))) & 7
            for half in range(2):
                eighth = chunk * 2 + half
                if last:
                    @pl.when(owner)
                    def _():
                        wait_for(arr2.at[pl.ds(eighth * S, S)], a2_recv.at[eighth])

                    @pl.when(jnp.logical_not(owner))
                    def _():
                        wait_for(arr2.at[pl.ds(eighth * S, S), pl.ds(0, 7)], a2_recv.at[eighth])
                else:
                    wait_for(arr1.at[pl.ds(eighth * S, S)], a1_recv.at[eighth])

            for j in range(2 * S):
                s = chunk * (2 * S) + j
                cols = pl.ds(pl.multiple_of(s * 128, 128), 128)
                c = slice(j * 128, (j + 1) * 128)
                for k in range(count):
                    x = (arr2[s, 7 if k == 3 else k]) if last else arr1[s, k]
                    hi, lo = split(jnp.broadcast_to(x, (16, 128)))
                    for q in range(4):
                        m = M[q * 16 : (q + 1) * 16, cols]
                        r = k * 64 + q * 16
                        LH[r : r + 16, c] = m * hi
                        LH[n + r : n + r + 16, c] = m * lo
                if last:
                    row = map_ref[pl.ds(grp * 128 + s, 1), :] >> 7
                    pieces = []
                    for q in range(2):
                        cur[q, pl.ds(8 + s, 1), :] = arr2[s, 5 + q]
                        x = arr2[s, 3 + q]
                        for dr in range(3):
                            pieces.append(jnp.where(row == dev + (dr - 1), x, zero_row))
                    pieces += [zero_row, zero_row]
                    piece = jnp.concatenate(pieces, axis=0)
                    hi = piece.astype(BF16).astype(F32)
                    LH[2 * n : 2 * n + 16, c] = jnp.concatenate([hi, piece - hi], axis=0).astype(BF16)
            c = CT[:, pl.ds(pl.multiple_of(chunk * (S * 256), 128), S * 256)]
            d = lax.dot_general(LH[: 2 * n + (16 if last else 0)], c, NT, preferred_element_type=F32)
            acc[low : low + n] += d[:n] + d[n : 2 * n]
            if last:
                dacc[...] += d[2 * n :]
            return 0

        lax.fori_loop(0, 64 // S, chunk_step, 0)

    oline = lax.broadcasted_iota(jnp.int32, (8, 256), 0)
    olane = lax.broadcasted_iota(jnp.int32, (8, 256), 1)
    coriolis = 0.5 + (linear * 8 + oline).astype(F32) / 2048.0

    def ocean_step(slot, source, emit, drift):
        def lap(a, z, q):
            above = jnp.where(has_up, ohalo[slot, 0, q, pl.ds(z, 1), :], 0.0)
            below = jnp.where(has_down, ohalo[slot, 1, q, pl.ds(z, 1), :], 0.0)
            r = jnp.where(olane == 255, 0.0, pltpu.roll(a, 255, 1)) + jnp.where(olane == 0, 0.0, pltpu.roll(a, 1, 1))
            r = r + jnp.where(oline == 0, above, pltpu.roll(a, 1, 0)) + jnp.where(oline == 7, below, pltpu.roll(a, 7, 0))
            return r - 4.0 * a

        def level(z, carry):
            pu, pv = carry
            u, v = source(0, z), source(1, z)
            zn = jnp.minimum(z + 1, NZ - 1)
            m0 = mix_ref[z]
            m1 = jnp.where(z == NZ - 1, 0.0, mix_ref[zn])
            nu, nv = source(0, zn), source(1, zn)
            p = prof_ref[z]
            wu = m1 * (nu - u) - m0 * (u - pu)
            wv = m1 * (nv - v) - m0 * (v - pv)
            emit(
                z,
                u + 0.2 * (0.2 * lap(u, z, 0) + wu + coriolis * v + p * drift[0]),
                v + 0.2 * (0.2 * lap(v, z, 1) + wv - coriolis * u + p * drift[1]),
            )
            return u, v

        zero = jnp.zeros((8, 256), F32)
        lax.fori_loop(0, NZ, level, (zero, zero), unroll=8)

    def emit1(z, u, v):
        B[0, z] = u
        B[1, z] = v

    def emit2(z, u, v):
        ou_ref[z] = u
        ov_ref[z] = v

    forward(0, HEAD, False)
    forward(HEAD * 64, TAIL, True)

    for k in range(SHARE):
        low = acc[k * 64 : (k + 1) * 64, 0:128]
        high = acc[k * 64 : (k + 1) * 64, 128:256]
        G[k, 8:72, :] = low
        G[k, 72:136, :] = high
        edge[0, k : k + 1, :] = jnp.where(top, high[63:64], low[0:1])
        edge[1, k : k + 1, :] = jnp.where(top, high[62:63], low[1:2])
    for r in range(2):
        for q in range(2):
            edge[r, SHARE + q : SHARE + q + 1, :] = jnp.where(
                top, cur[q, 135 - r : 136 - r, :], cur[q, 8 + r : 9 + r, :]
            )
        edge[r, 13:16, :] = jnp.zeros((3, 128), F32)
    exchange = pltpu.make_async_remote_copy(
        src_ref=edge, dst_ref=halo, send_sem=h_send, recv_sem=h_recv, device_id=(1 - grp, dev), device_id_type=MESH
    )
    exchange.start()

    drift = dacc[0:8] + dacc[8:16]
    wave_row = dev + lax.rem(lax.broadcasted_iota(jnp.int32, (8, 128), 0), 3) - 1
    drift = jnp.where(wave_row >= 64, drift[:, 128:], drift[:, :128])
    wide = jnp.dot(drift, spread_matrix(), precision=HIGH, preferred_element_type=F32)
    masks = couple_masks(cp_ref[...], dev)
    cells = []
    for q in range(2):
        sum_q = jnp.zeros((8, 256), F32)
        for dr in range(3):
            for delta in range(3):
                sum_q = sum_q + masks[dr][delta] * wide[q * 3 + dr : q * 3 + dr + 1, delta * 256 : (delta + 1) * 256]
        cells.append(sum_q)
    us, vs = cells

    drift_terms = (coriolis * vs, -coriolis * us)


    below_on = jnp.where(top, 1.0, 0.0)
    above_on = 1.0 - below_on
    blank = jnp.zeros((6, 128), F32)

    def pad(dst, index, k):
        h0 = halo[0, k : k + 1, :]
        h1 = halo[1, k : k + 1, :]
        dst[index, 0:8, :] = jnp.concatenate([blank, h1, h0], axis=0) * above_on
        dst[index, 136:144, :] = jnp.concatenate([h0, h1, blank], axis=0) * below_on

    lane = lax.broadcasted_iota(jnp.int32, (144, 128), 1)
    line = lax.broadcasted_iota(jnp.int32, (144, 128), 0)
    first_lane, last_lane = lane == 0, lane == 127
    keep = jnp.where(line < 8, above_on, jnp.where(line >= 136, below_on, 1.0))

    def pace_of(k):
        comp = jnp.minimum(first + k, KC - 1)
        way = lax.rem(comp, ND)
        pace = speed_ref[comp]
        return pace * dirs_ref[0, way], pace * dirs_ref[1, way]

    def propagate(k, _):
        pace_x, pace_y = pace_of(k)
        cx = cur[0] + pace_x
        cy = cur[1] + pace_y
        f = substep(G[k], cx, cy, first_lane, last_lane) * keep
        f = substep(f, cx, cy, first_lane, last_lane)
        H[k] = f[8:136]
        return 0

    def backward(t, _):
        chunk = (q16 - chunk_offset(15 - t)) & 15
        c = CT[:, pl.ds(pl.multiple_of(chunk * (S * 128), 128), S * 128)]
        T[...] = jnp.dot(FF[:RB], c, preferred_element_type=F32) + jnp.dot(FF[RB:], c, preferred_element_type=F32)
        where = map_ref[pl.ds(pl.multiple_of(grp * 128 + chunk * S, 8), S), :]
        row, col = where >> 7, where & 127
        taken = [jnp.zeros((S, 128), F32) for _ in range(SHARE - ONEHOT)]
        for r in range(128):
            hit = row == r
            for k in range(SHARE - ONEHOT):
                x = jnp.broadcast_to(H[ONEHOT + k, r : r + 1, :], (S, 128))
                y = jnp.take_along_axis(x, col, axis=1, mode="promise_in_bounds")
                taken[k] = jnp.where(hit, y, taken[k])
        for j in range(S):
            s = chunk * S + j
            for k in range(SHARE - ONEHOT):
                out[s, ONEHOT + k] = taken[k][j : j + 1]
            m = MF[:, pl.ds(pl.multiple_of(s * 128, 128), 128)]
            for k in range(ONEHOT):
                out[s, k] = jnp.sum(T[k * 64 : (k + 1) * 64, j * 128 : (j + 1) * 128] * m, axis=0, keepdims=True)

        def post(j, _):
            s = chunk * S + j

            @pl.when((s != dev) & owner)
            def _():
                pltpu.make_async_remote_copy(
                    src_ref=out.at[s],
                    dst_ref=ret.at[pl.ds(first, 11)],
                    send_sem=r_send,
                    recv_sem=r_recv,
                    device_id=(grp, s),
                    device_id_type=MESH,
                ).start()

            @pl.when((s != dev) & jnp.logical_not(owner))
            def _():
                pltpu.make_async_remote_copy(
                    src_ref=out.at[s, pl.ds(0, 10)],
                    dst_ref=ret.at[pl.ds(first, 10)],
                    send_sem=r_send,
                    recv_sem=r_recv,
                    device_id=(grp, s),
                    device_id_type=MESH,
                ).start()

            return 0

        lax.fori_loop(0, S, post, 0)
        return 0

    none = jnp.zeros((8, 128), F32)
    for k in range(SHARE):
        G[k, 0:8, :] = none
        G[k, 136:144, :] = none
    for q in range(2):
        cur[q, 0:8, :] = none
        cur[q, 136:144, :] = none

    lax.fori_loop(0, SHARE, propagate, 0)
    exchange.wait()
    for k in range(SHARE):
        pad(G, k, k)
    for q in range(2):
        pad(cur, q, SHARE + q)
    strip = pl.multiple_of(jnp.where(top, 112, 0), 8)
    strip_lane = lax.broadcasted_iota(jnp.int32, (32, 128), 1)
    strip_line = lax.broadcasted_iota(jnp.int32, (32, 128), 0) + strip
    strip_keep = jnp.where(strip_line < 8, above_on, jnp.where(strip_line >= 136, below_on, 1.0))
    strip_u, strip_v = cur[0, pl.ds(strip, 32), :], cur[1, pl.ds(strip, 32), :]
    for k in range(SHARE):
        pace_x, pace_y = pace_of(k)
        cx, cy = strip_u + pace_x, strip_v + pace_y
        f = substep(G[k, pl.ds(strip, 32), :], cx, cy, strip_lane == 0, strip_lane == 127) * strip_keep
        f = substep(f, cx, cy, strip_lane == 0, strip_lane == 127)
        H[k, pl.ds(pl.multiple_of(jnp.where(top, 120, 0), 8), 8), :] = jnp.where(top, f[16:24], f[8:16])
    for k in range(ONEHOT):
        for h in range(2):
            hi, lo = split(H[k, h * 64 : 64 + h * 64, :])
            FF[k * 64 : (k + 1) * 64, h * 128 : (h + 1) * 128] = hi
            FF[RB + k * 64 : RB + (k + 1) * 64, h * 128 : (h + 1) * 128] = lo
    lax.fori_loop(0, 5, backward, 0)
    ocean_wait(0)
    ocean_step(0, lambda q, z: (u_ref, v_ref)[q][z], emit1, drift_terms)
    stage_ocean(1, lambda z: B[0, z], lambda z: B[1, z])
    ocean_start(1)
    lax.fori_loop(5, 128 // S, backward, 0)
    for k in range(10):
        ret[first + k] = out[dev, k]

    @pl.when(owner)
    def _():
        ret[first + 10] = out[dev, 10]

    ocean_wait(1)
    ocean_step(1, lambda q, z: B[q, z], emit2, drift_terms)

    wait_for(pay1.at[pl.ds(0, 127)], a1_send)

    @pl.when(owner)
    def _():
        wait_for(pay2.at[pl.ds(0, 112), pl.ds(0, 7)], a2_send)
        wait_for(pay2.at[pl.ds(0, 15)], b_send)
        wait_for(out.at[pl.ds(0, 127)], r_send)
        wait_for(ret.at[pl.ds(0, KC - 11)], r_recv)

    @pl.when(jnp.logical_not(owner))
    def _():
        wait_for(pay2.at[pl.ds(0, 111), pl.ds(0, 7)], a2_send)
        wait_for(pay2.at[pl.ds(0, 16)], b_send)
        wait_for(out.at[pl.ds(0, 127), pl.ds(0, 10)], r_send)
        wait_for(ret.at[pl.ds(0, KC - 10)], r_recv)


def finish_kernel(r_ref, mask_ref, u_ref, v_ref, o_ref, ou_ref, ov_ref):
    ou_ref[...] = u_ref[...]
    ov_ref[...] = v_ref[...]
    o_ref[...] = r_ref[...] * mask_ref[...].astype(F32)


def body(spectra, sea_mask, card_map, dia_table, dia_coef, speed, stokes_weight, couple_point, ocean_u, ocean_v, mixing):
    sds = jax.ShapeDtypeStruct
    dirs = direction_table()
    trig = np.zeros((8, KP), np.float32)
    trig[:2, :KC] = np.tile(dirs, (1, KC // ND))
    profile = np.exp(-3.0 * (np.arange(NZ) + 0.5) / NZ).astype(np.float32)
    vmem = pl.BlockSpec(memory_space=pltpu.VMEM)
    smem = pl.BlockSpec(memory_space=pltpu.SMEM)
    dma = pltpu.SemaphoreType.DMA
    scratch = [
        pltpu.VMEM((KP, 256), BF16),
        pltpu.VMEM((KP, 256), BF16),
        pltpu.VMEM((KP, 256), BF16),
        pltpu.VMEM((4 * CH, KP), BF16),
        pltpu.VMEM((KP, 128), F32),
        pltpu.VMEM((8, KP), jnp.int32),
        pltpu.VMEM((KP, 8), F32),
        pltpu.VMEM((128, HEAD, 1, 128), F32),
        pltpu.VMEM((128, 8, 1, 128), F32),
        pltpu.VMEM((128, HEAD, 1, 128), F32),
        pltpu.VMEM((128, 8, 1, 128), F32),
        pltpu.VMEM((128, SHARE, 1, 128), F32),
        pltpu.VMEM((256, 16384), BF16),
        pltpu.VMEM((64, 16384), BF16),
        pltpu.VMEM((64, 16384), F32),
        pltpu.VMEM((128 * HEAD, S * 256), BF16),
        pltpu.VMEM((2 * RB, 256), BF16),
        pltpu.VMEM((R, 256), F32),
        pltpu.VMEM((16, 256), F32),
        pltpu.VMEM((RB, S * 128), F32),
        pltpu.VMEM((SHARE, 144, 128), F32),
        pltpu.VMEM((SHARE, 128, 128), F32),
        pltpu.VMEM((2, 144, 128), F32),
        pltpu.VMEM((2, 16, 128), F32),
        pltpu.VMEM((2, 16, 128), F32),
        pltpu.VMEM((3, 8, 128), F32),
        pltpu.VMEM((2, 8, 128), F32),
        pltpu.VMEM((2, 2, 2, NZ, 256), F32),
        pltpu.VMEM((2, 2, 2, NZ, 256), F32),
        pltpu.VMEM((2, NZ, 8, 256), F32),
        dma((2, 2)), dma((2, 2)), dma((2,)), dma((2,)),
        dma, dma((16,)), dma, dma((16,)), dma, dma, dma, dma, dma,
    ]
    ret, new_u, new_v = pl.pallas_call(
        step_kernel,
        out_shape=(sds((KC, 1, 128), F32), sds((NZ, 8, 256), F32), sds((NZ, 8, 256), F32)),
        in_specs=[vmem] * 7 + [smem] * 2 + [vmem] * 3 + [smem] * 2,
        out_specs=(vmem,) * 3,
        scratch_shapes=scratch,
        compiler_params=pltpu.CompilerParams(
            vmem_limit_bytes=VMEM_LIMIT, collective_id=0, has_side_effects=True
        ),
        name="step",
    )(
        spectra, sea_mask.reshape(1, 128), dia_table, dia_coef, stokes_weight,
        jnp.asarray(trig), card_map.reshape(256, 128), speed, jnp.asarray(dirs), couple_point, ocean_u, ocean_v,
        mixing, jnp.asarray(profile),
    )
    return pl.pallas_call(
        finish_kernel,
        out_shape=(sds((KC, 128), F32), sds((NZ, 8, 256), F32), sds((NZ, 8, 256), F32)),
        in_specs=[vmem] * 4,
        out_specs=(vmem,) * 3,
        name="finish",
    )(ret.reshape(KC, 128), sea_mask.reshape(1, 128), new_u, new_v)


def solution(mesh):
    both = ("grp", "dev")
    in_specs = (P(None, both), P(both), P(), P(), P(), P(), P(), P(both, None), P(None, both, None), P(None, both, None), P())
    out_specs = (P(None, both), P(None, both, None), P(None, both, None))
    return jax.shard_map(body, mesh=mesh, in_specs=in_specs, out_specs=out_specs, check_vma=False)
```
